32 devices in a mesh: seq: 4 (over y, x), fsdp: 8 (over z, core).
Axes of the slice: x: 2, y: 2, z: 4, core: 2. Of those that a mesh axis runs over, the one named last changes fastest.
Arguments:
- tokens: bfloat16 [8, 1024, 2048], P('fsdp', 'seq'), may hold values from -6 to 6
- qkv_weight: bfloat16 [2048, 6144], P('fsdp'), may hold values from -0.125 to 0.125
- out_weight: bfloat16 [2048, 2048], P('fsdp'), may hold values from -1.5 to 1.5
- up_weight: bfloat16 [2048, 8192], P('fsdp'), may hold values from -0.125 to 0.125
- down_weight: bfloat16 [8192, 2048], P('fsdp'), may hold values from -0.0625 to 0.0625
- norm_gain: bfloat16 [2048], P('fsdp'), may hold values from 0.5 to 1.5
- norm_bias: bfloat16 [2048], P('fsdp'), may hold values from -3 to 3
- qkv_bias: bfloat16 [6144], P('fsdp'), may hold values from -4 to 4
- out_bias: bfloat16 [2048], P('fsdp'), may hold values from -4 to 4
- up_bias: bfloat16 [8192], P('fsdp'), may hold values from -6 to 6
- down_bias: bfloat16 [2048], P('fsdp'), may hold values from -4 to 4
- cotangent: bfloat16 [8, 1024, 2048], P('fsdp', 'seq'), may hold values from -6 to 6
Outputs:
- block_out: bfloat16 [8, 1024, 2048], P('fsdp', 'seq')
- tokens_grad: bfloat16 [8, 1024, 2048], P('fsdp', 'seq')
- qkv_wgrad: float32 [2048, 6144], P('fsdp')
- out_wgrad: float32 [2048, 2048], P('fsdp')
- up_wgrad: float32 [2048, 8192], P('fsdp')
- down_wgrad: float32 [8192, 2048], P('fsdp')
- gain_grad: float32 [2048], P('fsdp')
- norm_bgrad: float32 [2048], P('fsdp')
- qkv_bgrad: float32 [4096], P('fsdp')
- value_bgrad: float32 [2048], P('fsdp')
- out_bgrad: float32 [2048], P('fsdp')
- up_bgrad: float32 [8192], P('fsdp')
- down_bgrad: float32 [2048], P('fsdp')
The draws below stay inside these ranges and needn't reach their ends.
All inputs are finite; a program needn't handle non-finite values.
Results may differ from the reference program's by a relative error of at most 0.011.
Values may be sent and summed in bfloat16 or wider, within the bound.
No kernel may reach another device: no remote copies, remote signals or barrier semaphores. Data moves between devices by JAX's collectives and lax.ppermute only.
A program may use at most 576 MiB of HBM per device.

```python
import math
import jax
import jax.numpy as jnp
from jax import lax

D = 2048
H = 32
HD = 64
ROT = 32
FF = 8192
SEQS = 8
LEN = 1024


def levels(stream_key, extent, cuts, smallest, top_value):
    gain = 1.0
    for dim, parts in cuts:
        heights = jax.random.uniform(jax.random.fold_in(jax.random.fold_in(stream_key, 6), dim), (parts,), jnp.float32, smallest / len(cuts), top_value / len(cuts))
        gain = gain * jnp.repeat(jnp.exp(heights), extent[dim] // parts).reshape((-1,) + (1,) * (len(extent) - 1 - dim))
    return gain


def scatter_about(stream_key, extent, scale, limit, cuts=(), held_as=jnp.bfloat16):
    array = jax.random.normal(stream_key, extent, jnp.float32) * scale
    if len(cuts) > 0:
        array = levels(stream_key, extent, cuts, -0.22, 0.18) * array
    return jnp.clip(array, min=-limit, max=limit).astype(held_as)


def setup_inputs(seed: int = 0) -> dict:
    splits = jax.random.split(jax.random.key(seed), 13)
    tokens = scatter_about(splits[0], (SEQS, LEN, D), 1.0, 6.0, ((0, 8), (1, 4)))
    qkv_weight = scatter_about(splits[1], (D, 3 * D), D ** -0.5, 0.125, ((0, 8),))
    out_weight = scatter_about(splits[2], (D, D), (max(D // 128, 4)) ** -0.5, 1.5, ((0, 8),))
    up_weight = scatter_about(splits[3], (D, FF), D ** -0.5, 0.125, ((0, 8),))
    down_weight = scatter_about(splits[4], (FF, D), FF ** -0.5, 0.0625, ((0, 8),))
    norm_gain = jnp.clip(1.0 + 0.1 * jax.random.normal(splits[5], (D,), jnp.float32), 0.5, 1.5).astype(jnp.bfloat16)
    norm_bias = scatter_about(splits[6], (D,), 0.2, 3.0, ((0, 8),))
    qkv_bias = scatter_about(splits[7], (3 * D,), 0.3, 4.0, ((0, 8),))
    out_bias = scatter_about(splits[8], (D,), 0.3, 4.0, ((0, 8),))
    up_bias = scatter_about(splits[9], (FF,), 0.5, 6.0, ((0, 8),))
    down_bias = scatter_about(splits[10], (D,), 0.3, 4.0, ((0, 8),))
    cotangent = scatter_about(splits[11], (SEQS, LEN, D), 1.0, 6.0, ((0, 8), (1, 4)))
    return {"tokens": tokens, "qkv_weight": qkv_weight, "out_weight": out_weight, "up_weight": up_weight, "down_weight": down_weight, "norm_gain": norm_gain, "norm_bias": norm_bias, "qkv_bias": qkv_bias, "out_bias": out_bias, "up_bias": up_bias, "down_bias": down_bias, "cotangent": cotangent}


@jax.custom_vjp
def low(v):
    return lax.optimization_barrier(v.astype(jnp.bfloat16)).astype(jnp.float32)

@jax.custom_vjp
def low_back(v):
    return v

def low_keep(v):
    return (low(v), None)

def low_pass(kept, grad):
    return (grad,)

def back_keep(v):
    return (v, None)

def back_low(kept, grad):
    return (low(grad),)
low.defvjp(low_keep, low_pass)
low_back.defvjp(back_keep, back_low)
epsilon = 1e-05
rope_base = 10000.0
masked_score = -1000000000.0

def products(left, right):
    return jnp.dot(left, right, precision=lax.Precision.HIGHEST)

def rotary_tables(positions):
    halves = ROT // 2
    frequency = rope_base ** (-(2.0 * jnp.arange(halves).astype(jnp.float32)) / ROT)
    angles = positions.astype(jnp.float32)[:, None] * frequency[None, :]
    return (jnp.cos(angles), jnp.sin(angles))

def rotate(values, cos_table, sin_table):
    halves = ROT // 2
    leading = values[..., :halves]
    trailing = values[..., halves:ROT]
    cos_wide = cos_table[:, None, :]
    sin_wide = sin_table[:, None, :]
    return jnp.concatenate([leading * cos_wide - trailing * sin_wide, trailing * cos_wide + leading * sin_wide, values[..., ROT:]], axis=-1)

def attend(queries, key_rows, values):
    length = queries.shape[0]
    block_rows = math.gcd(length, 512)
    score_scale = HD ** (-0.5)
    key_place = jnp.arange(length)

    def one_block(operands):
        query_block, first_row = operands
        scores = jnp.einsum('bhd,lhd->hbl', query_block, key_rows, precision=lax.Precision.HIGHEST) * score_scale
        scores = low_back(scores)
        query_place = first_row + jnp.arange(block_rows)
        visible = key_place[None, None, :] <= query_place[None, :, None]
        scores = jnp.where(visible, scores, masked_score)
        weights = jax.nn.softmax(scores, axis=-1)
        return jnp.einsum('hbl,lhd->bhd', low(weights), values, precision=lax.Precision.HIGHEST)
    stacked = queries.reshape(length // block_rows, block_rows, H, HD)
    firsts = jnp.arange(length // block_rows) * block_rows
    result = lax.map(jax.checkpoint(one_block), (stacked, firsts))
    return result.reshape(length, H * HD)

def layer(token_rows, params):
    qkv_weight, out_weight, up_weight, down_weight, norm_gain, norm_bias, qkv_bias, out_bias, up_bias, down_bias = params
    length = token_rows.shape[0]
    average = lax.optimization_barrier(jnp.mean(token_rows, axis=-1, keepdims=True))
    centred = token_rows - average
    variance = lax.optimization_barrier(jnp.mean(centred * centred, axis=-1, keepdims=True))
    normed = low(centred * lax.rsqrt(variance + epsilon) * norm_gain + norm_bias)
    mixed_cols = low_back(products(normed, qkv_weight) + qkv_bias)
    cos_table, sin_table = rotary_tables(jnp.arange(length))
    queries = low(rotate(mixed_cols[:, :D].reshape(length, H, HD), cos_table, sin_table))
    key_rows = low(rotate(mixed_cols[:, D:2 * D].reshape(length, H, HD), cos_table, sin_table))
    values = low(mixed_cols[:, 2 * D:].reshape(length, H, HD))
    attended = low_back(low(attend(queries, key_rows, values)))
    attn_branch = products(attended, out_weight) + out_bias
    hidden = low_back(products(normed, up_weight) + up_bias)
    activated = low(jax.nn.gelu(hidden, approximate=True))
    return token_rows + attn_branch + products(activated, down_weight) + down_bias

def reference(tokens, qkv_weight, out_weight, up_weight, down_weight, norm_gain, norm_bias, qkv_bias, out_bias, up_bias, down_bias, cotangent):
    params = tuple((tensor.astype(jnp.float32) for tensor in (qkv_weight, out_weight, up_weight, down_weight, norm_gain, norm_bias, qkv_bias, out_bias, up_bias, down_bias)))

    def forward(inputs, *weights):
        return lax.map(lambda token_rows: layer(token_rows, weights), inputs)
    result, pullback = jax.vjp(forward, tokens.astype(jnp.float32), *params)
    gradients = pullback(cotangent.astype(jnp.float32))
    qkv_bias_grad = gradients[7]
    return (result.astype(jnp.bfloat16), gradients[0].astype(jnp.bfloat16), gradients[1], gradients[2], gradients[3], gradients[4], gradients[5], gradients[6], qkv_bias_grad[:2 * D], qkv_bias_grad[2 * D:], gradients[8], gradients[9], gradients[10])
```

```python
import functools

import jax
import jax.numpy as jnp
from jax import lax
from jax.experimental import pallas as pl
from jax.experimental.pallas import tpu as pltpu
from jax.sharding import PartitionSpec as P

HD = 64
ROT = 32
PAIR = 2 * HD
CORES = 2
BLOCK = 256

epsilon = 1e-05
rope_base = 10000.0
masked_score = -1000000000.0
f32 = jnp.float32
bf16 = jnp.bfloat16


def rotary_lanes(length):
    halves = ROT // 2
    lane = jnp.arange(PAIR) % HD
    frequency = rope_base ** (-(2.0 * (lane % halves).astype(f32)) / ROT)
    angles = jnp.arange(length).astype(f32)[:, None] * frequency[None, :]
    rotated = lane < ROT
    cos = jnp.where(rotated, jnp.cos(angles), 1.0)
    sin = jnp.sin(angles)
    from_right = jnp.where(lane < halves, -sin, 0.0)
    from_left = jnp.where((lane >= halves) & rotated, sin, 0.0)
    return cos, from_right, from_left


def turn(x, cos, from_right, from_left):
    halves = ROT // 2
    return (
        x * cos
        + pltpu.roll(x, PAIR - halves, 1) * from_right
        + pltpu.roll(x, halves, 1) * from_left
    )


def last_last(left, right):
    return lax.dot_general(left, right, (((1,), (1,)), ((), ())), preferred_element_type=f32)


def plain_dot(left, right):
    return jnp.dot(left, right, preferred_element_type=f32)


def head_lanes(head):
    lane = lax.broadcasted_iota(jnp.int32, (1, PAIR), 1)
    return (lane >= head * HD) & (lane < (head + 1) * HD)


def visible_block(block):
    key_place = lax.broadcasted_iota(jnp.int32, (block, block), 0)
    query_place = lax.broadcasted_iota(jnp.int32, (block, block), 1)
    return key_place <= query_place


def attend_kernel(mixed_ref, cos_ref, right_ref, left_ref, heads_ref, out_ref, logsum_ref, turned):
    length = mixed_ref.shape[0]
    block = min(BLOCK, length)
    tables = (cos_ref[...], right_ref[...], left_ref[...])
    heads_ref[:, :PAIR] = (turn(mixed_ref[:, :PAIR], *tables) * HD**-0.5).astype(bf16)
    heads_ref[:, PAIR : 2 * PAIR] = turn(mixed_ref[:, PAIR : 2 * PAIR], *tables).astype(bf16)
    heads_ref[:, 2 * PAIR :] = mixed_ref[:, 2 * PAIR :].astype(bf16)
    values_t = jnp.transpose(mixed_ref[:, 2 * PAIR :]).astype(bf16)
    visible = visible_block(block)
    for head in range(2):
        lanes = head_lanes(head)
        rows = slice(head * HD, (head + 1) * HD)
        for i in range(length // block):
            here = slice(i * block, (i + 1) * block)
            query = heads_ref[here, :PAIR]
            query = jnp.where(lanes, query, jnp.zeros_like(query))
            diag = last_last(heads_ref[here, PAIR : 2 * PAIR], query)
            diag = jnp.where(visible, diag, masked_score)
            highest = jnp.max(diag, axis=0, keepdims=True)
            if i > 0:
                past = last_last(heads_ref[: i * block, PAIR : 2 * PAIR], query)
                highest = jnp.maximum(highest, jnp.max(past, axis=0, keepdims=True))
            diag = jnp.exp(diag - highest)
            total = jnp.sum(diag, axis=0, keepdims=True)
            result = plain_dot(values_t[rows, here], diag.astype(bf16))
            if i > 0:
                past = jnp.exp(past - highest)
                total = total + jnp.sum(past, axis=0, keepdims=True)
                result = result + plain_dot(values_t[rows, : i * block], past.astype(bf16))
            turned[rows, here] = result / total
            logsum_ref[head : head + 1, here] = highest + jnp.log(total)
    out_ref[...] = jnp.transpose(turned[...]).astype(bf16)


def attend_back_kernel(
    heads_ref, grad_ref, logsum_ref, cos_ref, right_ref, left_ref, back_ref, turned, key_sum, value_sum
):
    length = heads_ref.shape[0]
    block = min(BLOCK, length)
    tables = (cos_ref[...], -right_ref[...], -left_ref[...])
    scaled = heads_ref[:, PAIR : 2 * PAIR].astype(f32) * HD**-0.5
    keys_t = jnp.transpose(scaled).astype(bf16)
    visible = visible_block(block)
    key_sum[...] = jnp.zeros_like(key_sum)
    value_sum[...] = jnp.zeros_like(value_sum)
    for head in range(2):
        lanes = head_lanes(head)
        rows = slice(head * HD, (head + 1) * HD)
        for i in range(length // block):
            here = slice(i * block, (i + 1) * block)
            upto = slice(0, (i + 1) * block)
            query = heads_ref[here, :PAIR]
            query = jnp.where(lanes, query, jnp.zeros_like(query))
            grad = grad_ref[here, :]
            grad = jnp.where(lanes, grad, jnp.zeros_like(grad))
            logsum = logsum_ref[head : head + 1, here]
            parts = []
            inner = None
            for begin, end in ((0, i * block), (i * block, (i + 1) * block)):
                if begin == end:
                    continue
                probs = jnp.exp(last_last(heads_ref[begin:end, PAIR : 2 * PAIR], query) - logsum)
                if end > i * block:
                    probs = jnp.where(visible, probs, 0.0)
                prob_grad = last_last(heads_ref[begin:end, 2 * PAIR :], grad)
                term = jnp.sum(probs * prob_grad, axis=0, keepdims=True)
                inner = term if inner is None else inner + term
                parts.append((begin, end, probs, prob_grad))
            query_grad = None
            for begin, end, probs, prob_grad in parts:
                score_grad = (probs * (prob_grad - inner)).astype(bf16)
                value_sum[begin:end, :] += plain_dot(probs.astype(bf16), grad)
                key_sum[begin:end, :] += plain_dot(score_grad, query)
                term = plain_dot(keys_t[rows, begin:end], score_grad)
                query_grad = term if query_grad is None else query_grad + term
            turned[rows, here] = query_grad
    back_ref[:, :PAIR] = turn(jnp.transpose(turned[...]), *tables).astype(bf16)
    back_ref[:, PAIR : 2 * PAIR] = turn(key_sum[...], *tables).astype(bf16)
    back_ref[:, 2 * PAIR :] = value_sum[...].astype(bf16)


def attend(mixed, tables, length):
    count, width = mixed.shape[0] // length, mixed.shape[1]
    pairs = width // (3 * PAIR)
    table = pl.BlockSpec((length, PAIR), lambda n, p: (0, 0))
    wide = pl.BlockSpec((length, 3 * PAIR), lambda n, p: (n, p))
    return pl.pallas_call(
        attend_kernel,
        grid=(count, pairs),
        in_specs=[wide, table, table, table],
        out_specs=[
            wide,
            pl.BlockSpec((length, PAIR), lambda n, p: (n, p)),
            pl.BlockSpec((None, None, 2, length), lambda n, p: (n, p, 0, 0)),
        ],
        out_shape=[
            jax.ShapeDtypeStruct(mixed.shape, bf16),
            jax.ShapeDtypeStruct((count * length, pairs * PAIR), bf16),
            jax.ShapeDtypeStruct((count, pairs, 2, length), f32),
        ],
        scratch_shapes=[pltpu.VMEM((PAIR, length), f32)],
        compiler_params=pltpu.CompilerParams(vmem_limit_bytes=40 * 1024 * 1024),
        cost_estimate=pl.CostEstimate(
            flops=count * pairs * 2 * length * length * 64 * 4,
            bytes_accessed=mixed.size * 8,
            transcendentals=count * pairs * length * length,
        ),
        name="attend",
    )(mixed, *tables)


def attend_back(heads, grad, logsums, tables, length):
    count, width = heads.shape[0] // length, heads.shape[1]
    pairs = width // (3 * PAIR)
    table = pl.BlockSpec((length, PAIR), lambda n, p: (0, 0))
    wide = pl.BlockSpec((length, 3 * PAIR), lambda n, p: (n, p))
    return pl.pallas_call(
        attend_back_kernel,
        grid=(count, pairs),
        in_specs=[
            wide,
            pl.BlockSpec((length, PAIR), lambda n, p: (n, p)),
            pl.BlockSpec((None, None, 2, length), lambda n, p: (n, p, 0, 0)),
            table,
            table,
            table,
        ],
        out_specs=wide,
        out_shape=jax.ShapeDtypeStruct(heads.shape, bf16),
        scratch_shapes=[
            pltpu.VMEM((PAIR, length), f32),
            pltpu.VMEM((length, PAIR), f32),
            pltpu.VMEM((length, PAIR), f32),
        ],
        compiler_params=pltpu.CompilerParams(vmem_limit_bytes=40 * 1024 * 1024),
        cost_estimate=pl.CostEstimate(
            flops=count * pairs * 2 * length * length * 64 * 10,
            bytes_accessed=heads.size * 6,
            transcendentals=count * pairs * length * length,
        ),
        name="attend_back",
    )(heads, grad, logsums, *tables)


def norm_kernel(place_ref, gain_ref, bias_ref, *refs):
    *pieces, out_ref = refs
    half = len(pieces) // 2
    for i, piece in enumerate(pieces):

        @pl.when(pl.program_id(0) == i // half * half + ((i % half) ^ place_ref[0]))
        def _(piece=piece):
            x = piece[...].astype(f32)
            centred = x - jnp.mean(x, axis=-1, keepdims=True)
            variance = jnp.mean(centred * centred, axis=-1, keepdims=True)
            out_ref[...] = (
                centred * lax.rsqrt(variance + epsilon) * gain_ref[...] + bias_ref[...]
            ).astype(bf16)


def norm_both(place, pieces, gain, bias):
    local, d = pieces[0].shape
    fixed = lambda i, place: (0, 0)
    return pl.pallas_call(
        norm_kernel,
        grid_spec=pltpu.PrefetchScalarGridSpec(
            num_scalar_prefetch=1,
            grid=(len(pieces),),
            in_specs=[pl.BlockSpec((1, d), fixed)] * 2 + [pl.BlockSpec((local, d), fixed)] * len(pieces),
            out_specs=pl.BlockSpec((local, d), lambda i, place: (i, 0)),
        ),
        out_shape=jax.ShapeDtypeStruct((len(pieces) * local, d), bf16),
        compiler_params=pltpu.CompilerParams(vmem_limit_bytes=48 * 1024 * 1024),
        name="norm_both",
    )(place, gain[None], bias[None], *pieces)


def order_kernel(place_ref, *refs):
    *pieces, out_ref = refs
    for i, piece in enumerate(pieces):

        @pl.when(pl.program_id(0) == i)
        def _(piece=piece):
            out_ref[...] = piece[...]


def order_both(place, pieces):
    local, d = pieces[0].shape
    half = len(pieces) // 2
    return pl.pallas_call(
        order_kernel,
        grid_spec=pltpu.PrefetchScalarGridSpec(
            num_scalar_prefetch=1,
            grid=(len(pieces),),
            in_specs=[pl.BlockSpec((local, d), lambda i, place: (0, 0))] * len(pieces),
            out_specs=pl.BlockSpec(
                (local, d),
                lambda i, place: (
                    jnp.where(i < half, i ^ place[0], half + ((i - half) ^ place[0])),
                    0,
                ),
            ),
        ),
        out_shape=jax.ShapeDtypeStruct((len(pieces) * local, d), pieces[0].dtype),
        compiler_params=pltpu.CompilerParams(vmem_limit_bytes=48 * 1024 * 1024),
        name="order_both",
    )(place, *pieces)


def row_blocks(rows):
    return min(64, rows)


def unit_kernel(nz, ns, w, place_ref, in_ref, out_ref):
    for c in range(CORES):
        for q in range(nz):
            at = pl.multiple_of(((q * CORES + c) * ns + place_ref[0]) * w, w)
            to = (c * nz + q) * w
            out_ref[:, to : to + w] = in_ref[:, pl.ds(at, w)]


def unit_columns(weight, place, nz, ns, w):
    rows, ff = weight.shape
    block = row_blocks(rows)
    wide = CORES * nz * w
    return pl.pallas_call(
        functools.partial(unit_kernel, nz, ns, w),
        grid_spec=pltpu.PrefetchScalarGridSpec(
            num_scalar_prefetch=1,
            grid=(rows // block,),
            in_specs=[pl.BlockSpec((block, ff), lambda i, place: (i, 0))],
            out_specs=pl.BlockSpec((block, wide), lambda i, place: (i, 0)),
        ),
        out_shape=jax.ShapeDtypeStruct((rows, wide), weight.dtype),
        name="unit_columns",
    )(place, weight)


def place_units_kernel(nz, w, place_ref, *refs):
    *pieces, out_ref = refs
    ns = len(pieces)
    for d, piece in enumerate(pieces):
        device = place_ref[0] ^ d
        for q in range(nz):
            for c in range(CORES):
                to = pl.multiple_of(((q * CORES + c) * ns + device) * w, w)
                out_ref[:, pl.ds(to, w)] = piece[c, :, q * w : (q + 1) * w].astype(f32)


def place_units(place, pieces, nz, w):
    cores, rows, width = pieces[0].shape
    block = row_blocks(rows)
    ff = width * cores * len(pieces)
    return pl.pallas_call(
        functools.partial(place_units_kernel, nz, w),
        grid_spec=pltpu.PrefetchScalarGridSpec(
            num_scalar_prefetch=1,
            grid=(rows // block,),
            in_specs=[pl.BlockSpec((cores, block, width), lambda i, place: (0, i, 0)) for _ in pieces],
            out_specs=pl.BlockSpec((block, ff), lambda i, place: (i, 0)),
        ),
        out_shape=jax.ShapeDtypeStruct((rows, ff), f32),
        name="place_units",
    )(place, *pieces)


def low_half():
    return lax.broadcasted_iota(jnp.int32, (1, PAIR), 1) < HD


def lows(first, second):
    return jnp.where(low_half(), first, pltpu.roll(second, HD, 1))


def highs(first, second):
    return jnp.where(low_half(), pltpu.roll(first, HD, 1), second)


def head_kernel(nz, ns, place_ref, in_ref, out_ref):
    tiles = ns // 2
    part = nz * CORES * tiles
    even = lax.rem(place_ref[0], 2) == 0

    def tile(j, q, c):
        at = (j * part + (q * CORES + c) * tiles + lax.div(place_ref[0], 2)) * PAIR
        return in_ref[:, pl.ds(pl.multiple_of(at, PAIR), PAIR)].astype(f32)

    for c in range(CORES):
        for p in range(nz // 2):
            for j in range(3):
                first, second = tile(j, 2 * p, c), tile(j, 2 * p + 1, c)
                to = ((c * (nz // 2) + p) * 3 + j) * PAIR
                out_ref[:, to : to + PAIR] = jnp.where(
                    even, lows(first, second), highs(first, second)
                ).astype(out_ref.dtype)


def head_columns(weight, place, nz, ns):
    rows, width = weight.shape
    block = row_blocks(rows)
    wide = CORES * nz * 3 * HD
    return pl.pallas_call(
        functools.partial(head_kernel, nz, ns),
        grid_spec=pltpu.PrefetchScalarGridSpec(
            num_scalar_prefetch=1,
            grid=(rows // block,),
            in_specs=[pl.BlockSpec((block, width), lambda i, place: (i, 0))],
            out_specs=pl.BlockSpec((block, wide), lambda i, place: (i, 0)),
        ),
        out_shape=jax.ShapeDtypeStruct((rows, wide), weight.dtype),
        name="head_columns",
    )(place, weight)


def place_heads_kernel(nz, place_ref, *refs):
    *pieces, out_ref = refs
    tiles = len(pieces) // 2
    even = lax.rem(place_ref[0], 2) == 0
    for d in range(0, len(pieces), 2):
        tile = lax.div(place_ref[0] ^ d, 2)
        for j in range(3):
            for p in range(nz // 2):
                at = (p * 3 + j) * PAIR
                for c in range(CORES):
                    one = pieces[d][c, :, at : at + PAIR].astype(f32)
                    two = pieces[d + 1][c, :, at : at + PAIR].astype(f32)
                    first, second = jnp.where(even, one, two), jnp.where(even, two, one)
                    for q, value in ((2 * p, lows(first, second)), (2 * p + 1, highs(first, second))):
                        to = (((j * nz + q) * CORES + c) * tiles + tile) * PAIR
                        out_ref[:, pl.ds(pl.multiple_of(to, PAIR), PAIR)] = value


def place_heads(place, pieces, nz):
    cores, rows, width = pieces[0].shape
    block = row_blocks(rows)
    whole = width * cores * len(pieces)
    return pl.pallas_call(
        functools.partial(place_heads_kernel, nz),
        grid_spec=pltpu.PrefetchScalarGridSpec(
            num_scalar_prefetch=1,
            grid=(rows // block,),
            in_specs=[pl.BlockSpec((cores, block, width), lambda i, place: (0, i, 0)) for _ in pieces],
            out_specs=pl.BlockSpec((block, whole), lambda i, place: (i, 0)),
        ),
        out_shape=jax.ShapeDtypeStruct((rows, whole), f32),
        name="place_heads",
    )(place, *pieces)


def gelu_and_slope(u):
    cubic = 0.044715
    root = 0.7978845608
    square = u * u
    t = jnp.tanh(root * u * (1.0 + cubic * square))
    value = 0.5 * u * (1.0 + t)
    slope = 0.5 * (1.0 + t) + 0.5 * u * (1.0 - t * t) * root * (1.0 + 3.0 * cubic * square)
    return value, slope


def on_device(
    ns,
    nf,
    tokens,
    qkv_weight,
    out_weight,
    up_weight,
    down_weight,
    norm_gain,
    norm_bias,
    qkv_bias,
    out_bias,
    up_bias,
    down_bias,
    cotangent,
):
    nz = nf // CORES
    ranks = CORES * ns
    s = lax.axis_index("seq")
    f = lax.axis_index("fsdp")
    k = f % CORES
    z = f // CORES
    local, d = tokens.shape[1:]
    length = ns * local
    rows = qkv_weight.shape[0]
    ff = up_weight.shape[1]
    w = ff // (nf * ns)
    shard_heads = rows // HD
    spread = shard_heads % ns == 0 and (shard_heads // ns * nz) % 2 == 0
    hw = shard_heads // ns * HD
    one_each = spread and hw == HD and ns % 2 == 0 and nz % 2 == 0
    tiled = w % PAIR == 0
    place = s[None].astype(jnp.int32)
    rank_cols = d // ranks
    pairs = rank_cols // PAIR
    lines = [[CORES * z + c for z in range(nz)] for c in range(CORES)]
    swap = [(i, i ^ 1) for i in range(nf)]
    everyone = ("seq", "fsdp")

    def after(x, *others):
        return lax.optimization_barrier((x,) + others)[0]

    def other_core(x):
        return lax.ppermute(x, "fsdp", swap)

    def plane_send(x, d):
        return lax.ppermute(x, "seq", [(i, i ^ d) for i in range(ns)])

    def plane_pieces(x):
        return [x] + [plane_send(x, d) for d in range(1, ns)]

    def arrange(pieces, dtype):
        size = pieces[0].shape[0]
        whole = jnp.zeros((ns * size,) + pieces[0].shape[1:], dtype)
        for d, piece in enumerate(pieces):
            whole = lax.dynamic_update_slice_in_dim(whole, piece.astype(dtype), (s ^ d) * size, 0)
        return whole

    def pick(x, index, axis):
        return lax.dynamic_index_in_dim(x, index, axis, keepdims=False)

    vectors = (norm_gain, norm_bias, qkv_bias, out_bias, up_bias, down_bias)
    sizes = [v.shape[0] for v in vectors]
    small = jnp.concatenate(vectors)
    small = jnp.broadcast_to(small[None], (nf,) + small.shape)
    small = lax.all_to_all(small, "fsdp", split_axis=0, concat_axis=0, tiled=True)
    cuts, at = [], 0
    for size in sizes:
        cuts.append(small[:, at : at + size].reshape(-1).astype(f32))
        at += size
    gain, nbias, qkvb, outb, upb, downb = cuts

    def heads_of(weight):
        lead = weight.shape[0]
        if spread:
            part = pick(weight.reshape(lead, 3, nz, CORES, ns, hw), s, 4)
            part = part.transpose(0, 3, 1, 2, 4).reshape(lead, CORES, 3, pairs, PAIR)
        else:
            part = pick(weight.reshape(lead, 3, ns, CORES, pairs, PAIR), s, 2)
            part = part.transpose(0, 2, 1, 3, 4)
        return part.transpose(0, 1, 3, 2, 4).reshape(lead, CORES, 3 * rank_cols)

    def units_of(weight):
        lead = weight.shape[0]
        part = pick(weight.reshape(lead, nz, CORES, ns, w), s, 3)
        return part.transpose(0, 2, 1, 3).reshape(lead, CORES, nz * w)

    def core_half(x):
        return lax.dynamic_slice_in_dim(x, k * (x.shape[1] // CORES), x.shape[1] // CORES, 1)

    qkvb_mine = pick(heads_of(qkvb[None])[0], k, 0)
    upb_mine = pick(units_of(upb[None])[0], k, 0)
    tables = rotary_lanes(length)

    up_both = units_of(up_weight) if not tiled else unit_columns(up_weight, place, nz, ns, w)
    up_both = lax.all_gather(up_both.reshape(rows, -1), "fsdp", axis=0, tiled=True)
    up_mine = core_half(up_both)

    qkv_part = heads_of(qkv_weight) if not one_each else head_columns(qkv_weight, place, nz, ns)
    qkv_part = qkv_part.reshape(rows, CORES, -1)
    down_part = lax.dynamic_slice_in_dim(down_weight, s * w, w, 0)
    out_part = lax.dynamic_slice_in_dim(out_weight, s * hw, hw, 0)

    x_pieces = plane_pieces(tokens[0])
    ready = (gain, nbias, qkvb_mine, upb_mine, qkv_part, down_part, out_part) + tuple(tables)
    x_pieces = x_pieces[:1] + [after(piece, *ready) for piece in x_pieces[1:]]
    c_pieces = plane_pieces(after(cotangent[0], *x_pieces[1:]))
    x_pieces = x_pieces + [other_core(piece) for piece in x_pieces]

    down_part = after(down_part, x_pieces[ns - 1])
    down_mine = lax.all_gather(down_part, "fsdp", axis=0, tiled=True, axis_index_groups=lines)

    normed = norm_both(place, x_pieces, gain, nbias)

    qkv_part = after(qkv_part, normed)
    if one_each:
        keep = pick(qkv_part, k, 1)
        got = other_core(pick(qkv_part, 1 - k, 1))
        both = jnp.concatenate([jnp.where(k == 0, keep, got), jnp.where(k == 0, got, keep)])
        wide = hw * d // (CORES * rows)
        beside = out_part.reshape(hw, -1, wide).transpose(1, 0, 2).reshape(CORES * rows, wide)
        both = jnp.concatenate([both, beside], axis=1)
        both = lax.all_gather(both, "fsdp", axis=0, tiled=True, axis_index_groups=lines)
    else:
        qkv_both = lax.all_gather(qkv_part.reshape(rows, -1), "fsdp", axis=0, tiled=True)
        qkv_mine = core_half(qkv_both)
        if spread:
            out_mine = lax.all_gather(out_part, "fsdp", axis=0, tiled=True, axis_index_groups=lines)
        else:
            out_full = lax.all_gather(out_weight, "fsdp", axis=0, tiled=True)
            out_mine = lax.dynamic_slice_in_dim(out_full, (CORES * s + k) * rank_cols, rank_cols, 0)

    def first_first(left, right):
        return lax.dot_general(left, right, (((0,), (0,)), ((), ())), preferred_element_type=f32)

    pinned = after

    class Walk:
        def __init__(self, x):
            self.blocks = x.reshape((nz, -1) + x.shape[1:])
            self.hop = 0
            self.got = None

        def parts(self):
            hop = self.hop + 1
            ends = (jnp.minimum(nz - hop + z, nz - 1), jnp.maximum(hop + z - nz, 0))
            parts = [pick(self.blocks, end, 0) for end in ends]
            if self.got is not None:
                parts = [(p.astype(f32) + g.astype(f32)).astype(bf16) for p, g in zip(parts, self.got)]
            return parts

        def step(self, hops=1, after=None):
            parts = []
            for _ in range(hops):
                if after is not None:
                    self.got = [pinned(g, after) for g in self.got]
                parts = self.parts()
                self.hop += 1
                self.got = [step_line(p, self.hop, way) for p, way in zip(parts, (True, False))]
            return parts

        def rest(self, after=None):
            return self.step(nz - 1 - self.hop, after)

        def own(self):
            own = pick(self.blocks, z, 0).astype(f32)
            return (own + self.got[0].astype(f32) + self.got[1].astype(f32)).astype(bf16)

    def step_line(part, hops, forward):
        hops_ = []
        for c in range(CORES):
            for q in range(hops):
                at, to = (q, q + 1) if forward else (nz - 1 - q, nz - 2 - q)
                hops_.append((CORES * at + c, CORES * to + c))
        return lax.ppermute(part, "fsdp", hops_)

    def both_cores(x):
        keep = lax.dynamic_slice_in_dim(x, k * rows, rows, 0)
        got = other_core(lax.dynamic_slice_in_dim(x, (1 - k) * rows, rows, 0))
        return jnp.stack([jnp.where(k == 0, keep, got), jnp.where(k == 0, got, keep)])

    hidden = plain_dot(normed, up_mine) + upb_mine
    activated, slope = gelu_and_slope(hidden)
    activated = activated.astype(bf16)
    c_pieces = c_pieces[:1] + [after(piece, activated) for piece in c_pieces[1:]]
    c2 = order_both(place, c_pieces + [other_core(piece) for piece in c_pieces])
    down_local = first_first(activated, c2).astype(bf16)
    down_walk = Walk(down_local)
    down_walk.step()
    c2, down_mine = after(c2, down_local), after(down_mine, down_local)
    hidden_grad = (last_last(c2, down_mine) * slope).astype(bf16)
    hidden_grad = after(hidden_grad, *down_walk.step())
    up_local = first_first(normed, hidden_grad).astype(bf16)
    up_walk = Walk(up_local)
    up_walk.step()
    activated = after(activated, up_local)
    ff_branch = plain_dot(activated, down_mine).astype(bf16)
    hidden_grad = after(hidden_grad, ff_branch)
    ff_back = last_last(hidden_grad, up_mine).astype(bf16)

    if one_each:
        both = after(both, ff_back)
        qkv_mine = both[:, : 3 * rank_cols]
        out_mine = both[:, 3 * rank_cols :].reshape(nz, -1, hw, wide).transpose(0, 2, 1, 3)
        out_mine = out_mine.reshape(rank_cols, d)
    normed = after(normed, ff_back, *down_walk.rest())
    mixed = plain_dot(normed, qkv_mine) + qkvb_mine
    mixed = after(mixed, *up_walk.step())
    heads, attended, logsums = attend(mixed, tables, length)
    down_own = down_walk.own()
    down_pieces = plane_pieces(down_own)
    attended = after(attended, down_own)
    out_local = first_first(attended, c2).astype(bf16)
    if spread:
        out_walk = Walk(out_local)
        out_walk.step()
    c2 = after(c2, out_local)
    attended_grad = last_last(c2, out_mine).astype(bf16)
    attended = after(attended, attended_grad)

    def both_halves(left, right, dot, more):
        far = (dot(left[length:], right) + more[length:].astype(f32)).astype(bf16)
        got = other_core(far)
        near = (dot(after(left, far)[:length], right) + more[:length].astype(f32)).astype(bf16)
        return near, got

    def rank_parts(near, got):
        parts = []
        for d in range(ns):
            at = (s ^ d) * local
            part = lax.dynamic_slice_in_dim(near, at, local, 0).astype(f32)
            part = part + lax.dynamic_slice_in_dim(got, at, local, 0).astype(f32)
            parts.append(part if d == 0 else part.astype(bf16))
        return parts

    def rank_sum(parts, *passed):
        total = parts[0]
        for d in range(1, ns):
            total = total + after(plane_send(parts[d], d), *passed).astype(f32)
        return total

    near, got = both_halves(attended, out_mine, plain_dot, ff_branch)
    attended_grad = after(attended_grad, near, *up_walk.rest())
    mixed_grad = attend_back(heads, attended_grad, logsums, tables, length)
    normed = after(normed, mixed_grad)
    qkv_local = first_first(normed, mixed_grad).astype(bf16)
    if spread:
        qkv_walk = Walk(qkv_local)
        qkv_walk.step()
    branch_parts = rank_parts(near, after(got, qkv_local))
    mixed_grad = after(mixed_grad, *branch_parts)
    near, got = both_halves(mixed_grad, qkv_mine, last_last, ff_back)
    up_walk.got = [after(g, near) for g in up_walk.got]
    up_own = up_walk.own()
    up_both = both_cores(up_own)
    passed = [up_both]
    if spread:
        passed += qkv_walk.step(after=up_own)
        passed += out_walk.step(after=up_own)
    up_pieces = plane_pieces(up_both)
    grad_parts = rank_parts(near, after(got, *passed))
    branches = rank_sum(branch_parts, *grad_parts)
    if spread:
        passed = qkv_walk.rest(after=grad_parts[1]) + out_walk.rest(after=grad_parts[1])
    normed_grad = rank_sum(grad_parts, *passed)
    if spread:
        qkv_own, out_own = qkv_walk.own(), out_walk.own()
        out_pieces = plane_pieces(out_own)
    else:
        qkv_own = lax.psum_scatter(
            qkv_local, "fsdp", scatter_dimension=0, tiled=True, axis_index_groups=lines
        )
    qkv_both = both_cores(qkv_own)
    qkv_pieces = plane_pieces(qkv_both)
    up_pieces = up_pieces[:1] + [after(piece, qkv_both) for piece in up_pieces[1:]]
    down_pieces = down_pieces[:1] + [after(piece, near) for piece in down_pieces[1:]]

    token_rows = tokens[0].astype(f32)
    block_out = (token_rows + branches + outb + downb).astype(bf16)[None]

    centred_own = token_rows - jnp.mean(token_rows, axis=-1, keepdims=True)
    variance_own = jnp.mean(centred_own * centred_own, axis=-1, keepdims=True)
    inverse = lax.rsqrt(variance_own + epsilon)
    xhat = centred_own * inverse
    g = normed_grad * gain
    rows_grad = inverse * (
        g - jnp.mean(g, axis=-1, keepdims=True) - xhat * jnp.mean(g * xhat, axis=-1, keepdims=True)
    )
    upstream = cotangent[0].astype(f32)
    tokens_grad = (upstream + rows_grad).astype(bf16)[None]

    if spread and one_each:
        qkv_wgrad = place_heads(place, qkv_pieces, nz)
    elif spread:
        qkv_all = arrange([piece[None] for piece in qkv_pieces], bf16)
        qkv_all = qkv_all.reshape(ns, CORES, rows, pairs, 3, PAIR).transpose(0, 1, 2, 4, 3, 5)
        qkv_all = qkv_all.reshape(ns, CORES, rows, 3, nz, hw)
        qkv_wgrad = qkv_all.transpose(2, 3, 4, 1, 0, 5).reshape(rows, 3 * d).astype(f32)
    else:
        qkv_all = arrange([piece[None] for piece in qkv_pieces], bf16)
        qkv_all = qkv_all.reshape(ns, CORES, rows, pairs, 3, PAIR)
        qkv_wgrad = qkv_all.transpose(2, 4, 0, 1, 3, 5).reshape(rows, 3 * d).astype(f32)
    if spread:
        out_wgrad = arrange(out_pieces, f32)
    else:
        rank = CORES * s + k
        out_padded = lax.dynamic_update_slice_in_dim(
            jnp.zeros((d, d), bf16), out_local, rank * rank_cols, 0
        )
        out_shard = lax.psum_scatter(out_padded, "fsdp", scatter_dimension=0, tiled=True)
        out_wgrad = lax.psum(out_shard.astype(f32), "seq")
    if tiled:
        up_wgrad = place_units(place, up_pieces, nz, w)
    else:
        up_all = arrange([piece[None] for piece in up_pieces], bf16)
        up_all = up_all.reshape(ns, CORES, rows, nz, w)
        up_wgrad = up_all.transpose(2, 3, 1, 0, 4).reshape(rows, ff).astype(f32)
    down_wgrad = arrange(down_pieces, f32)

    mixed_sum = jnp.sum(mixed_grad.astype(f32), axis=0).reshape(pairs, 3, PAIR).transpose(1, 0, 2)
    if spread:
        mixed_sum = mixed_sum.reshape(3, nz, 1, 1, hw)
        mixed_full = jnp.zeros((3, nz, CORES, ns, hw), f32)
        mixed_full = lax.dynamic_update_slice(mixed_full, mixed_sum, (0, 0, k, s, 0))
    else:
        mixed_full = jnp.zeros((3, ns, CORES, rank_cols), f32)
        mixed_full = lax.dynamic_update_slice(
            mixed_full, mixed_sum.reshape(3, 1, 1, rank_cols), (0, s, k, 0)
        )
    hidden_sum = jnp.sum(hidden_grad.astype(f32), axis=0).reshape(nz, 1, 1, w)
    hidden_full = lax.dynamic_update_slice(
        jnp.zeros((nz, CORES, ns, w), f32), hidden_sum, (0, k, s, 0)
    )
    gain_local = jnp.sum(xhat * normed_grad, axis=0)
    nbias_local = jnp.sum(normed_grad, axis=0)
    c_local = jnp.sum(upstream, axis=0)
    sums = (
        mixed_full.reshape(-1)[: 2 * d],
        mixed_full.reshape(-1)[2 * d :],
        hidden_full.reshape(-1),
        gain_local,
        nbias_local,
        c_local,
    )
    flat = jnp.concatenate([v.reshape(nf, -1) for v in sums], axis=1)
    flat = jnp.broadcast_to(flat[None], (ns,) + flat.shape).reshape(ns * nf, -1)
    flat = lax.all_to_all(flat, everyone, split_axis=0, concat_axis=0, tiled=True)
    flat = jnp.sum(flat, axis=0)
    shards, at = [], 0
    for v in sums:
        size = v.shape[0] // nf
        shards.append(flat[at : at + size])
        at += size
    qkv_bgrad, value_bgrad, up_bgrad, gain_grad, norm_bgrad, out_bgrad = shards

    return (
        block_out,
        tokens_grad,
        qkv_wgrad,
        out_wgrad,
        up_wgrad,
        down_wgrad,
        gain_grad,
        norm_bgrad,
        qkv_bgrad,
        value_bgrad,
        out_bgrad,
        up_bgrad,
        out_bgrad,
    )


def solution(mesh):
    sharded = P("fsdp", "seq", None)
    matrix = P("fsdp", None)
    vector = P("fsdp")
    return jax.shard_map(
        functools.partial(on_device, mesh.shape["seq"], mesh.shape["fsdp"]),
        mesh=mesh,
        in_specs=(sharded,) + (matrix,) * 4 + (vector,) * 6 + (sharded,),
        out_specs=(sharded,) * 2 + (matrix,) * 4 + (vector,) * 7,
        check_vma=False,
    )
```

```python
import functools

import jax
import jax.numpy as jnp
from jax import lax
from jax.experimental import pallas as pl
from jax.experimental.pallas import tpu as pltpu
from jax.sharding import PartitionSpec as P

HD = 64
ROT = 32
PAIR = 2 * HD
CORES = 2
BLOCK = 256

epsilon = 1e-05
rope_base = 10000.0
masked_score = -1000000000.0
f32 = jnp.float32
bf16 = jnp.bfloat16


def rotary_lanes(length):
    halves = ROT // 2
    lane = jnp.arange(PAIR) % HD
    frequency = rope_base ** (-(2.0 * (lane % halves).astype(f32)) / ROT)
    angles = jnp.arange(length).astype(f32)[:, None] * frequency[None, :]
    rotated = lane < ROT
    cos = jnp.where(rotated, jnp.cos(angles), 1.0)
    sin = jnp.sin(angles)
    from_right = jnp.where(lane < halves, -sin, 0.0)
    from_left = jnp.where((lane >= halves) & rotated, sin, 0.0)
    return cos, from_right, from_left


def turn(x, cos, from_right, from_left):
    halves = ROT // 2
    return (
        x * cos
        + pltpu.roll(x, PAIR - halves, 1) * from_right
        + pltpu.roll(x, halves, 1) * from_left
    )


def last_last(left, right):
    return lax.dot_general(left, right, (((1,), (1,)), ((), ())), preferred_element_type=f32)


def plain_dot(left, right):
    return jnp.dot(left, right, preferred_element_type=f32)


def head_lanes(head):
    lane = lax.broadcasted_iota(jnp.int32, (1, PAIR), 1)
    return (lane >= head * HD) & (lane < (head + 1) * HD)


def visible_block(block):
    key_place = lax.broadcasted_iota(jnp.int32, (block, block), 0)
    query_place = lax.broadcasted_iota(jnp.int32, (block, block), 1)
    return key_place <= query_place


def attend_kernel(mixed_ref, cos_ref, right_ref, left_ref, heads_ref, out_ref, logsum_ref, turned):
    length = mixed_ref.shape[0]
    block = min(BLOCK, length)
    tables = (cos_ref[...], right_ref[...], left_ref[...])
    heads_ref[:, :PAIR] = (turn(mixed_ref[:, :PAIR], *tables) * HD**-0.5).astype(bf16)
    heads_ref[:, PAIR : 2 * PAIR] = turn(mixed_ref[:, PAIR : 2 * PAIR], *tables).astype(bf16)
    heads_ref[:, 2 * PAIR :] = mixed_ref[:, 2 * PAIR :].astype(bf16)
    values_t = jnp.transpose(mixed_ref[:, 2 * PAIR :]).astype(bf16)
    visible = visible_block(block)
    for head in range(2):
        lanes = head_lanes(head)
        rows = slice(head * HD, (head + 1) * HD)
        for i in range(length // block):
            here = slice(i * block, (i + 1) * block)
            query = heads_ref[here, :PAIR]
            query = jnp.where(lanes, query, jnp.zeros_like(query))
            diag = last_last(heads_ref[here, PAIR : 2 * PAIR], query)
            diag = jnp.where(visible, diag, masked_score)
            highest = jnp.max(diag, axis=0, keepdims=True)
            if i > 0:
                past = last_last(heads_ref[: i * block, PAIR : 2 * PAIR], query)
                highest = jnp.maximum(highest, jnp.max(past, axis=0, keepdims=True))
            diag = jnp.exp(diag - highest)
            total = jnp.sum(diag, axis=0, keepdims=True)
            result = plain_dot(values_t[rows, here], diag.astype(bf16))
            if i > 0:
                past = jnp.exp(past - highest)
                total = total + jnp.sum(past, axis=0, keepdims=True)
                result = result + plain_dot(values_t[rows, : i * block], past.astype(bf16))
            turned[rows, here] = result / total
            logsum_ref[head : head + 1, here] = highest + jnp.log(total)
    out_ref[...] = jnp.transpose(turned[...]).astype(bf16)


def attend_back_kernel(
    heads_ref, grad_ref, logsum_ref, cos_ref, right_ref, left_ref, back_ref, turned, key_sum, value_sum
):
    length = heads_ref.shape[0]
    block = min(BLOCK, length)
    tables = (cos_ref[...], -right_ref[...], -left_ref[...])
    scaled = heads_ref[:, PAIR : 2 * PAIR].astype(f32) * HD**-0.5
    keys_t = jnp.transpose(scaled).astype(bf16)
    visible = visible_block(block)
    key_sum[...] = jnp.zeros_like(key_sum)
    value_sum[...] = jnp.zeros_like(value_sum)
    for head in range(2):
        lanes = head_lanes(head)
        rows = slice(head * HD, (head + 1) * HD)
        for i in range(length // block):
            here = slice(i * block, (i + 1) * block)
            upto = slice(0, (i + 1) * block)
            query = heads_ref[here, :PAIR]
            query = jnp.where(lanes, query, jnp.zeros_like(query))
            grad = grad_ref[here, :]
            grad = jnp.where(lanes, grad, jnp.zeros_like(grad))
            logsum = logsum_ref[head : head + 1, here]
            parts = []
            inner = None
            for begin, end in ((0, i * block), (i * block, (i + 1) * block)):
                if begin == end:
                    continue
                probs = jnp.exp(last_last(heads_ref[begin:end, PAIR : 2 * PAIR], query) - logsum)
                if end > i * block:
                    probs = jnp.where(visible, probs, 0.0)
                prob_grad = last_last(heads_ref[begin:end, 2 * PAIR :], grad)
                term = jnp.sum(probs * prob_grad, axis=0, keepdims=True)
                inner = term if inner is None else inner + term
                parts.append((begin, end, probs, prob_grad))
            query_grad = None
            for begin, end, probs, prob_grad in parts:
                score_grad = (probs * (prob_grad - inner)).astype(bf16)
                value_sum[begin:end, :] += plain_dot(probs.astype(bf16), grad)
                key_sum[begin:end, :] += plain_dot(score_grad, query)
                term = plain_dot(keys_t[rows, begin:end], score_grad)
                query_grad = term if query_grad is None else query_grad + term
            turned[rows, here] = query_grad
    back_ref[:, :PAIR] = turn(jnp.transpose(turned[...]), *tables).astype(bf16)
    back_ref[:, PAIR : 2 * PAIR] = turn(key_sum[...], *tables).astype(bf16)
    back_ref[:, 2 * PAIR :] = value_sum[...].astype(bf16)


def attend(mixed, tables, length):
    count, width = mixed.shape[0] // length, mixed.shape[1]
    pairs = width // (3 * PAIR)
    table = pl.BlockSpec((length, PAIR), lambda n, p: (0, 0))
    wide = pl.BlockSpec((length, 3 * PAIR), lambda n, p: (n, p))
    return pl.pallas_call(
        attend_kernel,
        grid=(count, pairs),
        in_specs=[wide, table, table, table],
        out_specs=[
            wide,
            pl.BlockSpec((length, PAIR), lambda n, p: (n, p)),
            pl.BlockSpec((None, None, 2, length), lambda n, p: (n, p, 0, 0)),
        ],
        out_shape=[
            jax.ShapeDtypeStruct(mixed.shape, bf16),
            jax.ShapeDtypeStruct((count * length, pairs * PAIR), bf16),
            jax.ShapeDtypeStruct((count, pairs, 2, length), f32),
        ],
        scratch_shapes=[pltpu.VMEM((PAIR, length), f32)],
        compiler_params=pltpu.CompilerParams(vmem_limit_bytes=40 * 1024 * 1024),
        cost_estimate=pl.CostEstimate(
            flops=count * pairs * 2 * length * length * 64 * 4,
            bytes_accessed=mixed.size * 8,
            transcendentals=count * pairs * length * length,
        ),
        name="attend",
    )(mixed, *tables)


def attend_back(heads, grad, logsums, tables, length):
    count, width = heads.shape[0] // length, heads.shape[1]
    pairs = width // (3 * PAIR)
    table = pl.BlockSpec((length, PAIR), lambda n, p: (0, 0))
    wide = pl.BlockSpec((length, 3 * PAIR), lambda n, p: (n, p))
    return pl.pallas_call(
        attend_back_kernel,
        grid=(count, pairs),
        in_specs=[
            wide,
            pl.BlockSpec((length, PAIR), lambda n, p: (n, p)),
            pl.BlockSpec((None, None, 2, length), lambda n, p: (n, p, 0, 0)),
            table,
            table,
            table,
        ],
        out_specs=wide,
        out_shape=jax.ShapeDtypeStruct(heads.shape, bf16),
        scratch_shapes=[
            pltpu.VMEM((PAIR, length), f32),
            pltpu.VMEM((length, PAIR), f32),
            pltpu.VMEM((length, PAIR), f32),
        ],
        compiler_params=pltpu.CompilerParams(vmem_limit_bytes=40 * 1024 * 1024),
        cost_estimate=pl.CostEstimate(
            flops=count * pairs * 2 * length * length * 64 * 10,
            bytes_accessed=heads.size * 6,
            transcendentals=count * pairs * length * length,
        ),
        name="attend_back",
    )(heads, grad, logsums, *tables)


def norm_kernel(places_ref, gain_ref, bias_ref, *refs):
    *pieces, out_ref = refs
    for i, piece in enumerate(pieces):

        @pl.when(pl.program_id(0) == i)
        def _(piece=piece):
            x = piece[...].astype(f32)
            centred = x - jnp.mean(x, axis=-1, keepdims=True)
            variance = jnp.mean(centred * centred, axis=-1, keepdims=True)
            out_ref[...] = (
                centred * lax.rsqrt(variance + epsilon) * gain_ref[...] + bias_ref[...]
            ).astype(bf16)


def order_kernel(places_ref, *refs):
    *pieces, out_ref = refs
    for i, piece in enumerate(pieces):

        @pl.when(pl.program_id(0) == i)
        def _(piece=piece):
            out_ref[...] = piece[...].astype(out_ref.dtype)


def order_pieces(kernel, name, places, pieces, vectors=(), dtype=bf16):
    local, d = pieces[0].shape
    fixed = lambda i, places: (0, 0)
    return pl.pallas_call(
        kernel,
        grid_spec=pltpu.PrefetchScalarGridSpec(
            num_scalar_prefetch=1,
            grid=(len(pieces),),
            in_specs=[pl.BlockSpec((1, d), fixed)] * len(vectors)
            + [pl.BlockSpec((local, d), fixed)] * len(pieces),
            out_specs=pl.BlockSpec((local, d), lambda i, places: (places[i], 0)),
        ),
        out_shape=jax.ShapeDtypeStruct((len(pieces) * local, d), dtype),
        compiler_params=pltpu.CompilerParams(vmem_limit_bytes=48 * 1024 * 1024),
        name=name,
    )(places, *[v[None] for v in vectors], *pieces)


def row_blocks(rows):
    return min(64, rows)


def unit_kernel(nz, ns, w, place_ref, in_ref, out_ref):
    for c in range(CORES):
        for q in range(nz):
            at = pl.multiple_of(((q * CORES + c) * ns + place_ref[0]) * w, w)
            to = (c * nz + q) * w
            out_ref[:, to : to + w] = in_ref[:, pl.ds(at, w)]


def unit_columns(weight, place, nz, ns, w):
    rows, ff = weight.shape
    block = row_blocks(rows)
    wide = CORES * nz * w
    return pl.pallas_call(
        functools.partial(unit_kernel, nz, ns, w),
        grid_spec=pltpu.PrefetchScalarGridSpec(
            num_scalar_prefetch=1,
            grid=(rows // block,),
            in_specs=[pl.BlockSpec((block, ff), lambda i, place: (i, 0))],
            out_specs=pl.BlockSpec((block, wide), lambda i, place: (i, 0)),
        ),
        out_shape=jax.ShapeDtypeStruct((rows, wide), weight.dtype),
        name="unit_columns",
    )(place, weight)


def place_units_kernel(nz, w, places_ref, *refs):
    *pieces, out_ref = refs
    ns = len(pieces)
    for i, piece in enumerate(pieces):
        device = places_ref[i]
        for q in range(nz):
            for c in range(CORES):
                to = pl.multiple_of(((q * CORES + c) * ns + device) * w, w)
                out_ref[:, pl.ds(to, w)] = piece[c, :, q * w : (q + 1) * w].astype(f32)


def place_units(places, pieces, nz, w):
    cores, rows, width = pieces[0].shape
    block = row_blocks(rows)
    ff = width * cores * len(pieces)
    return pl.pallas_call(
        functools.partial(place_units_kernel, nz, w),
        grid_spec=pltpu.PrefetchScalarGridSpec(
            num_scalar_prefetch=1,
            grid=(rows // block,),
            in_specs=[pl.BlockSpec((cores, block, width), lambda i, places: (0, i, 0)) for _ in pieces],
            out_specs=pl.BlockSpec((block, ff), lambda i, places: (i, 0)),
        ),
        out_shape=jax.ShapeDtypeStruct((rows, ff), f32),
        name="place_units",
    )(places, *pieces)


def low_half():
    return lax.broadcasted_iota(jnp.int32, (1, PAIR), 1) < HD


def lows(first, second):
    return jnp.where(low_half(), first, pltpu.roll(second, HD, 1))


def highs(first, second):
    return jnp.where(low_half(), pltpu.roll(first, HD, 1), second)


def head_kernel(nz, ns, place_ref, in_ref, out_ref):
    tiles = ns // 2
    part = nz * CORES * tiles
    even = lax.rem(place_ref[0], 2) == 0

    def tile(j, q, c):
        at = (j * part + (q * CORES + c) * tiles + lax.div(place_ref[0], 2)) * PAIR
        return in_ref[:, pl.ds(pl.multiple_of(at, PAIR), PAIR)].astype(f32)

    for c in range(CORES):
        for p in range(nz // 2):
            for j in range(3):
                first, second = tile(j, 2 * p, c), tile(j, 2 * p + 1, c)
                to = ((c * (nz // 2) + p) * 3 + j) * PAIR
                out_ref[:, to : to + PAIR] = jnp.where(
                    even, lows(first, second), highs(first, second)
                ).astype(out_ref.dtype)


def head_columns(weight, place, nz, ns):
    rows, width = weight.shape
    block = row_blocks(rows)
    wide = CORES * nz * 3 * HD
    return pl.pallas_call(
        functools.partial(head_kernel, nz, ns),
        grid_spec=pltpu.PrefetchScalarGridSpec(
            num_scalar_prefetch=1,
            grid=(rows // block,),
            in_specs=[pl.BlockSpec((block, width), lambda i, place: (i, 0))],
            out_specs=pl.BlockSpec((block, wide), lambda i, place: (i, 0)),
        ),
        out_shape=jax.ShapeDtypeStruct((rows, wide), weight.dtype),
        name="head_columns",
    )(place, weight)


def place_heads_kernel(nz, places_ref, *refs):
    *pieces, out_ref = refs
    ns = len(pieces)
    tiles = ns // 2
    even = lax.rem(places_ref[0], 2) == 0
    straight = (places_ref[0] ^ places_ref[1]) == 1
    for a in range(0, ns, 2):
        mates = [(a, a + 1)] if ns != 4 else [((0, 1), (0, 2)), ((2, 3), (1, 3))][a // 2]
        tile = lax.div(places_ref[mates[0][0]] if ns == 4 else places_ref[a], 2)
        if ns == 4:
            tile = jnp.where(straight, tile, lax.div(places_ref[mates[1][0]], 2))
        for j in range(3):
            for p in range(nz // 2):
                at = (p * 3 + j) * PAIR
                for c in range(CORES):
                    loaded = [[pieces[i][c, :, at : at + PAIR].astype(f32) for i in pair] for pair in mates]
                    one, two = loaded[0]
                    if ns == 4:
                        one = jnp.where(straight, one, loaded[1][0])
                        two = jnp.where(straight, two, loaded[1][1])
                    first, second = jnp.where(even, one, two), jnp.where(even, two, one)
                    for q, value in ((2 * p, lows(first, second)), (2 * p + 1, highs(first, second))):
                        to = (((j * nz + q) * CORES + c) * tiles + tile) * PAIR
                        out_ref[:, pl.ds(pl.multiple_of(to, PAIR), PAIR)] = value


def place_heads(places, pieces, nz):
    cores, rows, width = pieces[0].shape
    block = row_blocks(rows)
    whole = width * cores * len(pieces)
    return pl.pallas_call(
        functools.partial(place_heads_kernel, nz),
        grid_spec=pltpu.PrefetchScalarGridSpec(
            num_scalar_prefetch=1,
            grid=(rows // block,),
            in_specs=[pl.BlockSpec((cores, block, width), lambda i, places: (0, i, 0)) for _ in pieces],
            out_specs=pl.BlockSpec((block, whole), lambda i, places: (i, 0)),
        ),
        out_shape=jax.ShapeDtypeStruct((rows, whole), f32),
        name="place_heads",
    )(places, *pieces)


def gelu_and_slope(u):
    cubic = 0.044715
    root = 0.7978845608
    square = u * u
    t = jnp.tanh(root * u * (1.0 + cubic * square))
    value = 0.5 * u * (1.0 + t)
    slope = 0.5 * (1.0 + t) + 0.5 * u * (1.0 - t * t) * root * (1.0 + 3.0 * cubic * square)
    return value, slope


def on_device(
    ns,
    nf,
    tokens,
    qkv_weight,
    out_weight,
    up_weight,
    down_weight,
    norm_gain,
    norm_bias,
    qkv_bias,
    out_bias,
    up_bias,
    down_bias,
    cotangent,
):
    nz = nf // CORES
    ranks = CORES * ns
    s = lax.axis_index("seq")
    f = lax.axis_index("fsdp")
    k = f % CORES
    z = f // CORES
    local, d = tokens.shape[1:]
    length = ns * local
    rows = qkv_weight.shape[0]
    ff = up_weight.shape[1]
    w = ff // (nf * ns)
    shard_heads = rows // HD
    spread = shard_heads % ns == 0 and (shard_heads // ns * nz) % 2 == 0
    hw = shard_heads // ns * HD
    one_each = spread and hw == HD and ns % 2 == 0 and nz % 2 == 0
    tiled = w % PAIR == 0
    place = s[None].astype(jnp.int32)
    rank_cols = d // ranks
    pairs = rank_cols // PAIR
    lines = [[CORES * z + c for z in range(nz)] for c in range(CORES)]
    swap = [(i, i ^ 1) for i in range(nf)]
    everyone = ("seq", "fsdp")

    def after(x, *others):
        return lax.optimization_barrier((x,) + others)[0]

    def other_core(x):
        return lax.ppermute(x, "fsdp", swap)

    two_steps = ns == 4

    def plane_send(x, d):
        return lax.ppermute(x, "seq", [(i, i ^ d) for i in range(ns)])

    def plane_hop(x, second):
        hops = []
        for i in range(ns):
            for g in range(nf):
                hops.append((i * nf + g, (i ^ (1 + (g % CORES ^ second))) * nf + g))
        return lax.ppermute(x, everyone, hops)

    first_hop, second_hop = 1 + k, 2 - k
    steps = [0, first_hop, second_hop, 3] if two_steps else list(range(ns))
    other_steps = [0, second_hop, first_hop, 3] if two_steps else steps
    places = jnp.stack([s ^ step for step in steps]).astype(jnp.int32)
    other_places = jnp.stack([s ^ step for step in other_steps]).astype(jnp.int32)
    both_places = jnp.concatenate([places, ns + other_places])

    def plane_pieces(x, *passed):
        if not two_steps:
            return [x] + [plane_send(x, d) for d in range(1, ns)]
        near, far = plane_hop(x, 0), plane_hop(x, 1)
        return [x, near, far, plane_hop(after(near, *passed), 1)]

    def arrange(pieces, dtype):
        size = pieces[0].shape[0]
        whole = jnp.zeros((ns * size,) + pieces[0].shape[1:], dtype)
        for at, piece in zip(steps, pieces):
            whole = lax.dynamic_update_slice_in_dim(whole, piece.astype(dtype), (s ^ at) * size, 0)
        return whole

    def pick(x, index, axis):
        return lax.dynamic_index_in_dim(x, index, axis, keepdims=False)

    vectors = (norm_gain, norm_bias, qkv_bias, out_bias, up_bias, down_bias)
    sizes = [v.shape[0] for v in vectors]
    small = jnp.concatenate(vectors)
    small = jnp.broadcast_to(small[None], (nf,) + small.shape)
    small = lax.all_to_all(small, "fsdp", split_axis=0, concat_axis=0, tiled=True)
    cuts, at = [], 0
    for size in sizes:
        cuts.append(small[:, at : at + size].reshape(-1).astype(f32))
        at += size
    gain, nbias, qkvb, outb, upb, downb = cuts

    def heads_of(weight):
        lead = weight.shape[0]
        if spread:
            part = pick(weight.reshape(lead, 3, nz, CORES, ns, hw), s, 4)
            part = part.transpose(0, 3, 1, 2, 4).reshape(lead, CORES, 3, pairs, PAIR)
        else:
            part = pick(weight.reshape(lead, 3, ns, CORES, pairs, PAIR), s, 2)
            part = part.transpose(0, 2, 1, 3, 4)
        return part.transpose(0, 1, 3, 2, 4).reshape(lead, CORES, 3 * rank_cols)

    def units_of(weight):
        lead = weight.shape[0]
        part = pick(weight.reshape(lead, nz, CORES, ns, w), s, 3)
        return part.transpose(0, 2, 1, 3).reshape(lead, CORES, nz * w)

    def core_half(x):
        return lax.dynamic_slice_in_dim(x, k * (x.shape[1] // CORES), x.shape[1] // CORES, 1)

    qkvb_mine = pick(heads_of(qkvb[None])[0], k, 0)
    upb_mine = pick(units_of(upb[None])[0], k, 0)
    tables = rotary_lanes(length)

    up_both = units_of(up_weight) if not tiled else unit_columns(up_weight, place, nz, ns, w)
    up_both = lax.all_gather(up_both.reshape(rows, -1), "fsdp", axis=0, tiled=True)
    up_mine = core_half(up_both)

    qkv_part = heads_of(qkv_weight) if not one_each else head_columns(qkv_weight, place, nz, ns)
    qkv_part = qkv_part.reshape(rows, CORES, -1)
    down_part = lax.dynamic_slice_in_dim(down_weight, s * w, w, 0)
    out_part = lax.dynamic_slice_in_dim(out_weight, s * hw, hw, 0)

    x_pieces = plane_pieces(tokens[0])
    ready = (gain, nbias, qkvb_mine, upb_mine, qkv_part, down_part, out_part) + tuple(tables)
    x_pieces = x_pieces[:1] + [after(piece, *ready) for piece in x_pieces[1:]]
    c_pieces = plane_pieces(after(cotangent[0], *x_pieces[1:]))
    x_pieces = x_pieces + [other_core(piece) for piece in x_pieces]

    normed = order_pieces(norm_kernel, "norm_both", both_places, x_pieces, (gain, nbias))

    down_part = after(down_part, x_pieces[ns - 1])
    down_mine = lax.all_gather(down_part, "fsdp", axis=0, tiled=True, axis_index_groups=lines)

    qkv_part = after(qkv_part, normed)
    if one_each:
        keep = pick(qkv_part, k, 1)
        got = other_core(pick(qkv_part, 1 - k, 1))
        both = jnp.concatenate([jnp.where(k == 0, keep, got), jnp.where(k == 0, got, keep)])
        wide = hw * d // (CORES * rows)
        beside = out_part.reshape(hw, -1, wide).transpose(1, 0, 2).reshape(CORES * rows, wide)
        both = jnp.concatenate([both, beside], axis=1)
        both = lax.all_gather(both, "fsdp", axis=0, tiled=True, axis_index_groups=lines)
    else:
        qkv_both = lax.all_gather(qkv_part.reshape(rows, -1), "fsdp", axis=0, tiled=True)
        qkv_mine = core_half(qkv_both)
        if spread:
            out_mine = lax.all_gather(out_part, "fsdp", axis=0, tiled=True, axis_index_groups=lines)
        else:
            out_full = lax.all_gather(out_weight, "fsdp", axis=0, tiled=True)
            out_mine = lax.dynamic_slice_in_dim(out_full, (CORES * s + k) * rank_cols, rank_cols, 0)

    def first_first(left, right):
        return lax.dot_general(left, right, (((0,), (0,)), ((), ())), preferred_element_type=f32)

    pinned = after

    class Walk:
        def __init__(self, x):
            self.blocks = x.reshape((nz, -1) + x.shape[1:])
            self.hop = 0
            self.got = None

        def parts(self):
            hop = self.hop + 1
            ends = (jnp.minimum(nz - hop + z, nz - 1), jnp.maximum(hop + z - nz, 0))
            parts = [pick(self.blocks, end, 0) for end in ends]
            if self.got is not None:
                parts = [(p.astype(f32) + g.astype(f32)).astype(bf16) for p, g in zip(parts, self.got)]
            return parts

        def step(self, hops=1, after=None):
            parts = []
            for _ in range(hops):
                if after is not None:
                    self.got = [pinned(g, after) for g in self.got]
                parts = self.parts()
                self.hop += 1
                self.got = [step_line(p, self.hop, way) for p, way in zip(parts, (True, False))]
            return parts

        def rest(self, after=None):
            return self.step(nz - 1 - self.hop, after)

        def own(self):
            own = pick(self.blocks, z, 0).astype(f32)
            return (own + self.got[0].astype(f32) + self.got[1].astype(f32)).astype(bf16)

    def step_line(part, hops, forward):
        hops_ = []
        for c in range(CORES):
            for q in range(hops):
                at, to = (q, q + 1) if forward else (nz - 1 - q, nz - 2 - q)
                hops_.append((CORES * at + c, CORES * to + c))
        return lax.ppermute(part, "fsdp", hops_)

    def both_cores(x):
        keep = lax.dynamic_slice_in_dim(x, k * rows, rows, 0)
        got = other_core(lax.dynamic_slice_in_dim(x, (1 - k) * rows, rows, 0))
        return jnp.stack([jnp.where(k == 0, keep, got), jnp.where(k == 0, got, keep)])

    def halves(left, right, dot, more=None):
        far = dot(left[length:], right)
        near = dot(left[:length], right)
        if more is not None:
            far, near = far + more[0].astype(f32), near + more[1].astype(f32)
        return far.astype(bf16), near.astype(bf16)

    def rank_parts(near, got):
        parts = []
        for step in steps:
            at = (s ^ step) * local
            part = lax.dynamic_slice_in_dim(near, at, local, 0).astype(f32)
            parts.append(part + lax.dynamic_slice_in_dim(got, at, local, 0).astype(f32))
        return parts[:1] + [part.astype(bf16) for part in parts[1:]]

    def rank_sum(parts, *passed):
        if not two_steps:
            total = parts[0]
            for d in range(1, ns):
                total = total + plane_send(parts[d], d).astype(f32)
            return total
        across = plane_hop(parts[3], 0)
        beside = plane_hop(parts[1], 0)
        across = after(across, *passed)
        rest = plane_hop((parts[2].astype(f32) + across.astype(f32)).astype(bf16), 1)
        return parts[0] + beside.astype(f32) + rest.astype(f32)

    hidden = plain_dot(normed, up_mine) + upb_mine
    activated, slope = gelu_and_slope(hidden)
    activated = activated.astype(bf16)
    c_pieces = c_pieces[:1] + [after(piece, activated) for piece in c_pieces[1:]]
    c2 = order_pieces(order_kernel, "order_both", both_places, c_pieces + [other_core(piece) for piece in c_pieces])
    down_local = first_first(activated, c2).astype(bf16)
    down_walk = Walk(down_local)
    down_walk.step()

    def line_sum(x):
        return lax.psum_scatter(
            x, "fsdp", scatter_dimension=0, tiled=True, axis_index_groups=lines
        )

    c2, down_mine = after(c2, down_local), after(down_mine, down_local)
    hidden_grad = (last_last(c2, down_mine) * slope).astype(bf16)
    up_local = first_first(normed, hidden_grad).astype(bf16)
    up_own = line_sum(up_local)
    activated = after(activated, up_local, *down_walk.step(after=up_local))
    branch_more = halves(activated, down_mine, plain_dot)
    hidden_grad = after(hidden_grad, *branch_more)
    back_more = halves(hidden_grad, up_mine, last_last)

    if one_each:
        both = after(both, *back_more)
        qkv_mine = both[:, : 3 * rank_cols]
        out_mine = both[:, 3 * rank_cols :].reshape(nz, -1, hw, wide).transpose(0, 2, 1, 3)
        out_mine = out_mine.reshape(rank_cols, d)
    normed = after(normed, *down_walk.rest(after=back_more[0]))
    mixed = plain_dot(normed, qkv_mine) + qkvb_mine
    heads, attended, logsums = attend(mixed, tables, length)
    c2 = after(c2, attended)
    attended_grad = last_last(c2, out_mine).astype(bf16)
    attended = after(attended, attended_grad)
    branch_far, branch_near = halves(attended, out_mine, plain_dot, branch_more)
    branch_got = other_core(branch_far)
    attended = after(attended, branch_near)
    out_local = first_first(attended, c2).astype(bf16)
    branch_parts = rank_parts(branch_near, after(branch_got, out_local))
    attended_grad = after(attended_grad, *branch_parts)
    mixed_grad = attend_back(heads, attended_grad, logsums, tables, length)
    normed = after(normed, mixed_grad)
    qkv_local = first_first(normed, mixed_grad).astype(bf16)
    if one_each:
        beside = out_local.reshape(nz, hw, -1, wide).transpose(0, 2, 1, 3).reshape(d, wide)
        beside = jnp.concatenate([qkv_local, beside], axis=1)
        own = line_sum(after(beside, up_own))
        qkv_own = own[:, : 3 * rank_cols]
        out_own = own[:, 3 * rank_cols :].reshape(-1, hw, wide).transpose(1, 0, 2).reshape(hw, d)
    else:
        qkv_own = line_sum(qkv_local)
        out_own = line_sum(out_local) if spread else None
    down_walk.got = [after(g, qkv_local) for g in down_walk.got]
    down_own = down_walk.own()
    branches = rank_sum(branch_parts, down_own)
    mixed_grad = after(mixed_grad, down_own)
    far, near = halves(mixed_grad, qkv_mine, last_last, back_more)
    got = other_core(far)
    down_pieces = plane_pieces(down_own, near)
    up_both = both_cores(after(up_own, near))
    grad_parts = rank_parts(near, after(got, up_both))
    branches = after(branches, *grad_parts)
    up_pieces = plane_pieces(up_both, *grad_parts)
    normed_grad = rank_sum(grad_parts, branches)
    up_pieces = [up_both] + [after(piece, normed_grad) for piece in up_pieces[1:]]
    down_pieces = down_pieces[:1] + [after(piece, *grad_parts) for piece in down_pieces[1:]]
    qkv_both = both_cores(qkv_own)
    qkv_pieces = plane_pieces(qkv_both)
    out_pieces = plane_pieces(after(out_own, qkv_both)) if spread else None

    token_rows = tokens[0].astype(f32)
    block_out = (token_rows + branches + outb + downb).astype(bf16)[None]

    centred_own = token_rows - jnp.mean(token_rows, axis=-1, keepdims=True)
    variance_own = jnp.mean(centred_own * centred_own, axis=-1, keepdims=True)
    inverse = lax.rsqrt(variance_own + epsilon)
    xhat = centred_own * inverse
    g = normed_grad * gain
    rows_grad = inverse * (
        g - jnp.mean(g, axis=-1, keepdims=True) - xhat * jnp.mean(g * xhat, axis=-1, keepdims=True)
    )
    upstream = cotangent[0].astype(f32)
    tokens_grad = (upstream + rows_grad).astype(bf16)[None]

    if spread and one_each:
        qkv_wgrad = place_heads(places, qkv_pieces, nz)
    elif spread:
        qkv_all = arrange([piece[None] for piece in qkv_pieces], bf16)
        qkv_all = qkv_all.reshape(ns, CORES, rows, pairs, 3, PAIR).transpose(0, 1, 2, 4, 3, 5)
        qkv_all = qkv_all.reshape(ns, CORES, rows, 3, nz, hw)
        qkv_wgrad = qkv_all.transpose(2, 3, 4, 1, 0, 5).reshape(rows, 3 * d).astype(f32)
    else:
        qkv_all = arrange([piece[None] for piece in qkv_pieces], bf16)
        qkv_all = qkv_all.reshape(ns, CORES, rows, pairs, 3, PAIR)
        qkv_wgrad = qkv_all.transpose(2, 4, 0, 1, 3, 5).reshape(rows, 3 * d).astype(f32)
    if spread:
        out_wgrad = order_pieces(order_kernel, "place_out", places, out_pieces, dtype=f32)
    else:
        rank = CORES * s + k
        out_padded = lax.dynamic_update_slice_in_dim(
            jnp.zeros((d, d), bf16), out_local, rank * rank_cols, 0
        )
        out_shard = lax.psum_scatter(out_padded, "fsdp", scatter_dimension=0, tiled=True)
        out_wgrad = lax.psum(out_shard.astype(f32), "seq")
    if tiled:
        up_wgrad = place_units(places, up_pieces, nz, w)
    else:
        up_all = arrange([piece[None] for piece in up_pieces], bf16)
        up_all = up_all.reshape(ns, CORES, rows, nz, w)
        up_wgrad = up_all.transpose(2, 3, 1, 0, 4).reshape(rows, ff).astype(f32)
    down_wgrad = order_pieces(order_kernel, "place_down", places, down_pieces, dtype=f32)

    mixed_sum = jnp.sum(mixed_grad.astype(f32), axis=0).reshape(pairs, 3, PAIR).transpose(1, 0, 2)
    if spread:
        mixed_sum = mixed_sum.reshape(3, nz, 1, 1, hw)
        mixed_full = jnp.zeros((3, nz, CORES, ns, hw), f32)
        mixed_full = lax.dynamic_update_slice(mixed_full, mixed_sum, (0, 0, k, s, 0))
    else:
        mixed_full = jnp.zeros((3, ns, CORES, rank_cols), f32)
        mixed_full = lax.dynamic_update_slice(
            mixed_full, mixed_sum.reshape(3, 1, 1, rank_cols), (0, s, k, 0)
        )
    hidden_sum = jnp.sum(hidden_grad.astype(f32), axis=0).reshape(nz, 1, 1, w)
    hidden_full = lax.dynamic_update_slice(
        jnp.zeros((nz, CORES, ns, w), f32), hidden_sum, (0, k, s, 0)
    )
    gain_local = jnp.sum(xhat * normed_grad, axis=0)
    nbias_local = jnp.sum(normed_grad, axis=0)
    c_local = jnp.sum(upstream, axis=0)
    sums = (
        mixed_full.reshape(-1)[: 2 * d],
        mixed_full.reshape(-1)[2 * d :],
        hidden_full.reshape(-1),
        gain_local,
        nbias_local,
        c_local,
    )
    flat = jnp.concatenate([v.reshape(nf, -1) for v in sums], axis=1)
    flat = jnp.broadcast_to(flat[None], (ns,) + flat.shape).reshape(ns * nf, -1)
    flat = lax.all_to_all(flat, everyone, split_axis=0, concat_axis=0, tiled=True)
    flat = jnp.sum(flat, axis=0)
    shards, at = [], 0
    for v in sums:
        size = v.shape[0] // nf
        shards.append(flat[at : at + size])
        at += size
    qkv_bgrad, value_bgrad, up_bgrad, gain_grad, norm_bgrad, out_bgrad = shards

    return (
        block_out,
        tokens_grad,
        qkv_wgrad,
        out_wgrad,
        up_wgrad,
        down_wgrad,
        gain_grad,
        norm_bgrad,
        qkv_bgrad,
        value_bgrad,
        out_bgrad,
        up_bgrad,
        out_bgrad,
    )


def solution(mesh):
    sharded = P("fsdp", "seq", None)
    matrix = P("fsdp", None)
    vector = P("fsdp")
    return jax.shard_map(
        functools.partial(on_device, mesh.shape["seq"], mesh.shape["fsdp"]),
        mesh=mesh,
        in_specs=(sharded,) + (matrix,) * 4 + (vector,) * 6 + (sharded,),
        out_specs=(sharded,) * 2 + (matrix,) * 4 + (vector,) * 7,
        check_vma=False,
    )
```

```python
import functools

import jax
import jax.numpy as jnp
from jax import lax
from jax.experimental import pallas as pl
from jax.experimental.pallas import tpu as pltpu
from jax.sharding import PartitionSpec as P

HD = 64
ROT = 32
PAIR = 2 * HD
CORES = 2
BLOCK = 256

epsilon = 1e-05
rope_base = 10000.0
masked_score = -1000000000.0
f32 = jnp.float32
bf16 = jnp.bfloat16


def rotary_lanes(length):
    halves = ROT // 2
    lane = jnp.arange(PAIR) % HD
    frequency = rope_base ** (-(2.0 * (lane % halves).astype(f32)) / ROT)
    angles = jnp.arange(length).astype(f32)[:, None] * frequency[None, :]
    rotated = lane < ROT
    cos = jnp.where(rotated, jnp.cos(angles), 1.0)
    sin = jnp.sin(angles)
    from_right = jnp.where(lane < halves, -sin, 0.0)
    from_left = jnp.where((lane >= halves) & rotated, sin, 0.0)
    return cos, from_right, from_left


def turn(x, cos, from_right, from_left):
    halves = ROT // 2
    return (
        x * cos
        + pltpu.roll(x, PAIR - halves, 1) * from_right
        + pltpu.roll(x, halves, 1) * from_left
    )


def last_last(left, right):
    return lax.dot_general(left, right, (((1,), (1,)), ((), ())), preferred_element_type=f32)


def plain_dot(left, right):
    return jnp.dot(left, right, preferred_element_type=f32)


def head_lanes(head):
    lane = lax.broadcasted_iota(jnp.int32, (1, PAIR), 1)
    return (lane >= head * HD) & (lane < (head + 1) * HD)


def visible_block(block):
    key_place = lax.broadcasted_iota(jnp.int32, (block, block), 0)
    query_place = lax.broadcasted_iota(jnp.int32, (block, block), 1)
    return key_place <= query_place


def attend_kernel(mixed_ref, cos_ref, right_ref, left_ref, heads_ref, out_ref, logsum_ref, turned):
    length = mixed_ref.shape[0]
    block = min(BLOCK, length)
    tables = (cos_ref[...], right_ref[...], left_ref[...])
    heads_ref[:, :PAIR] = (turn(mixed_ref[:, :PAIR], *tables) * HD**-0.5).astype(bf16)
    heads_ref[:, PAIR : 2 * PAIR] = turn(mixed_ref[:, PAIR : 2 * PAIR], *tables).astype(bf16)
    heads_ref[:, 2 * PAIR :] = mixed_ref[:, 2 * PAIR :].astype(bf16)
    values_t = jnp.transpose(mixed_ref[:, 2 * PAIR :]).astype(bf16)
    visible = visible_block(block)
    for head in range(2):
        lanes = head_lanes(head)
        rows = slice(head * HD, (head + 1) * HD)
        for i in range(length // block):
            here = slice(i * block, (i + 1) * block)
            query = heads_ref[here, :PAIR]
            query = jnp.where(lanes, query, jnp.zeros_like(query))
            diag = last_last(heads_ref[here, PAIR : 2 * PAIR], query)
            diag = jnp.where(visible, diag, masked_score)
            highest = jnp.max(diag, axis=0, keepdims=True)
            if i > 0:
                past = last_last(heads_ref[: i * block, PAIR : 2 * PAIR], query)
                highest = jnp.maximum(highest, jnp.max(past, axis=0, keepdims=True))
            diag = jnp.exp(diag - highest)
            total = jnp.sum(diag, axis=0, keepdims=True)
            result = plain_dot(values_t[rows, here], diag.astype(bf16))
            if i > 0:
                past = jnp.exp(past - highest)
                total = total + jnp.sum(past, axis=0, keepdims=True)
                result = result + plain_dot(values_t[rows, : i * block], past.astype(bf16))
            turned[rows, here] = result / total
            logsum_ref[head : head + 1, here] = highest + jnp.log(total)
    out_ref[...] = jnp.transpose(turned[...]).astype(bf16)


def attend_back_kernel(
    heads_ref, grad_ref, logsum_ref, cos_ref, right_ref, left_ref, back_ref, turned, key_sum, value_sum
):
    length = heads_ref.shape[0]
    block = min(BLOCK, length)
    tables = (cos_ref[...], -right_ref[...], -left_ref[...])
    scaled = heads_ref[:, PAIR : 2 * PAIR].astype(f32) * HD**-0.5
    keys_t = jnp.transpose(scaled).astype(bf16)
    visible = visible_block(block)
    key_sum[...] = jnp.zeros_like(key_sum)
    value_sum[...] = jnp.zeros_like(value_sum)
    for head in range(2):
        lanes = head_lanes(head)
        rows = slice(head * HD, (head + 1) * HD)
        for i in range(length // block):
            here = slice(i * block, (i + 1) * block)
            upto = slice(0, (i + 1) * block)
            query = heads_ref[here, :PAIR]
            query = jnp.where(lanes, query, jnp.zeros_like(query))
            grad = grad_ref[here, :]
            grad = jnp.where(lanes, grad, jnp.zeros_like(grad))
            logsum = logsum_ref[head : head + 1, here]
            parts = []
            inner = None
            for begin, end in ((0, i * block), (i * block, (i + 1) * block)):
                if begin == end:
                    continue
                probs = jnp.exp(last_last(heads_ref[begin:end, PAIR : 2 * PAIR], query) - logsum)
                if end > i * block:
                    probs = jnp.where(visible, probs, 0.0)
                prob_grad = last_last(heads_ref[begin:end, 2 * PAIR :], grad)
                term = jnp.sum(probs * prob_grad, axis=0, keepdims=True)
                inner = term if inner is None else inner + term
                parts.append((begin, end, probs, prob_grad))
            query_grad = None
            for begin, end, probs, prob_grad in parts:
                score_grad = (probs * (prob_grad - inner)).astype(bf16)
                value_sum[begin:end, :] += plain_dot(probs.astype(bf16), grad)
                key_sum[begin:end, :] += plain_dot(score_grad, query)
                term = plain_dot(keys_t[rows, begin:end], score_grad)
                query_grad = term if query_grad is None else query_grad + term
            turned[rows, here] = query_grad
    back_ref[:, :PAIR] = turn(jnp.transpose(turned[...]), *tables).astype(bf16)
    back_ref[:, PAIR : 2 * PAIR] = turn(key_sum[...], *tables).astype(bf16)
    back_ref[:, 2 * PAIR :] = value_sum[...].astype(bf16)


def attend(mixed, tables, length):
    count, width = mixed.shape[0] // length, mixed.shape[1]
    pairs = width // (3 * PAIR)
    table = pl.BlockSpec((length, PAIR), lambda n, p: (0, 0))
    wide = pl.BlockSpec((length, 3 * PAIR), lambda n, p: (n, p))
    return pl.pallas_call(
        attend_kernel,
        grid=(count, pairs),
        in_specs=[wide, table, table, table],
        out_specs=[
            wide,
            pl.BlockSpec((length, PAIR), lambda n, p: (n, p)),
            pl.BlockSpec((None, None, 2, length), lambda n, p: (n, p, 0, 0)),
        ],
        out_shape=[
            jax.ShapeDtypeStruct(mixed.shape, bf16),
            jax.ShapeDtypeStruct((count * length, pairs * PAIR), bf16),
            jax.ShapeDtypeStruct((count, pairs, 2, length), f32),
        ],
        scratch_shapes=[pltpu.VMEM((PAIR, length), f32)],
        compiler_params=pltpu.CompilerParams(vmem_limit_bytes=40 * 1024 * 1024),
        cost_estimate=pl.CostEstimate(
            flops=count * pairs * 2 * length * length * 64 * 4,
            bytes_accessed=mixed.size * 8,
            transcendentals=count * pairs * length * length,
        ),
        name="attend",
    )(mixed, *tables)


def attend_back(heads, grad, logsums, tables, length):
    count, width = heads.shape[0] // length, heads.shape[1]
    pairs = width // (3 * PAIR)
    table = pl.BlockSpec((length, PAIR), lambda n, p: (0, 0))
    wide = pl.BlockSpec((length, 3 * PAIR), lambda n, p: (n, p))
    return pl.pallas_call(
        attend_back_kernel,
        grid=(count, pairs),
        in_specs=[
            wide,
            pl.BlockSpec((length, PAIR), lambda n, p: (n, p)),
            pl.BlockSpec((None, None, 2, length), lambda n, p: (n, p, 0, 0)),
            table,
            table,
            table,
        ],
        out_specs=wide,
        out_shape=jax.ShapeDtypeStruct(heads.shape, bf16),
        scratch_shapes=[
            pltpu.VMEM((PAIR, length), f32),
            pltpu.VMEM((length, PAIR), f32),
            pltpu.VMEM((length, PAIR), f32),
        ],
        compiler_params=pltpu.CompilerParams(vmem_limit_bytes=40 * 1024 * 1024),
        cost_estimate=pl.CostEstimate(
            flops=count * pairs * 2 * length * length * 64 * 10,
            bytes_accessed=heads.size * 6,
            transcendentals=count * pairs * length * length,
        ),
        name="attend_back",
    )(heads, grad, logsums, *tables)


def norm_kernel(places_ref, gain_ref, bias_ref, *refs):
    *pieces, out_ref = refs
    for i, piece in enumerate(pieces):

        @pl.when(pl.program_id(0) == i)
        def _(piece=piece):
            x = piece[...].astype(f32)
            centred = x - jnp.mean(x, axis=-1, keepdims=True)
            variance = jnp.mean(centred * centred, axis=-1, keepdims=True)
            out_ref[...] = (
                centred * lax.rsqrt(variance + epsilon) * gain_ref[...] + bias_ref[...]
            ).astype(bf16)


def order_kernel(places_ref, *refs):
    *pieces, out_ref = refs
    for i, piece in enumerate(pieces):

        @pl.when(pl.program_id(0) == i)
        def _(piece=piece):
            out_ref[...] = piece[...].astype(out_ref.dtype)


def order_pieces(kernel, name, places, pieces, vectors=(), dtype=bf16, size=None):
    local, d = pieces[0].shape
    size = local if size is None else size
    last = local // size - 1
    fixed = lambda i, places: (0, 0)
    return pl.pallas_call(
        kernel,
        grid_spec=pltpu.PrefetchScalarGridSpec(
            num_scalar_prefetch=1,
            grid=(len(pieces),),
            in_specs=[pl.BlockSpec((1, d), fixed)] * len(vectors)
            + [pl.BlockSpec((size, d), lambda i, places: (last, 0))] * len(pieces),
            out_specs=pl.BlockSpec((size, d), lambda i, places: (places[i], 0)),
        ),
        out_shape=jax.ShapeDtypeStruct((len(pieces) * size, d), dtype),
        compiler_params=pltpu.CompilerParams(vmem_limit_bytes=48 * 1024 * 1024),
        name=name,
    )(places, *[v[None] for v in vectors], *pieces)


def row_blocks(rows):
    return min(64, rows)


def unit_kernel(nz, ns, w, place_ref, in_ref, out_ref):
    for c in range(CORES):
        for q in range(nz):
            at = pl.multiple_of(((q * CORES + c) * ns + place_ref[0]) * w, w)
            to = (c * nz + q) * w
            out_ref[:, to : to + w] = in_ref[:, pl.ds(at, w)]


def unit_columns(weight, place, nz, ns, w):
    rows, ff = weight.shape
    block = row_blocks(rows)
    wide = CORES * nz * w
    return pl.pallas_call(
        functools.partial(unit_kernel, nz, ns, w),
        grid_spec=pltpu.PrefetchScalarGridSpec(
            num_scalar_prefetch=1,
            grid=(rows // block,),
            in_specs=[pl.BlockSpec((block, ff), lambda i, place: (i, 0))],
            out_specs=pl.BlockSpec((block, wide), lambda i, place: (i, 0)),
        ),
        out_shape=jax.ShapeDtypeStruct((rows, wide), weight.dtype),
        name="unit_columns",
    )(place, weight)


def place_units_kernel(nz, w, places_ref, *refs):
    *pieces, out_ref = refs
    ns = len(pieces)
    for i, piece in enumerate(pieces):
        for c in range(CORES):
            for q in range(nz):
                core = c ^ places_ref[ns]
                to = pl.multiple_of(((q * CORES + core) * ns + places_ref[i]) * w, w)
                at = (c * nz + q) * w
                out_ref[:, pl.ds(to, w)] = piece[:, at : at + w].astype(f32)


def place_units(places, pieces, rows, nz, w):
    width = pieces[0].shape[1]
    block = row_blocks(rows)
    ff = width * len(pieces)
    return pl.pallas_call(
        functools.partial(place_units_kernel, nz, w),
        grid_spec=pltpu.PrefetchScalarGridSpec(
            num_scalar_prefetch=1,
            grid=(rows // block,),
            in_specs=[pl.BlockSpec((block, width), lambda i, places: (i, 0)) for _ in pieces],
            out_specs=pl.BlockSpec((block, ff), lambda i, places: (i, 0)),
        ),
        out_shape=jax.ShapeDtypeStruct((rows, ff), f32),
        name="place_units",
    )(places, *pieces)


def low_half():
    return lax.broadcasted_iota(jnp.int32, (1, PAIR), 1) < HD


def lows(first, second):
    return jnp.where(low_half(), first, pltpu.roll(second, HD, 1))


def highs(first, second):
    return jnp.where(low_half(), pltpu.roll(first, HD, 1), second)


def head_kernel(nz, ns, place_ref, in_ref, out_ref):
    tiles = ns // 2
    part = nz * CORES * tiles
    even = lax.rem(place_ref[0], 2) == 0

    def tile(j, q, c):
        at = (j * part + (q * CORES + c) * tiles + lax.div(place_ref[0], 2)) * PAIR
        return in_ref[:, pl.ds(pl.multiple_of(at, PAIR), PAIR)].astype(f32)

    for c in range(CORES):
        for p in range(nz // 2):
            for j in range(3):
                first, second = tile(j, 2 * p, c), tile(j, 2 * p + 1, c)
                to = ((c * (nz // 2) + p) * 3 + j) * PAIR
                out_ref[:, to : to + PAIR] = jnp.where(
                    even, lows(first, second), highs(first, second)
                ).astype(out_ref.dtype)


def head_columns(weight, place, nz, ns):
    rows, width = weight.shape
    block = row_blocks(rows)
    wide = CORES * nz * 3 * HD
    return pl.pallas_call(
        functools.partial(head_kernel, nz, ns),
        grid_spec=pltpu.PrefetchScalarGridSpec(
            num_scalar_prefetch=1,
            grid=(rows // block,),
            in_specs=[pl.BlockSpec((block, width), lambda i, place: (i, 0))],
            out_specs=pl.BlockSpec((block, wide), lambda i, place: (i, 0)),
        ),
        out_shape=jax.ShapeDtypeStruct((rows, wide), weight.dtype),
        name="head_columns",
    )(place, weight)


def place_heads_kernel(nz, places_ref, *refs):
    *pieces, out_ref = refs
    ns = len(pieces)
    tiles = ns // 2
    even = lax.rem(places_ref[0], 2) == 0
    straight = (places_ref[0] ^ places_ref[1]) == 1
    for a in range(0, ns, 2):
        mates = [(a, a + 1)] if ns != 4 else [((0, 1), (0, 2)), ((2, 3), (1, 3))][a // 2]
        tile = lax.div(places_ref[mates[0][0]] if ns == 4 else places_ref[a], 2)
        if ns == 4:
            tile = jnp.where(straight, tile, lax.div(places_ref[mates[1][0]], 2))
        for j in range(3):
            for p in range(nz // 2):
                at = (p * 3 + j) * PAIR
                for c in range(CORES):
                    own = slice(c * nz * 3 * HD + at, c * nz * 3 * HD + at + PAIR)
                    loaded = [[pieces[i][:, own].astype(f32) for i in pair] for pair in mates]
                    core = c ^ places_ref[ns]
                    one, two = loaded[0]
                    if ns == 4:
                        one = jnp.where(straight, one, loaded[1][0])
                        two = jnp.where(straight, two, loaded[1][1])
                    first, second = jnp.where(even, one, two), jnp.where(even, two, one)
                    for q, value in ((2 * p, lows(first, second)), (2 * p + 1, highs(first, second))):
                        to = (((j * nz + q) * CORES + core) * tiles + tile) * PAIR
                        out_ref[:, pl.ds(pl.multiple_of(to, PAIR), PAIR)] = value


def place_heads(places, pieces, nz):
    rows = pieces[0].shape[0]
    width = CORES * nz * 3 * HD
    block = row_blocks(rows)
    whole = width * len(pieces)
    return pl.pallas_call(
        functools.partial(place_heads_kernel, nz),
        grid_spec=pltpu.PrefetchScalarGridSpec(
            num_scalar_prefetch=1,
            grid=(rows // block,),
            in_specs=[pl.BlockSpec((block, width), lambda i, places: (i, 0)) for _ in pieces],
            out_specs=pl.BlockSpec((block, whole), lambda i, places: (i, 0)),
        ),
        out_shape=jax.ShapeDtypeStruct((rows, whole), f32),
        name="place_heads",
    )(places, *pieces)


def place_out_kernel(places_ref, *refs):
    *pieces, out_ref = refs
    rows = out_ref.shape[0]
    for i, piece in enumerate(pieces):

        @pl.when(pl.program_id(0) == i)
        def _(piece=piece):
            wide = piece.shape[1]
            for r in range(piece.shape[0] // rows):
                out_ref[:, r * wide : (r + 1) * wide] = piece[r * rows : (r + 1) * rows, :].astype(f32)


def place_out(places, pieces, wide, hw, d):
    rows, width = pieces[0].shape
    return pl.pallas_call(
        place_out_kernel,
        grid_spec=pltpu.PrefetchScalarGridSpec(
            num_scalar_prefetch=1,
            grid=(len(pieces),),
            in_specs=[pl.BlockSpec((rows, wide), lambda i, places: (0, width // wide - 1)) for _ in pieces],
            out_specs=pl.BlockSpec((hw, d), lambda i, places: (places[i], 0)),
        ),
        out_shape=jax.ShapeDtypeStruct((len(pieces) * hw, d), f32),
        name="place_out",
    )(places, *pieces)


def gelu_and_slope(u):
    cubic = 0.044715
    root = 0.7978845608
    square = u * u
    t = jnp.tanh(root * u * (1.0 + cubic * square))
    value = 0.5 * u * (1.0 + t)
    slope = 0.5 * (1.0 + t) + 0.5 * u * (1.0 - t * t) * root * (1.0 + 3.0 * cubic * square)
    return value, slope


def on_device(
    ns,
    nf,
    tokens,
    qkv_weight,
    out_weight,
    up_weight,
    down_weight,
    norm_gain,
    norm_bias,
    qkv_bias,
    out_bias,
    up_bias,
    down_bias,
    cotangent,
):
    nz = nf // CORES
    ranks = CORES * ns
    s = lax.axis_index("seq")
    f = lax.axis_index("fsdp")
    k = f % CORES
    z = f // CORES
    local, d = tokens.shape[1:]
    length = ns * local
    rows = qkv_weight.shape[0]
    ff = up_weight.shape[1]
    w = ff // (nf * ns)
    shard_heads = rows // HD
    spread = shard_heads % ns == 0 and (shard_heads // ns * nz) % 2 == 0
    hw = shard_heads // ns * HD
    one_each = spread and hw == HD and ns % 2 == 0 and nz % 2 == 0
    tiled = w % PAIR == 0
    place = s[None].astype(jnp.int32)
    rank_cols = d // ranks
    pairs = rank_cols // PAIR
    lines = [[CORES * z + c for z in range(nz)] for c in range(CORES)]
    swap = [(i, i ^ 1) for i in range(nf)]
    everyone = ("seq", "fsdp")

    def after(x, *others):
        return lax.optimization_barrier((x,) + others)[0]

    def other_core(x):
        return lax.ppermute(x, "fsdp", swap)

    two_steps = ns == 4

    def plane_send(x, d):
        return lax.ppermute(x, "seq", [(i, i ^ d) for i in range(ns)])

    def plane_hop(x, second):
        hops = []
        for i in range(ns):
            for g in range(nf):
                hops.append((i * nf + g, (i ^ (1 + (g % CORES ^ second))) * nf + g))
        return lax.ppermute(x, everyone, hops)

    first_hop, second_hop = 1 + k, 2 - k
    steps = [0, first_hop, second_hop, 3] if two_steps else list(range(ns))
    other_steps = [0, second_hop, first_hop, 3] if two_steps else steps
    places = jnp.stack([s ^ step for step in steps]).astype(jnp.int32)
    other_places = jnp.stack([s ^ step for step in other_steps]).astype(jnp.int32)
    both_places = jnp.concatenate([places, ns + other_places])
    places = jnp.concatenate([places, k[None].astype(jnp.int32)])

    class Pieces:
        def __init__(self, x):
            self.pieces = [x]
            if two_steps:
                self.pieces += [plane_hop(x, 0), plane_hop(x, 1)]
            else:
                self.pieces += [plane_send(x, d) for d in range(1, ns)]

        def middle(self, *passed):
            if two_steps:
                near = after(self.pieces[1], self.pieces[2], *passed)
                self.pieces.append(plane_hop(near, 1))
                return [near]
            return self.pieces[1:]

        def all(self, *passed):
            return self.pieces[:1] + [after(piece, *passed) for piece in self.pieces[1:]]

    def plane_pieces(x):
        pieces = Pieces(x)
        pieces.middle()
        return pieces.pieces

    def arrange(pieces, dtype):
        size = pieces[0].shape[0]
        whole = jnp.zeros((ns * size,) + pieces[0].shape[1:], dtype)
        for at, piece in zip(steps, pieces):
            whole = lax.dynamic_update_slice_in_dim(whole, piece.astype(dtype), (s ^ at) * size, 0)
        return whole

    def pick(x, index, axis):
        return lax.dynamic_index_in_dim(x, index, axis, keepdims=False)

    vectors = (norm_gain, norm_bias, qkv_bias, out_bias, up_bias, down_bias)
    sizes = [v.shape[0] for v in vectors]
    small = jnp.concatenate(vectors)
    small = jnp.broadcast_to(small[None], (nf,) + small.shape)
    small = lax.all_to_all(small, "fsdp", split_axis=0, concat_axis=0, tiled=True)
    cuts, at = [], 0
    for size in sizes:
        cuts.append(small[:, at : at + size].reshape(-1).astype(f32))
        at += size
    gain, nbias, qkvb, outb, upb, downb = cuts

    def heads_of(weight):
        lead = weight.shape[0]
        if spread:
            part = pick(weight.reshape(lead, 3, nz, CORES, ns, hw), s, 4)
            part = part.transpose(0, 3, 1, 2, 4).reshape(lead, CORES, 3, pairs, PAIR)
        else:
            part = pick(weight.reshape(lead, 3, ns, CORES, pairs, PAIR), s, 2)
            part = part.transpose(0, 2, 1, 3, 4)
        return part.transpose(0, 1, 3, 2, 4).reshape(lead, CORES, 3 * rank_cols)

    def units_of(weight):
        lead = weight.shape[0]
        part = pick(weight.reshape(lead, nz, CORES, ns, w), s, 3)
        return part.transpose(0, 2, 1, 3).reshape(lead, CORES, nz * w)

    def core_half(x):
        return lax.dynamic_slice_in_dim(x, k * (x.shape[1] // CORES), x.shape[1] // CORES, 1)

    qkvb_mine = pick(heads_of(qkvb[None])[0], k, 0)
    upb_mine = pick(units_of(upb[None])[0], k, 0)
    tables = rotary_lanes(length)

    up_part = units_of(up_weight) if not tiled else unit_columns(up_weight, place, nz, ns, w)
    up_part = up_part.reshape(rows, -1)
    down_part = lax.dynamic_slice_in_dim(down_weight, s * w, w, 0)
    merged = up_part.shape[1] == d
    if merged:
        ff_both = lax.all_gather(jnp.concatenate([up_part, down_part]), "fsdp", axis=0, tiled=True)
    else:
        up_both = lax.all_gather(up_part, "fsdp", axis=0, tiled=True)
        down_mine = lax.all_gather(down_part, "fsdp", axis=0, tiled=True, axis_index_groups=lines)

    qkv_part = heads_of(qkv_weight) if not one_each else head_columns(qkv_weight, place, nz, ns)
    qkv_part = qkv_part.reshape(rows, CORES, -1)
    out_part = lax.dynamic_slice_in_dim(out_weight, s * hw, hw, 0)

    x_pieces = plane_pieces(tokens[0])
    ready = (gain, nbias, qkvb_mine, upb_mine, qkv_part, out_part) + tuple(tables)
    x_pieces = x_pieces[:1] + [after(piece, *ready) for piece in x_pieces[1:]]
    c_pieces = plane_pieces(after(cotangent[0], *x_pieces[1:]))
    x_pieces = x_pieces + [other_core(piece) for piece in x_pieces]

    normed = order_pieces(norm_kernel, "norm_both", both_places, x_pieces, (gain, nbias))

    normed = order_pieces(norm_kernel, "norm_both", both_places, x_pieces, (gain, nbias))

    down_part = after(down_part, x_pieces[ns - 1])

    if one_each:
        out_wide = d * hw // rows
        beside = out_part.reshape(hw, -1, out_wide).transpose(1, 0, 2).reshape(rows, out_wide)
        both = jnp.concatenate([qkv_part.reshape(rows, -1), beside], axis=1)
        both = lax.all_gather(after(both, normed), "fsdp", axis=0, tiled=True)
    else:
        qkv_both = lax.all_gather(qkv_part.reshape(rows, -1), "fsdp", axis=0, tiled=True)
        qkv_mine = core_half(qkv_both)
        if spread:
            out_mine = lax.all_gather(out_part, "fsdp", axis=0, tiled=True, axis_index_groups=lines)
        else:
            out_full = lax.all_gather(out_weight, "fsdp", axis=0, tiled=True)
            out_mine = lax.dynamic_slice_in_dim(out_full, (CORES * s + k) * rank_cols, rank_cols, 0)

    def first_first(left, right):
        return lax.dot_general(left, right, (((0,), (0,)), ((), ())), preferred_element_type=f32)

    pinned = after

    class Walk:
        def __init__(self, x):
            self.blocks = x.reshape((nz, -1) + x.shape[1:])
            self.hop = 0
            self.got = None

        def parts(self):
            hop = self.hop + 1
            ends = (jnp.minimum(nz - hop + z, nz - 1), jnp.maximum(hop + z - nz, 0))
            parts = [pick(self.blocks, end, 0) for end in ends]
            if self.got is not None:
                parts = [(p.astype(f32) + g.astype(f32)).astype(bf16) for p, g in zip(parts, self.got)]
            return parts

        def step(self, hops=1, after=None):
            parts = []
            for _ in range(hops):
                if after is not None:
                    self.got = [pinned(g, after) for g in self.got]
                parts = self.parts()
                self.hop += 1
                self.got = [step_line(p, self.hop, way) for p, way in zip(parts, (True, False))]
            return parts

        def rest(self, after=None):
            return self.step(nz - 1 - self.hop, after)

        def own(self):
            own = pick(self.blocks, z, 0).astype(f32)
            return (own + self.got[0].astype(f32) + self.got[1].astype(f32)).astype(bf16)

    def step_line(part, hops, forward):
        hops_ = []
        for c in range(CORES):
            for q in range(hops):
                at, to = (q, q + 1) if forward else (nz - 1 - q, nz - 2 - q)
                hops_.append((CORES * at + c, CORES * to + c))
        return lax.ppermute(part, "fsdp", hops_)

    def pair_cores(x):
        by_core = x.reshape(nz, CORES, rows, -1)
        keep, got = pick(by_core, k, 1), other_core(pick(by_core, 1 - k, 1))
        return jnp.concatenate([keep, got], axis=2).reshape(nz * rows, -1)

    def both_in_order(pieces):
        every = arrange([piece[None] for piece in pieces], bf16).reshape(ns, rows, CORES, -1)
        return jnp.where(k == 0, every, every[:, :, ::-1])

    def halves(left, right, dot, more=None):
        far = dot(left[length:], right)
        near = dot(left[:length], right)
        if more is not None:
            far, near = far + more[0].astype(f32), near + more[1].astype(f32)
        return far.astype(bf16), near.astype(bf16)

    def rank_parts(near, got):
        parts = []
        for step in steps:
            at = (s ^ step) * local
            part = lax.dynamic_slice_in_dim(near, at, local, 0).astype(f32)
            parts.append(part + lax.dynamic_slice_in_dim(got, at, local, 0).astype(f32))
        return parts[:1] + [part.astype(bf16) for part in parts[1:]]

    class RankSum:
        def __init__(self, parts):
            self.parts = parts
            if two_steps:
                self.across, self.beside = plane_hop(parts[3], 0), plane_hop(parts[1], 0)
            else:
                self.others = [plane_send(parts[d], d) for d in range(1, ns)]

        def middle(self, *passed):
            if not two_steps:
                return list(passed)
            across = after(self.across, self.beside, *passed)
            self.rest = (self.parts[2].astype(f32) + across.astype(f32)).astype(bf16)
            return [self.rest]

        def total(self, *passed):
            others = [self.beside, plane_hop(self.rest, 1)] if two_steps else self.others
            total = self.parts[0]
            for other in others:
                total = total + after(other, *passed).astype(f32)
            return total

    def line_sum(x):
        return lax.psum_scatter(
            x, "fsdp", scatter_dimension=0, tiled=True, axis_index_groups=lines
        )

    c_pieces = c_pieces[:1] + [after(piece, normed) for piece in c_pieces[1:]]
    c2 = order_pieces(order_kernel, "order_both", both_places, c_pieces + [other_core(piece) for piece in c_pieces])
    if merged:
        ff_both = after(ff_both, c2).reshape(nz, CORES, rows + w, d)
        up_mine = core_half(ff_both[:, :, :rows].reshape(d, d))
        down_mine = pick(ff_both[:, :, rows:], k, 1).reshape(nz * w, d)
    else:
        up_mine = core_half(up_both)
    hidden = plain_dot(normed, up_mine) + upb_mine
    activated, slope = gelu_and_slope(hidden)
    activated = activated.astype(bf16)
    down_local = first_first(activated, c2).astype(bf16)
    c2 = after(c2, down_local)
    hidden_grad = (last_last(c2, down_mine) * slope).astype(bf16)
    up_local = pair_cores(first_first(normed, hidden_grad).astype(bf16))
    if merged:
        ff_local = [x.reshape(nz, -1, d) for x in (up_local, down_local)]
        ff_local = [jnp.concatenate(ff_local, axis=1).reshape(-1, d)]
    else:
        ff_local = [up_local, down_local]
    ff_own = [line_sum(x) for x in ff_local]

    if one_each:
        both = after(both, *ff_local)
        qkv_mine = lax.dynamic_slice_in_dim(both, k * 3 * rank_cols, 3 * rank_cols, 1)
        out_mine = pick(both.reshape(nz, CORES, rows, -1), k, 1)[:, :, CORES * 3 * rank_cols :]
        out_mine = out_mine.reshape(nz, -1, hw, out_wide).transpose(0, 2, 1, 3).reshape(rank_cols, d)
    normed = after(normed, *ff_local)
    mixed = plain_dot(normed, qkv_mine) + qkvb_mine
    heads, attended, logsums = attend(mixed, tables, length)
    c2 = after(c2, attended)
    attended_grad = last_last(c2, out_mine).astype(bf16)
    attended = after(attended, attended_grad)
    out_local = first_first(attended, c2).astype(bf16)
    beside = []
    if one_each:
        beside = out_local.reshape(nz, hw, -1, out_wide).transpose(0, 2, 1, 3)
        beside = [beside.reshape(nz * rows, out_wide)]
    activated, attended = after(activated, out_local), after(attended, out_local)
    branch_far, branch_near = halves(activated, down_mine, plain_dot, halves(attended, out_mine, plain_dot))
    branch_got = after(other_core(branch_far), branch_near, *beside)
    branch_parts = rank_parts(branch_near, branch_got)
    branch_sum = RankSum(branch_parts)
    attended_grad = after(attended_grad, *branch_parts)
    mixed_grad = attend_back(heads, attended_grad, logsums, tables, length)
    normed = after(normed, mixed_grad)
    qkv_local = first_first(normed, mixed_grad).astype(bf16)
    passed = branch_sum.middle(qkv_local)
    hidden_grad, mixed_grad = after(hidden_grad, *passed), after(mixed_grad, *passed)
    far, near = halves(hidden_grad, up_mine, last_last, halves(mixed_grad, qkv_mine, last_last))
    got = other_core(far)
    branches = branch_sum.total(near)
    attn_local = pair_cores(after(qkv_local, near, branches))
    attn_local = jnp.concatenate([attn_local] + beside, axis=1)
    grad_parts = rank_parts(near, after(got, attn_local))
    grad_sum = RankSum(grad_parts)
    ff_own = [after(x, *grad_parts) for x in ff_own]
    attn_own = line_sum(after(attn_local, *ff_own))
    out_own = line_sum(out_local) if spread and not one_each else None
    ff_pieces = [Pieces(x) for x in ff_own]
    passed = grad_sum.middle(*ff_own)
    normed_grad = grad_sum.total(*passed)
    passed = [normed_grad] + [x for pieces in ff_pieces for x in pieces.middle(*passed)]
    attn_pieces = Pieces(after(attn_own, *passed))

    token_rows = tokens[0].astype(f32)
    block_out = (token_rows + branches + outb + downb).astype(bf16)[None]

    centred_own = token_rows - jnp.mean(token_rows, axis=-1, keepdims=True)
    variance_own = jnp.mean(centred_own * centred_own, axis=-1, keepdims=True)
    inverse = lax.rsqrt(variance_own + epsilon)
    xhat = centred_own * inverse
    g = normed_grad * gain
    rows_grad = inverse * (
        g - jnp.mean(g, axis=-1, keepdims=True) - xhat * jnp.mean(g * xhat, axis=-1, keepdims=True)
    )
    upstream = cotangent[0].astype(f32)
    tokens_grad = (upstream + rows_grad).astype(bf16)[None]

    def everyone_sum(sums):
        flat = jnp.concatenate([v.reshape(nf, -1) for v in sums], axis=1)
        flat = jnp.broadcast_to(flat[None], (ns,) + flat.shape).reshape(ns * nf, -1)
        flat = lax.all_to_all(flat, everyone, split_axis=0, concat_axis=0, tiled=True)
        flat = jnp.sum(flat, axis=0)
        shards, at = [], 0
        for v in sums:
            size = v.shape[0] // nf
            shards.append(flat[at : at + size])
            at += size
        return shards

    mixed_grad, hidden_grad = after(mixed_grad, normed_grad), after(hidden_grad, normed_grad)
    mixed_sum = jnp.sum(mixed_grad.astype(f32), axis=0).reshape(pairs, 3, PAIR).transpose(1, 0, 2)
    if spread:
        mixed_sum = mixed_sum.reshape(3, nz, 1, 1, hw)
        mixed_full = jnp.zeros((3, nz, CORES, ns, hw), f32)
        mixed_full = lax.dynamic_update_slice(mixed_full, mixed_sum, (0, 0, k, s, 0))
    else:
        mixed_full = jnp.zeros((3, ns, CORES, rank_cols), f32)
        mixed_full = lax.dynamic_update_slice(
            mixed_full, mixed_sum.reshape(3, 1, 1, rank_cols), (0, s, k, 0)
        )
    hidden_sum = jnp.sum(hidden_grad.astype(f32), axis=0).reshape(nz, 1, 1, w)
    hidden_full = lax.dynamic_update_slice(
        jnp.zeros((nz, CORES, ns, w), f32), hidden_sum, (0, k, s, 0)
    )
    c_local = jnp.sum(after(cotangent[0], normed_grad).astype(f32), axis=0)
    sums = (
        mixed_full.reshape(-1)[: 2 * d],
        mixed_full.reshape(-1)[2 * d :],
        hidden_full.reshape(-1),
        c_local,
        jnp.sum(xhat * normed_grad, axis=0),
        jnp.sum(normed_grad, axis=0),
    )
    bias_grads = everyone_sum(sums)
    qkv_bgrad, value_bgrad, up_bgrad, out_bgrad, gain_grad, norm_bgrad = bias_grads

    passed = attn_pieces.middle(tokens_grad, *bias_grads)
    ff_pieces = [pieces.all(*passed) for pieces in ff_pieces]
    up_pieces, down_pieces = ff_pieces[0], ff_pieces[-1]
    if tiled:
        up_wgrad = place_units(places, up_pieces, rows, nz, w)
    else:
        up_all = both_in_order(up_pieces).reshape(ns, rows, CORES, nz, w)
        up_wgrad = up_all.transpose(1, 3, 2, 0, 4).reshape(rows, ff).astype(f32)
    down_wgrad = order_pieces(order_kernel, "place_down", places, down_pieces, dtype=f32, size=w)

    attn_pieces = attn_pieces.all(up_wgrad, down_wgrad)
    out_pieces = plane_pieces(out_own) if spread and not one_each else None
    if one_each:
        qkv_wgrad = place_heads(places, attn_pieces, nz)
        out_wgrad = place_out(places, attn_pieces, out_wide, hw, d)
    elif spread:
        qkv_all = both_in_order(attn_pieces).reshape(ns, rows, CORES, pairs, 3, PAIR)
        qkv_all = qkv_all.transpose(0, 2, 1, 4, 3, 5).reshape(ns, CORES, rows, 3, nz, hw)
        qkv_wgrad = qkv_all.transpose(2, 3, 4, 1, 0, 5).reshape(rows, 3 * d).astype(f32)
        out_wgrad = order_pieces(order_kernel, "place_out", places, out_pieces, dtype=f32)
    else:
        qkv_all = both_in_order(attn_pieces).reshape(ns, rows, CORES, pairs, 3, PAIR)
        qkv_wgrad = qkv_all.transpose(1, 4, 0, 2, 3, 5).reshape(rows, 3 * d).astype(f32)
        rank = CORES * s + k
        out_padded = lax.dynamic_update_slice_in_dim(
            jnp.zeros((d, d), bf16), out_local, rank * rank_cols, 0
        )
        out_shard = lax.psum_scatter(out_padded, "fsdp", scatter_dimension=0, tiled=True)
        out_wgrad = lax.psum(out_shard.astype(f32), "seq")
    return (
        block_out,
        tokens_grad,
        qkv_wgrad,
        out_wgrad,
        up_wgrad,
        down_wgrad,
        gain_grad,
        norm_bgrad,
        qkv_bgrad,
        value_bgrad,
        out_bgrad,
        up_bgrad,
        out_bgrad,
    )


def solution(mesh):
    sharded = P("fsdp", "seq", None)
    matrix = P("fsdp", None)
    vector = P("fsdp")
    return jax.shard_map(
        functools.partial(on_device, mesh.shape["seq"], mesh.shape["fsdp"]),
        mesh=mesh,
        in_specs=(sharded,) + (matrix,) * 4 + (vector,) * 6 + (sharded,),
        out_specs=(sharded,) * 2 + (matrix,) * 4 + (vector,) * 7,
        check_vma=False,
    )
```

```python
import functools

import jax
import jax.numpy as jnp
from jax import lax
from jax.experimental import pallas as pl
from jax.experimental.pallas import tpu as pltpu
from jax.sharding import PartitionSpec as P

HD = 64
ROT = 32
PAIR = 2 * HD
CORES = 2
BLOCK = 256

epsilon = 1e-05
rope_base = 10000.0
masked_score = -1000000000.0
f32 = jnp.float32
bf16 = jnp.bfloat16


def rotary_lanes(length):
    halves = ROT // 2
    lane = jnp.arange(PAIR) % HD
    frequency = rope_base ** (-(2.0 * (lane % halves).astype(f32)) / ROT)
    angles = jnp.arange(length).astype(f32)[:, None] * frequency[None, :]
    rotated = lane < ROT
    cos = jnp.where(rotated, jnp.cos(angles), 1.0)
    sin = jnp.sin(angles)
    from_right = jnp.where(lane < halves, -sin, 0.0)
    from_left = jnp.where((lane >= halves) & rotated, sin, 0.0)
    return cos, from_right, from_left


def turn(x, cos, from_right, from_left):
    halves = ROT // 2
    return (
        x * cos
        + pltpu.roll(x, PAIR - halves, 1) * from_right
        + pltpu.roll(x, halves, 1) * from_left
    )


def last_last(left, right):
    return lax.dot_general(left, right, (((1,), (1,)), ((), ())), preferred_element_type=f32)


def plain_dot(left, right):
    return jnp.dot(left, right, preferred_element_type=f32)


def head_lanes(head):
    lane = lax.broadcasted_iota(jnp.int32, (1, PAIR), 1)
    return (lane >= head * HD) & (lane < (head + 1) * HD)


def visible_block(block):
    key_place = lax.broadcasted_iota(jnp.int32, (block, block), 0)
    query_place = lax.broadcasted_iota(jnp.int32, (block, block), 1)
    return key_place <= query_place


def attend_kernel(mixed_ref, cos_ref, right_ref, left_ref, heads_ref, out_ref, logsum_ref, turned):
    length = mixed_ref.shape[0]
    block = min(BLOCK, length)
    tables = (cos_ref[...], right_ref[...], left_ref[...])
    heads_ref[:, :PAIR] = (turn(mixed_ref[:, :PAIR], *tables) * HD**-0.5).astype(bf16)
    heads_ref[:, PAIR : 2 * PAIR] = turn(mixed_ref[:, PAIR : 2 * PAIR], *tables).astype(bf16)
    heads_ref[:, 2 * PAIR :] = mixed_ref[:, 2 * PAIR :].astype(bf16)
    values_t = jnp.transpose(mixed_ref[:, 2 * PAIR :]).astype(bf16)
    visible = visible_block(block)
    for head in range(2):
        lanes = head_lanes(head)
        rows = slice(head * HD, (head + 1) * HD)
        for i in range(length // block):
            here = slice(i * block, (i + 1) * block)
            query = heads_ref[here, :PAIR]
            query = jnp.where(lanes, query, jnp.zeros_like(query))
            diag = last_last(heads_ref[here, PAIR : 2 * PAIR], query)
            diag = jnp.where(visible, diag, masked_score)
            highest = jnp.max(diag, axis=0, keepdims=True)
            if i > 0:
                past = last_last(heads_ref[: i * block, PAIR : 2 * PAIR], query)
                highest = jnp.maximum(highest, jnp.max(past, axis=0, keepdims=True))
            diag = jnp.exp(diag - highest)
            total = jnp.sum(diag, axis=0, keepdims=True)
            result = plain_dot(values_t[rows, here], diag.astype(bf16))
            if i > 0:
                past = jnp.exp(past - highest)
                total = total + jnp.sum(past, axis=0, keepdims=True)
                result = result + plain_dot(values_t[rows, : i * block], past.astype(bf16))
            turned[rows, here] = result / total
            logsum_ref[head : head + 1, here] = highest + jnp.log(total)
    out_ref[...] = jnp.transpose(turned[...]).astype(bf16)


def attend_back_kernel(
    heads_ref, grad_ref, logsum_ref, cos_ref, right_ref, left_ref, back_ref, turned, key_sum, value_sum
):
    length = heads_ref.shape[0]
    block = min(BLOCK, length)
    tables = (cos_ref[...], -right_ref[...], -left_ref[...])
    scaled = heads_ref[:, PAIR : 2 * PAIR].astype(f32) * HD**-0.5
    keys_t = jnp.transpose(scaled).astype(bf16)
    visible = visible_block(block)
    key_sum[...] = jnp.zeros_like(key_sum)
    value_sum[...] = jnp.zeros_like(value_sum)
    for head in range(2):
        lanes = head_lanes(head)
        rows = slice(head * HD, (head + 1) * HD)
        for i in range(length // block):
            here = slice(i * block, (i + 1) * block)
            upto = slice(0, (i + 1) * block)
            query = heads_ref[here, :PAIR]
            query = jnp.where(lanes, query, jnp.zeros_like(query))
            grad = grad_ref[here, :]
            grad = jnp.where(lanes, grad, jnp.zeros_like(grad))
            logsum = logsum_ref[head : head + 1, here]
            parts = []
            inner = None
            for begin, end in ((0, i * block), (i * block, (i + 1) * block)):
                if begin == end:
                    continue
                probs = jnp.exp(last_last(heads_ref[begin:end, PAIR : 2 * PAIR], query) - logsum)
                if end > i * block:
                    probs = jnp.where(visible, probs, 0.0)
                prob_grad = last_last(heads_ref[begin:end, 2 * PAIR :], grad)
                term = jnp.sum(probs * prob_grad, axis=0, keepdims=True)
                inner = term if inner is None else inner + term
                parts.append((begin, end, probs, prob_grad))
            query_grad = None
            for begin, end, probs, prob_grad in parts:
                score_grad = (probs * (prob_grad - inner)).astype(bf16)
                value_sum[begin:end, :] += plain_dot(probs.astype(bf16), grad)
                key_sum[begin:end, :] += plain_dot(score_grad, query)
                term = plain_dot(keys_t[rows, begin:end], score_grad)
                query_grad = term if query_grad is None else query_grad + term
            turned[rows, here] = query_grad
    back_ref[:, :PAIR] = turn(jnp.transpose(turned[...]), *tables).astype(bf16)
    back_ref[:, PAIR : 2 * PAIR] = turn(key_sum[...], *tables).astype(bf16)
    back_ref[:, 2 * PAIR :] = value_sum[...].astype(bf16)


def attend(mixed, tables, length):
    count, width = mixed.shape[0] // length, mixed.shape[1]
    pairs = width // (3 * PAIR)
    table = pl.BlockSpec((length, PAIR), lambda n, p: (0, 0))
    wide = pl.BlockSpec((length, 3 * PAIR), lambda n, p: (n, p))
    return pl.pallas_call(
        attend_kernel,
        grid=(count, pairs),
        in_specs=[wide, table, table, table],
        out_specs=[
            wide,
            pl.BlockSpec((length, PAIR), lambda n, p: (n, p)),
            pl.BlockSpec((None, None, 2, length), lambda n, p: (n, p, 0, 0)),
        ],
        out_shape=[
            jax.ShapeDtypeStruct(mixed.shape, bf16),
            jax.ShapeDtypeStruct((count * length, pairs * PAIR), bf16),
            jax.ShapeDtypeStruct((count, pairs, 2, length), f32),
        ],
        scratch_shapes=[pltpu.VMEM((PAIR, length), f32)],
        compiler_params=pltpu.CompilerParams(vmem_limit_bytes=40 * 1024 * 1024),
        cost_estimate=pl.CostEstimate(
            flops=count * pairs * 2 * length * length * 64 * 4,
            bytes_accessed=mixed.size * 8,
            transcendentals=count * pairs * length * length,
        ),
        name="attend",
    )(mixed, *tables)


def attend_back(heads, grad, logsums, tables, length):
    count, width = heads.shape[0] // length, heads.shape[1]
    pairs = width // (3 * PAIR)
    table = pl.BlockSpec((length, PAIR), lambda n, p: (0, 0))
    wide = pl.BlockSpec((length, 3 * PAIR), lambda n, p: (n, p))
    return pl.pallas_call(
        attend_back_kernel,
        grid=(count, pairs),
        in_specs=[
            wide,
            pl.BlockSpec((length, PAIR), lambda n, p: (n, p)),
            pl.BlockSpec((None, None, 2, length), lambda n, p: (n, p, 0, 0)),
            table,
            table,
            table,
        ],
        out_specs=wide,
        out_shape=jax.ShapeDtypeStruct(heads.shape, bf16),
        scratch_shapes=[
            pltpu.VMEM((PAIR, length), f32),
            pltpu.VMEM((length, PAIR), f32),
            pltpu.VMEM((length, PAIR), f32),
        ],
        compiler_params=pltpu.CompilerParams(vmem_limit_bytes=40 * 1024 * 1024),
        cost_estimate=pl.CostEstimate(
            flops=count * pairs * 2 * length * length * 64 * 10,
            bytes_accessed=heads.size * 6,
            transcendentals=count * pairs * length * length,
        ),
        name="attend_back",
    )(heads, grad, logsums, *tables)


def norm_kernel(rows, places_ref, gain_ref, bias_ref, *refs):
    *pieces, out_ref, near_ref, far_ref = refs
    core = places_ref[len(pieces)]
    for i, piece in enumerate(pieces):

        @pl.when(pl.program_id(0) == i)
        def _(piece=piece):
            x = piece[...].astype(f32)
            centred = x - jnp.mean(x, axis=-1, keepdims=True)
            variance = jnp.mean(centred * centred, axis=-1, keepdims=True)
            out_ref[...] = (
                centred * lax.rsqrt(variance + epsilon) * gain_ref[...] + bias_ref[...]
            ).astype(bf16)

    for q in range(near_ref.shape[1] // rows):
        for side, half_ref in ((core, near_ref), (1 - core, far_ref)):
            at = pl.multiple_of((q * CORES + side) * rows, rows)
            half_ref[:, q * rows : (q + 1) * rows] = out_ref[:, pl.ds(at, rows)]


def norm_pieces(places, pieces, gain, bias, rows):
    local, d = pieces[0].shape
    fixed = lambda i, places: (0, 0)
    there = lambda i, places: (places[i], 0)
    count = len(pieces) * local
    return pl.pallas_call(
        functools.partial(norm_kernel, rows),
        grid_spec=pltpu.PrefetchScalarGridSpec(
            num_scalar_prefetch=1,
            grid=(len(pieces),),
            in_specs=[pl.BlockSpec((1, d), fixed)] * 2 + [pl.BlockSpec((local, d), fixed)] * len(pieces),
            out_specs=[
                pl.BlockSpec((local, d), there),
                pl.BlockSpec((local, d // CORES), there),
                pl.BlockSpec((local, d // CORES), there),
            ],
        ),
        out_shape=[
            jax.ShapeDtypeStruct((count, d), bf16),
            jax.ShapeDtypeStruct((count, d // CORES), bf16),
            jax.ShapeDtypeStruct((count, d // CORES), bf16),
        ],
        compiler_params=pltpu.CompilerParams(vmem_limit_bytes=48 * 1024 * 1024),
        name="norm_pieces",
    )(places, gain[None], bias[None], *pieces)


def order_kernel(places_ref, *refs):
    *pieces, out_ref = refs
    for i, piece in enumerate(pieces):

        @pl.when(pl.program_id(0) == i)
        def _(piece=piece):
            out_ref[...] = piece[...].astype(out_ref.dtype)


def order_pieces(kernel, name, places, pieces, vectors=(), dtype=bf16, size=None):
    local, d = pieces[0].shape
    size = local if size is None else size
    last = local // size - 1
    fixed = lambda i, places: (0, 0)
    return pl.pallas_call(
        kernel,
        grid_spec=pltpu.PrefetchScalarGridSpec(
            num_scalar_prefetch=1,
            grid=(len(pieces),),
            in_specs=[pl.BlockSpec((1, d), fixed)] * len(vectors)
            + [pl.BlockSpec((size, d), lambda i, places: (last, 0))] * len(pieces),
            out_specs=pl.BlockSpec((size, d), lambda i, places: (places[i], 0)),
        ),
        out_shape=jax.ShapeDtypeStruct((len(pieces) * size, d), dtype),
        compiler_params=pltpu.CompilerParams(vmem_limit_bytes=48 * 1024 * 1024),
        name=name,
    )(places, *[v[None] for v in vectors], *pieces)


def row_blocks(rows):
    return min(64, rows)


def unit_kernel(nz, ns, w, place_ref, in_ref, out_ref):
    for c in range(CORES):
        for q in range(nz):
            at = pl.multiple_of(((q * CORES + c) * ns + place_ref[0]) * w, w)
            to = (c * nz + q) * w
            out_ref[:, to : to + w] = in_ref[:, pl.ds(at, w)]


def unit_columns(weight, place, nz, ns, w):
    rows, ff = weight.shape
    block = row_blocks(rows)
    wide = CORES * nz * w
    return pl.pallas_call(
        functools.partial(unit_kernel, nz, ns, w),
        grid_spec=pltpu.PrefetchScalarGridSpec(
            num_scalar_prefetch=1,
            grid=(rows // block,),
            in_specs=[pl.BlockSpec((block, ff), lambda i, place: (i, 0))],
            out_specs=pl.BlockSpec((block, wide), lambda i, place: (i, 0)),
        ),
        out_shape=jax.ShapeDtypeStruct((rows, wide), weight.dtype),
        name="unit_columns",
    )(place, weight)


def place_units_kernel(nz, w, places_ref, *refs):
    *pieces, out_ref = refs
    ns = len(pieces)
    for i, piece in enumerate(pieces):
        for c in range(CORES):
            for q in range(nz):
                core = c ^ places_ref[ns]
                to = pl.multiple_of(((q * CORES + core) * ns + places_ref[i]) * w, w)
                at = (c * nz + q) * w
                out_ref[:, pl.ds(to, w)] = piece[:, at : at + w].astype(f32)


def place_units(places, pieces, rows, nz, w):
    width = pieces[0].shape[1]
    block = row_blocks(rows)
    ff = width * len(pieces)
    return pl.pallas_call(
        functools.partial(place_units_kernel, nz, w),
        grid_spec=pltpu.PrefetchScalarGridSpec(
            num_scalar_prefetch=1,
            grid=(rows // block,),
            in_specs=[pl.BlockSpec((block, width), lambda i, places: (i, 0)) for _ in pieces],
            out_specs=pl.BlockSpec((block, ff), lambda i, places: (i, 0)),
        ),
        out_shape=jax.ShapeDtypeStruct((rows, ff), f32),
        name="place_units",
    )(places, *pieces)


def low_half():
    return lax.broadcasted_iota(jnp.int32, (1, PAIR), 1) < HD


def lows(first, second):
    return jnp.where(low_half(), first, pltpu.roll(second, HD, 1))


def highs(first, second):
    return jnp.where(low_half(), pltpu.roll(first, HD, 1), second)


def head_kernel(nz, ns, place_ref, in_ref, out_ref):
    tiles = ns // 2
    part = nz * CORES * tiles
    even = lax.rem(place_ref[0], 2) == 0

    def tile(j, q, c):
        at = (j * part + (q * CORES + c) * tiles + lax.div(place_ref[0], 2)) * PAIR
        return in_ref[:, pl.ds(pl.multiple_of(at, PAIR), PAIR)].astype(f32)

    for c in range(CORES):
        for p in range(nz // 2):
            for j in range(3):
                first, second = tile(j, 2 * p, c), tile(j, 2 * p + 1, c)
                to = ((c * (nz // 2) + p) * 3 + j) * PAIR
                out_ref[:, to : to + PAIR] = jnp.where(
                    even, lows(first, second), highs(first, second)
                ).astype(out_ref.dtype)


def head_columns(weight, place, nz, ns):
    rows, width = weight.shape
    block = row_blocks(rows)
    wide = CORES * nz * 3 * HD
    return pl.pallas_call(
        functools.partial(head_kernel, nz, ns),
        grid_spec=pltpu.PrefetchScalarGridSpec(
            num_scalar_prefetch=1,
            grid=(rows // block,),
            in_specs=[pl.BlockSpec((block, width), lambda i, place: (i, 0))],
            out_specs=pl.BlockSpec((block, wide), lambda i, place: (i, 0)),
        ),
        out_shape=jax.ShapeDtypeStruct((rows, wide), weight.dtype),
        name="head_columns",
    )(place, weight)


def place_heads_kernel(nz, places_ref, *refs):
    *pieces, out_ref = refs
    ns = len(pieces)
    tiles = ns // 2
    even = lax.rem(places_ref[0], 2) == 0
    straight = (places_ref[0] ^ places_ref[1]) == 1
    for a in range(0, ns, 2):
        mates = [(a, a + 1)] if ns != 4 else [((0, 1), (0, 2)), ((2, 3), (1, 3))][a // 2]
        tile = lax.div(places_ref[mates[0][0]] if ns == 4 else places_ref[a], 2)
        if ns == 4:
            tile = jnp.where(straight, tile, lax.div(places_ref[mates[1][0]], 2))
        for j in range(3):
            for p in range(nz // 2):
                at = (p * 3 + j) * PAIR
                for c in range(CORES):
                    own = slice(c * nz * 3 * HD + at, c * nz * 3 * HD + at + PAIR)
                    loaded = [[pieces[i][:, own].astype(f32) for i in pair] for pair in mates]
                    core = c ^ places_ref[ns]
                    one, two = loaded[0]
                    if ns == 4:
                        one = jnp.where(straight, one, loaded[1][0])
                        two = jnp.where(straight, two, loaded[1][1])
                    first, second = jnp.where(even, one, two), jnp.where(even, two, one)
                    for q, value in ((2 * p, lows(first, second)), (2 * p + 1, highs(first, second))):
                        to = (((j * nz + q) * CORES + core) * tiles + tile) * PAIR
                        out_ref[:, pl.ds(pl.multiple_of(to, PAIR), PAIR)] = value


def place_heads(places, pieces, nz):
    rows = pieces[0].shape[0]
    width = CORES * nz * 3 * HD
    block = row_blocks(rows)
    whole = width * len(pieces)
    return pl.pallas_call(
        functools.partial(place_heads_kernel, nz),
        grid_spec=pltpu.PrefetchScalarGridSpec(
            num_scalar_prefetch=1,
            grid=(rows // block,),
            in_specs=[pl.BlockSpec((block, width), lambda i, places: (i, 0)) for _ in pieces],
            out_specs=pl.BlockSpec((block, whole), lambda i, places: (i, 0)),
        ),
        out_shape=jax.ShapeDtypeStruct((rows, whole), f32),
        name="place_heads",
    )(places, *pieces)


def place_out_kernel(places_ref, *refs):
    *pieces, out_ref = refs
    rows = out_ref.shape[0]
    for i, piece in enumerate(pieces):

        @pl.when(pl.program_id(0) == i)
        def _(piece=piece):
            wide = piece.shape[1]
            for r in range(piece.shape[0] // rows):
                out_ref[:, r * wide : (r + 1) * wide] = piece[r * rows : (r + 1) * rows, :].astype(f32)


def place_out(places, pieces, wide, hw, d):
    rows, width = pieces[0].shape
    return pl.pallas_call(
        place_out_kernel,
        grid_spec=pltpu.PrefetchScalarGridSpec(
            num_scalar_prefetch=1,
            grid=(len(pieces),),
            in_specs=[pl.BlockSpec((rows, wide), lambda i, places: (0, width // wide - 1)) for _ in pieces],
            out_specs=pl.BlockSpec((hw, d), lambda i, places: (places[i], 0)),
        ),
        out_shape=jax.ShapeDtypeStruct((len(pieces) * hw, d), f32),
        name="place_out",
    )(places, *pieces)


def pack_kernel(near_ref, got_ref, out_ref, packed_ref):
    width = near_ref.shape[1]
    hw = out_ref.shape[0]
    wide = packed_ref.shape[1] - 2 * width
    packed_ref[:, :width] = near_ref[...]
    packed_ref[:, width : 2 * width] = got_ref[...]
    for i in range(out_ref.shape[1] // wide):
        packed_ref[i * hw : (i + 1) * hw, 2 * width :] = out_ref[:, i * wide : (i + 1) * wide]


def pack(near, got, out_local, rows, hw):
    count, width = near.shape
    d = out_local.shape[1]
    whole = 2 * width + d * hw // rows
    half = pl.BlockSpec((rows, width), lambda i: (i, 0))
    return pl.pallas_call(
        pack_kernel,
        grid=(count // rows,),
        in_specs=[half, half, pl.BlockSpec((hw, d), lambda i: (i, 0))],
        out_specs=pl.BlockSpec((rows, whole), lambda i: (i, 0)),
        out_shape=jax.ShapeDtypeStruct((count, whole), bf16),
        name="pack",
    )(near, got, out_local)


def two_products_kernel(first_ref, first_right_ref, second_ref, second_right_ref, far_ref, near_ref):
    def products(out_ref):
        width = out_ref.shape[1]
        step = min(512, width)
        for at in range(0, width, step):
            columns = slice(at, at + step)
            out_ref[:, columns] = (
                last_last(first_ref[...], first_right_ref[columns, :])
                + last_last(second_ref[...], second_right_ref[columns, :])
            ).astype(bf16)

    half = pl.num_programs(0) // 2
    pl.when(pl.program_id(0) < half)(lambda: products(far_ref))
    pl.when(pl.program_id(0) >= half)(lambda: products(near_ref))


def two_products(first, first_right, second, second_right):
    rows = first.shape[0] // 2
    block = min(512, rows)
    half = rows // block
    width = first_right.shape[0]

    def left(x):
        return pl.BlockSpec((block, x.shape[1]), lambda i: (lax.rem(i + half, 2 * half), 0))

    def right(x):
        return pl.BlockSpec(x.shape, lambda i: (0, 0))

    depth = first.shape[1] + second.shape[1]
    out = jax.ShapeDtypeStruct((rows, width), bf16)
    return pl.pallas_call(
        two_products_kernel,
        grid=(2 * half,),
        in_specs=[left(first), right(first_right), left(second), right(second_right)],
        out_specs=[
            pl.BlockSpec((block, width), lambda i: (jnp.minimum(i, half - 1), 0)),
            pl.BlockSpec((block, width), lambda i: (jnp.maximum(i - half, 0), 0)),
        ],
        out_shape=[out, out],
        compiler_params=pltpu.CompilerParams(vmem_limit_bytes=48 * 1024 * 1024),
        cost_estimate=pl.CostEstimate(
            flops=4 * rows * width * depth,
            bytes_accessed=2 * (2 * rows + width) * depth + 4 * rows * width,
            transcendentals=0,
        ),
        name="two_products",
    )(first, first_right, second, second_right)


def gelu_and_slope(u):
    cubic = 0.044715
    root = 0.7978845608
    square = u * u
    t = jnp.tanh(root * u * (1.0 + cubic * square))
    value = 0.5 * u * (1.0 + t)
    slope = 0.5 * (1.0 + t) + 0.5 * u * (1.0 - t * t) * root * (1.0 + 3.0 * cubic * square)
    return value, slope


def on_device(
    ns,
    nf,
    tokens,
    qkv_weight,
    out_weight,
    up_weight,
    down_weight,
    norm_gain,
    norm_bias,
    qkv_bias,
    out_bias,
    up_bias,
    down_bias,
    cotangent,
):
    nz = nf // CORES
    ranks = CORES * ns
    s = lax.axis_index("seq")
    f = lax.axis_index("fsdp")
    k = f % CORES
    z = f // CORES
    local, d = tokens.shape[1:]
    length = ns * local
    rows = qkv_weight.shape[0]
    ff = up_weight.shape[1]
    w = ff // (nf * ns)
    shard_heads = rows // HD
    spread = shard_heads % ns == 0 and (shard_heads // ns * nz) % 2 == 0
    hw = shard_heads // ns * HD
    one_each = spread and hw == HD and ns % 2 == 0 and nz % 2 == 0
    tiled = w % PAIR == 0
    place = s[None].astype(jnp.int32)
    rank_cols = d // ranks
    pairs = rank_cols // PAIR
    lines = [[CORES * z + c for z in range(nz)] for c in range(CORES)]
    swap = [(i, i ^ 1) for i in range(nf)]
    everyone = ("seq", "fsdp")

    def after(x, *others):
        return lax.optimization_barrier((x,) + others)[0]

    def other_core(x):
        return lax.ppermute(x, "fsdp", swap)

    two_steps = ns == 4

    def plane_send(x, d):
        return lax.ppermute(x, "seq", [(i, i ^ d) for i in range(ns)])

    def plane_hop(x, second):
        hops = []
        for i in range(ns):
            for g in range(nf):
                hops.append((i * nf + g, (i ^ (1 + (g % CORES ^ second))) * nf + g))
        return lax.ppermute(x, everyone, hops)

    first_hop, second_hop = 1 + k, 2 - k
    steps = [0, first_hop, second_hop, 3] if two_steps else list(range(ns))
    other_steps = [0, second_hop, first_hop, 3] if two_steps else steps
    places = jnp.stack([s ^ step for step in steps]).astype(jnp.int32)
    other_places = jnp.stack([s ^ step for step in other_steps]).astype(jnp.int32)
    both_places = jnp.concatenate([places, ns + other_places])
    places = jnp.concatenate([places, k[None].astype(jnp.int32)])

    class Pieces:
        def __init__(self, x):
            self.pieces = [x]
            if two_steps:
                self.pieces += [plane_hop(x, 0), plane_hop(x, 1)]
            else:
                self.pieces += [plane_send(x, d) for d in range(1, ns)]

        def middle(self, *passed):
            if two_steps:
                near = after(self.pieces[1], self.pieces[2], *passed)
                self.pieces.append(plane_hop(near, 1))
                return [near]
            return self.pieces[1:]

        def all(self, *passed):
            return self.pieces[:1] + [after(piece, *passed) for piece in self.pieces[1:]]

    def plane_pieces(x):
        pieces = Pieces(x)
        pieces.middle()
        return pieces.pieces

    def arrange(pieces, dtype):
        size = pieces[0].shape[0]
        whole = jnp.zeros((ns * size,) + pieces[0].shape[1:], dtype)
        for at, piece in zip(steps, pieces):
            whole = lax.dynamic_update_slice_in_dim(whole, piece.astype(dtype), (s ^ at) * size, 0)
        return whole

    def pick(x, index, axis):
        return lax.dynamic_index_in_dim(x, index, axis, keepdims=False)

    vectors = (norm_gain, norm_bias, qkv_bias, out_bias, up_bias, down_bias)
    sizes = [v.shape[0] for v in vectors]
    small = jnp.concatenate(vectors)
    small = jnp.broadcast_to(small[None], (nf,) + small.shape)
    small = lax.all_to_all(small, "fsdp", split_axis=0, concat_axis=0, tiled=True)
    cuts, at = [], 0
    for size in sizes:
        cuts.append(small[:, at : at + size].reshape(-1).astype(f32))
        at += size
    gain, nbias, qkvb, outb, upb, downb = cuts

    def heads_of(weight):
        lead = weight.shape[0]
        if spread:
            part = pick(weight.reshape(lead, 3, nz, CORES, ns, hw), s, 4)
            part = part.transpose(0, 3, 1, 2, 4).reshape(lead, CORES, 3, pairs, PAIR)
        else:
            part = pick(weight.reshape(lead, 3, ns, CORES, pairs, PAIR), s, 2)
            part = part.transpose(0, 2, 1, 3, 4)
        return part.transpose(0, 1, 3, 2, 4).reshape(lead, CORES, 3 * rank_cols)

    def units_of(weight):
        lead = weight.shape[0]
        part = pick(weight.reshape(lead, nz, CORES, ns, w), s, 3)
        return part.transpose(0, 2, 1, 3).reshape(lead, CORES, nz * w)

    def core_half(x):
        return lax.dynamic_slice_in_dim(x, k * (x.shape[1] // CORES), x.shape[1] // CORES, 1)

    qkvb_mine = pick(heads_of(qkvb[None])[0], k, 0)
    upb_mine = pick(units_of(upb[None])[0], k, 0)
    tables = rotary_lanes(length)

    up_part = units_of(up_weight) if not tiled else unit_columns(up_weight, place, nz, ns, w)
    up_part = up_part.reshape(rows, -1)
    down_part = lax.dynamic_slice_in_dim(down_weight, s * w, w, 0)
    merged = up_part.shape[1] == d
    if merged:
        ff_both = lax.all_gather(jnp.concatenate([up_part, down_part]), "fsdp", axis=0, tiled=True)
    else:
        up_both = lax.all_gather(up_part, "fsdp", axis=0, tiled=True)
        down_mine = lax.all_gather(down_part, "fsdp", axis=0, tiled=True, axis_index_groups=lines)

    qkv_part = heads_of(qkv_weight) if not one_each else head_columns(qkv_weight, place, nz, ns)
    qkv_part = qkv_part.reshape(rows, CORES, -1)
    out_part = lax.dynamic_slice_in_dim(out_weight, s * hw, hw, 0)

    x_pieces = plane_pieces(tokens[0])
    ready = (gain, nbias, qkvb_mine, upb_mine, qkv_part, out_part) + tuple(tables)
    x_pieces = x_pieces[:1] + [after(piece, *ready) for piece in x_pieces[1:]]
    c_pieces = plane_pieces(after(cotangent[0], *x_pieces[1:]))
    x_pieces = x_pieces + [other_core(piece) for piece in x_pieces]

    norm_places = jnp.concatenate([both_places, k[None].astype(jnp.int32)])
    normed, normed_near, normed_far = norm_pieces(norm_places, x_pieces, gain, nbias, rows)

    if one_each:
        out_wide = d * hw // rows
        beside = out_part.reshape(hw, -1, out_wide).transpose(1, 0, 2).reshape(rows, out_wide)
        both = jnp.concatenate([qkv_part.reshape(rows, -1), beside], axis=1)
        both = lax.all_gather(after(both, normed), "fsdp", axis=0, tiled=True)
    else:
        qkv_both = lax.all_gather(qkv_part.reshape(rows, -1), "fsdp", axis=0, tiled=True)
        qkv_mine = core_half(qkv_both)
        if spread:
            out_mine = lax.all_gather(out_part, "fsdp", axis=0, tiled=True, axis_index_groups=lines)
        else:
            out_full = lax.all_gather(out_weight, "fsdp", axis=0, tiled=True)
            out_mine = lax.dynamic_slice_in_dim(out_full, (CORES * s + k) * rank_cols, rank_cols, 0)

    def first_first(left, right):
        return lax.dot_general(left, right, (((0,), (0,)), ((), ())), preferred_element_type=f32)

    def pair_cores(x):
        by_core = x.reshape(nz, CORES, rows, -1)
        keep, got = pick(by_core, k, 1), other_core(pick(by_core, 1 - k, 1))
        return jnp.concatenate([keep, got], axis=2).reshape(nz * rows, -1)

    def both_in_order(pieces):
        every = arrange([piece[None] for piece in pieces], bf16).reshape(ns, rows, CORES, -1)
        return jnp.where(k == 0, every, every[:, :, ::-1])

    def halves(left, right, dot, more=None):
        far = dot(left[length:], right)
        near = dot(left[:length], right)
        if more is not None:
            far, near = far + more[0].astype(f32), near + more[1].astype(f32)
        return far.astype(bf16), near.astype(bf16)

    def rank_parts(near, got):
        parts = []
        for step in steps:
            at = (s ^ step) * local
            part = lax.dynamic_slice_in_dim(near, at, local, 0).astype(f32)
            parts.append(part + lax.dynamic_slice_in_dim(got, at, local, 0).astype(f32))
        return parts[:1] + [part.astype(bf16) for part in parts[1:]]

    class RankSum:
        def __init__(self, parts):
            self.parts = parts
            if two_steps:
                self.across, self.beside = plane_hop(parts[3], 0), plane_hop(parts[1], 0)
            else:
                self.others = [plane_send(parts[d], d) for d in range(1, ns)]

        def first(self):
            return [self.across, self.beside] if two_steps else self.others

        def middle(self, *passed):
            if not two_steps:
                return list(passed)
            across = after(self.across, self.beside, *passed)
            self.rest = (self.parts[2].astype(f32) + across.astype(f32)).astype(bf16)
            return [self.rest]

        def total(self, *passed):
            others = [self.beside, plane_hop(self.rest, 1)] if two_steps else self.others
            total = self.parts[0]
            for other in others:
                total = total + after(other, *passed).astype(f32)
            return total

    def line_sum(x):
        return lax.psum_scatter(
            x, "fsdp", scatter_dimension=0, tiled=True, axis_index_groups=lines
        )

    c_pieces = c_pieces[:1] + [after(piece, normed) for piece in c_pieces[1:]]
    c2 = order_pieces(order_kernel, "order_both", both_places, c_pieces + [other_core(piece) for piece in c_pieces])
    if merged:
        ff_both = after(ff_both, c2).reshape(nz, CORES, rows + w, d)
        up_mine = core_half(ff_both[:, :, :rows].reshape(d, d))
        down_mine = pick(ff_both[:, :, rows:], k, 1).reshape(nz * w, d)
    else:
        up_mine = core_half(up_both)
    hidden = plain_dot(normed, up_mine) + upb_mine
    activated, slope = gelu_and_slope(hidden)
    activated = activated.astype(bf16)
    down_local = first_first(activated, c2).astype(bf16)
    c2 = after(c2, down_local)
    hidden_grad = (last_last(c2, down_mine) * slope).astype(bf16)
    up_local = pair_cores(first_first(normed, hidden_grad).astype(bf16))
    if merged:
        ff_local = [x.reshape(nz, -1, d) for x in (up_local, down_local)]
        ff_local = [jnp.concatenate(ff_local, axis=1).reshape(-1, d)]
    else:
        ff_local = [up_local, down_local]
    ff_own = [line_sum(x) for x in ff_local]

    if one_each:
        both = after(both, *ff_local)
        qkv_mine = lax.dynamic_slice_in_dim(both, k * 3 * rank_cols, 3 * rank_cols, 1)
        out_mine = pick(both.reshape(nz, CORES, rows, -1), k, 1)[:, :, CORES * 3 * rank_cols :]
        out_mine = out_mine.reshape(nz, -1, hw, out_wide).transpose(0, 2, 1, 3).reshape(rank_cols, d)
    normed = after(normed, *ff_local)
    mixed = plain_dot(normed, qkv_mine) + qkvb_mine
    heads, attended, logsums = attend(mixed, tables, length)
    c2 = after(c2, attended)
    attended_grad = last_last(c2, out_mine).astype(bf16)
    attended = after(attended, attended_grad)
    out_local = first_first(attended, c2).astype(bf16)
    activated, attended = after(activated, out_local), after(attended, out_local)
    branch_far, branch_near = halves(activated, down_mine, plain_dot, halves(attended, out_mine, plain_dot))
    branch_got = after(other_core(branch_far), branch_near)
    branch_parts = rank_parts(branch_near, branch_got)
    branch_sum = RankSum(branch_parts)
    attended_grad = after(attended_grad, *branch_parts)
    mixed_grad = attend_back(heads, attended_grad, logsums, tables, length)
    normed_far = after(normed_far, mixed_grad)
    qkv_far = first_first(normed_far, mixed_grad).astype(bf16)
    qkv_got = other_core(qkv_far)
    normed_near = after(normed_near, qkv_far)
    qkv_near = first_first(normed_near, mixed_grad).astype(bf16)
    passed = branch_sum.middle(qkv_near)
    hidden_grad, mixed_grad = after(hidden_grad, *passed), after(mixed_grad, qkv_got)
    far, near = two_products(hidden_grad, up_mine, mixed_grad, qkv_mine)
    got = other_core(far)
    if one_each:
        attn_local = pack(qkv_near, after(qkv_got, near), out_local, rows, hw)
    else:
        attn_local = jnp.concatenate([qkv_near, qkv_got], axis=1)
    grad_parts = rank_parts(near, after(got, attn_local))
    grad_sum = RankSum(grad_parts)
    branches = branch_sum.total(*grad_parts)
    mixed_grad, hidden_grad = after(mixed_grad, branches), after(hidden_grad, branches)
    mixed_sum = jnp.sum(mixed_grad.astype(f32), axis=0).reshape(pairs, 3, PAIR).transpose(1, 0, 2)
    if spread:
        mixed_sum = mixed_sum.reshape(3, nz, 1, 1, hw)
        mixed_full = jnp.zeros((3, nz, CORES, ns, hw), f32)
        mixed_full = lax.dynamic_update_slice(mixed_full, mixed_sum, (0, 0, k, s, 0))
    else:
        mixed_full = jnp.zeros((3, ns, CORES, rank_cols), f32)
        mixed_full = lax.dynamic_update_slice(
            mixed_full, mixed_sum.reshape(3, 1, 1, rank_cols), (0, s, k, 0)
        )
    hidden_sum = jnp.sum(hidden_grad.astype(f32), axis=0).reshape(nz, 1, 1, w)
    hidden_full = lax.dynamic_update_slice(
        jnp.zeros((nz, CORES, ns, w), f32), hidden_sum, (0, k, s, 0)
    )
    c_local = jnp.sum(after(cotangent[0], branches).astype(f32), axis=0)
    passed = (branches, mixed_full, hidden_full, c_local)
    ff_own = [after(x, *passed, *grad_sum.first()) for x in ff_own]
    attn_own = line_sum(after(attn_local, *ff_own))
    out_own = line_sum(out_local) if spread and not one_each else None
    ff_pieces = [Pieces(x) for x in ff_own]
    passed = grad_sum.middle(*ff_own)
    normed_grad = grad_sum.total(*passed)

    token_rows = tokens[0].astype(f32)
    block_out = (token_rows + branches + outb + downb).astype(bf16)[None]

    centred_own = token_rows - jnp.mean(token_rows, axis=-1, keepdims=True)
    variance_own = jnp.mean(centred_own * centred_own, axis=-1, keepdims=True)
    inverse = lax.rsqrt(variance_own + epsilon)
    xhat = centred_own * inverse
    g = normed_grad * gain
    rows_grad = inverse * (
        g - jnp.mean(g, axis=-1, keepdims=True) - xhat * jnp.mean(g * xhat, axis=-1, keepdims=True)
    )
    upstream = cotangent[0].astype(f32)
    tokens_grad = (upstream + rows_grad).astype(bf16)[None]

    passed = [x for pieces in ff_pieces for x in pieces.middle(tokens_grad)]
    attn_pieces = Pieces(after(attn_own, *passed))
    ff_pieces = [pieces.all(attn_pieces.pieces[0]) for pieces in ff_pieces]
    up_pieces, down_pieces = ff_pieces[0], ff_pieces[-1]
    if tiled:
        up_wgrad = place_units(places, up_pieces, rows, nz, w)
    else:
        up_all = both_in_order(up_pieces).reshape(ns, rows, CORES, nz, w)
        up_wgrad = up_all.transpose(1, 3, 2, 0, 4).reshape(rows, ff).astype(f32)
    passed = attn_pieces.middle(up_wgrad)
    down_pieces = down_pieces[:1] + [after(piece, *passed) for piece in down_pieces[1:]]
    down_wgrad = order_pieces(order_kernel, "place_down", places, down_pieces, dtype=f32, size=w)

    def everyone_sum(sums):
        flat = jnp.concatenate([v.reshape(nf, -1) for v in sums], axis=1)
        flat = jnp.broadcast_to(flat[None], (ns,) + flat.shape).reshape(ns * nf, -1)
        flat = lax.all_to_all(after(flat, *passed), everyone, split_axis=0, concat_axis=0, tiled=True)
        flat = jnp.sum(flat, axis=0)
        shards, at = [], 0
        for v in sums:
            size = v.shape[0] // nf
            shards.append(flat[at : at + size])
            at += size
        return shards

    sums = (
        mixed_full.reshape(-1)[: 2 * d],
        mixed_full.reshape(-1)[2 * d :],
        hidden_full.reshape(-1),
        c_local,
        jnp.sum(xhat * normed_grad, axis=0),
        jnp.sum(normed_grad, axis=0),
    )
    bias_grads = everyone_sum(sums)
    qkv_bgrad, value_bgrad, up_bgrad, out_bgrad, gain_grad, norm_bgrad = bias_grads

    attn_pieces = attn_pieces.all()
    out_pieces = plane_pieces(out_own) if spread and not one_each else None
    if one_each:
        qkv_wgrad = place_heads(places, attn_pieces, nz)
        out_wgrad = place_out(places, attn_pieces, out_wide, hw, d)
    elif spread:
        qkv_all = both_in_order(attn_pieces).reshape(ns, rows, CORES, pairs, 3, PAIR)
        qkv_all = qkv_all.transpose(0, 2, 1, 4, 3, 5).reshape(ns, CORES, rows, 3, nz, hw)
        qkv_wgrad = qkv_all.transpose(2, 3, 4, 1, 0, 5).reshape(rows, 3 * d).astype(f32)
        out_wgrad = order_pieces(order_kernel, "place_out", places, out_pieces, dtype=f32)
    else:
        qkv_all = both_in_order(attn_pieces).reshape(ns, rows, CORES, pairs, 3, PAIR)
        qkv_wgrad = qkv_all.transpose(1, 4, 0, 2, 3, 5).reshape(rows, 3 * d).astype(f32)
        rank = CORES * s + k
        out_padded = lax.dynamic_update_slice_in_dim(
            jnp.zeros((d, d), bf16), out_local, rank * rank_cols, 0
        )
        out_shard = lax.psum_scatter(out_padded, "fsdp", scatter_dimension=0, tiled=True)
        out_wgrad = lax.psum(out_shard.astype(f32), "seq")
    return (
        block_out,
        tokens_grad,
        qkv_wgrad,
        out_wgrad,
        up_wgrad,
        down_wgrad,
        gain_grad,
        norm_bgrad,
        qkv_bgrad,
        value_bgrad,
        out_bgrad,
        up_bgrad,
        out_bgrad,
    )


def solution(mesh):
    sharded = P("fsdp", "seq", None)
    matrix = P("fsdp", None)
    vector = P("fsdp")
    return jax.shard_map(
        functools.partial(on_device, mesh.shape["seq"], mesh.shape["fsdp"]),
        mesh=mesh,
        in_specs=(sharded,) + (matrix,) * 4 + (vector,) * 6 + (sharded,),
        out_specs=(sharded,) * 2 + (matrix,) * 4 + (vector,) * 7,
        check_vma=False,
    )
```

```python
import functools

import jax
import jax.numpy as jnp
from jax import lax
from jax.experimental import pallas as pl
from jax.experimental.pallas import tpu as pltpu
from jax.sharding import PartitionSpec as P

HD = 64
ROT = 32
PAIR = 2 * HD
CORES = 2
BLOCK = 256

epsilon = 1e-05
rope_base = 10000.0
masked_score = -1000000000.0
f32 = jnp.float32
bf16 = jnp.bfloat16


def rotary_lanes(length):
    halves = ROT // 2
    lane = jnp.arange(PAIR) % HD
    frequency = rope_base ** (-(2.0 * (lane % halves).astype(f32)) / ROT)
    angles = jnp.arange(length).astype(f32)[:, None] * frequency[None, :]
    rotated = lane < ROT
    cos = jnp.where(rotated, jnp.cos(angles), 1.0)
    sin = jnp.sin(angles)
    from_right = jnp.where(lane < halves, -sin, 0.0)
    from_left = jnp.where((lane >= halves) & rotated, sin, 0.0)
    return cos, from_right, from_left


def turn(x, cos, from_right, from_left):
    halves = ROT // 2
    return (
        x * cos
        + pltpu.roll(x, PAIR - halves, 1) * from_right
        + pltpu.roll(x, halves, 1) * from_left
    )


def last_last(left, right):
    return lax.dot_general(left, right, (((1,), (1,)), ((), ())), preferred_element_type=f32)


def plain_dot(left, right):
    return jnp.dot(left, right, preferred_element_type=f32)


def head_lanes(head):
    lane = lax.broadcasted_iota(jnp.int32, (1, PAIR), 1)
    return (lane >= head * HD) & (lane < (head + 1) * HD)


def visible_block(block):
    key_place = lax.broadcasted_iota(jnp.int32, (block, block), 0)
    query_place = lax.broadcasted_iota(jnp.int32, (block, block), 1)
    return key_place <= query_place


def attend_kernel(mixed_ref, cos_ref, right_ref, left_ref, heads_ref, out_ref, logsum_ref, turned):
    length = mixed_ref.shape[0]
    block = min(BLOCK, length)
    tables = (cos_ref[...], right_ref[...], left_ref[...])
    heads_ref[:, :PAIR] = (turn(mixed_ref[:, :PAIR], *tables) * HD**-0.5).astype(bf16)
    heads_ref[:, PAIR : 2 * PAIR] = turn(mixed_ref[:, PAIR : 2 * PAIR], *tables).astype(bf16)
    heads_ref[:, 2 * PAIR :] = mixed_ref[:, 2 * PAIR :].astype(bf16)
    values_t = jnp.transpose(mixed_ref[:, 2 * PAIR :]).astype(bf16)
    visible = visible_block(block)
    for head in range(2):
        lanes = head_lanes(head)
        rows = slice(head * HD, (head + 1) * HD)
        for i in range(length // block):
            here = slice(i * block, (i + 1) * block)
            query = heads_ref[here, :PAIR]
            query = jnp.where(lanes, query, jnp.zeros_like(query))
            diag = last_last(heads_ref[here, PAIR : 2 * PAIR], query)
            diag = jnp.where(visible, diag, masked_score)
            highest = jnp.max(diag, axis=0, keepdims=True)
            if i > 0:
                past = last_last(heads_ref[: i * block, PAIR : 2 * PAIR], query)
                highest = jnp.maximum(highest, jnp.max(past, axis=0, keepdims=True))
            diag = jnp.exp(diag - highest)
            total = jnp.sum(diag, axis=0, keepdims=True)
            result = plain_dot(values_t[rows, here], diag.astype(bf16))
            if i > 0:
                past = jnp.exp(past - highest)
                total = total + jnp.sum(past, axis=0, keepdims=True)
                result = result + plain_dot(values_t[rows, : i * block], past.astype(bf16))
            turned[rows, here] = result / total
            logsum_ref[head : head + 1, here] = highest + jnp.log(total)
    out_ref[...] = jnp.transpose(turned[...]).astype(bf16)


def attend_back_kernel(
    heads_ref, grad_ref, logsum_ref, cos_ref, right_ref, left_ref, back_ref, turned, key_sum, value_sum
):
    length = heads_ref.shape[0]
    block = min(BLOCK, length)
    tables = (cos_ref[...], -right_ref[...], -left_ref[...])
    scaled = heads_ref[:, PAIR : 2 * PAIR].astype(f32) * HD**-0.5
    keys_t = jnp.transpose(scaled).astype(bf16)
    visible = visible_block(block)
    key_sum[...] = jnp.zeros_like(key_sum)
    value_sum[...] = jnp.zeros_like(value_sum)
    for head in range(2):
        lanes = head_lanes(head)
        rows = slice(head * HD, (head + 1) * HD)
        for i in range(length // block):
            here = slice(i * block, (i + 1) * block)
            upto = slice(0, (i + 1) * block)
            query = heads_ref[here, :PAIR]
            query = jnp.where(lanes, query, jnp.zeros_like(query))
            grad = grad_ref[here, :]
            grad = jnp.where(lanes, grad, jnp.zeros_like(grad))
            logsum = logsum_ref[head : head + 1, here]
            parts = []
            inner = None
            for begin, end in ((0, i * block), (i * block, (i + 1) * block)):
                if begin == end:
                    continue
                probs = jnp.exp(last_last(heads_ref[begin:end, PAIR : 2 * PAIR], query) - logsum)
                if end > i * block:
                    probs = jnp.where(visible, probs, 0.0)
                prob_grad = last_last(heads_ref[begin:end, 2 * PAIR :], grad)
                term = jnp.sum(probs * prob_grad, axis=0, keepdims=True)
                inner = term if inner is None else inner + term
                parts.append((begin, end, probs, prob_grad))
            query_grad = None
            for begin, end, probs, prob_grad in parts:
                score_grad = (probs * (prob_grad - inner)).astype(bf16)
                value_sum[begin:end, :] += plain_dot(probs.astype(bf16), grad)
                key_sum[begin:end, :] += plain_dot(score_grad, query)
                term = plain_dot(keys_t[rows, begin:end], score_grad)
                query_grad = term if query_grad is None else query_grad + term
            turned[rows, here] = query_grad
    back_ref[:, :PAIR] = turn(jnp.transpose(turned[...]), *tables).astype(bf16)
    back_ref[:, PAIR : 2 * PAIR] = turn(key_sum[...], *tables).astype(bf16)
    back_ref[:, 2 * PAIR :] = value_sum[...].astype(bf16)


def attend(mixed, tables, length):
    count, width = mixed.shape[0] // length, mixed.shape[1]
    pairs = width // (3 * PAIR)
    table = pl.BlockSpec((length, PAIR), lambda n, p: (0, 0))
    wide = pl.BlockSpec((length, 3 * PAIR), lambda n, p: (n, p))
    return pl.pallas_call(
        attend_kernel,
        grid=(count, pairs),
        in_specs=[wide, table, table, table],
        out_specs=[
            wide,
            pl.BlockSpec((length, PAIR), lambda n, p: (n, p)),
            pl.BlockSpec((None, None, 2, length), lambda n, p: (n, p, 0, 0)),
        ],
        out_shape=[
            jax.ShapeDtypeStruct(mixed.shape, bf16),
            jax.ShapeDtypeStruct((count * length, pairs * PAIR), bf16),
            jax.ShapeDtypeStruct((count, pairs, 2, length), f32),
        ],
        scratch_shapes=[pltpu.VMEM((PAIR, length), f32)],
        compiler_params=pltpu.CompilerParams(vmem_limit_bytes=40 * 1024 * 1024),
        cost_estimate=pl.CostEstimate(
            flops=count * pairs * 2 * length * length * 64 * 4,
            bytes_accessed=mixed.size * 8,
            transcendentals=count * pairs * length * length,
        ),
        name="attend",
    )(mixed, *tables)


def attend_back(heads, grad, logsums, tables, length):
    count, width = heads.shape[0] // length, heads.shape[1]
    pairs = width // (3 * PAIR)
    table = pl.BlockSpec((length, PAIR), lambda n, p: (0, 0))
    wide = pl.BlockSpec((length, 3 * PAIR), lambda n, p: (n, p))
    return pl.pallas_call(
        attend_back_kernel,
        grid=(count, pairs),
        in_specs=[
            wide,
            pl.BlockSpec((length, PAIR), lambda n, p: (n, p)),
            pl.BlockSpec((None, None, 2, length), lambda n, p: (n, p, 0, 0)),
            table,
            table,
            table,
        ],
        out_specs=wide,
        out_shape=jax.ShapeDtypeStruct(heads.shape, bf16),
        scratch_shapes=[
            pltpu.VMEM((PAIR, length), f32),
            pltpu.VMEM((length, PAIR), f32),
            pltpu.VMEM((length, PAIR), f32),
        ],
        compiler_params=pltpu.CompilerParams(vmem_limit_bytes=40 * 1024 * 1024),
        cost_estimate=pl.CostEstimate(
            flops=count * pairs * 2 * length * length * 64 * 10,
            bytes_accessed=heads.size * 6,
            transcendentals=count * pairs * length * length,
        ),
        name="attend_back",
    )(heads, grad, logsums, *tables)


def norm_kernel(rows, places_ref, gain_ref, bias_ref, *refs):
    *pieces, out_ref, near_ref, far_ref = refs
    core = places_ref[len(pieces)]
    for i, piece in enumerate(pieces):

        @pl.when(pl.program_id(0) == i)
        def _(piece=piece):
            x = piece[...].astype(f32)
            centred = x - jnp.mean(x, axis=-1, keepdims=True)
            variance = jnp.mean(centred * centred, axis=-1, keepdims=True)
            out_ref[...] = (
                centred * lax.rsqrt(variance + epsilon) * gain_ref[...] + bias_ref[...]
            ).astype(bf16)

    for q in range(near_ref.shape[1] // rows):
        for side, half_ref in ((core, near_ref), (1 - core, far_ref)):
            at = pl.multiple_of((q * CORES + side) * rows, rows)
            half_ref[:, q * rows : (q + 1) * rows] = out_ref[:, pl.ds(at, rows)]


def norm_pieces(places, pieces, gain, bias, rows):
    local, d = pieces[0].shape
    fixed = lambda i, places: (0, 0)
    there = lambda i, places: (places[i], 0)
    count = len(pieces) * local
    return pl.pallas_call(
        functools.partial(norm_kernel, rows),
        grid_spec=pltpu.PrefetchScalarGridSpec(
            num_scalar_prefetch=1,
            grid=(len(pieces),),
            in_specs=[pl.BlockSpec((1, d), fixed)] * 2 + [pl.BlockSpec((local, d), fixed)] * len(pieces),
            out_specs=[
                pl.BlockSpec((local, d), there),
                pl.BlockSpec((local, d // CORES), there),
                pl.BlockSpec((local, d // CORES), there),
            ],
        ),
        out_shape=[
            jax.ShapeDtypeStruct((count, d), bf16),
            jax.ShapeDtypeStruct((count, d // CORES), bf16),
            jax.ShapeDtypeStruct((count, d // CORES), bf16),
        ],
        compiler_params=pltpu.CompilerParams(vmem_limit_bytes=48 * 1024 * 1024),
        name="norm_pieces",
    )(places, gain[None], bias[None], *pieces)


def order_kernel(places_ref, *refs):
    *pieces, out_ref = refs
    for i, piece in enumerate(pieces):

        @pl.when(pl.program_id(0) == i)
        def _(piece=piece):
            out_ref[...] = piece[...].astype(out_ref.dtype)


def order_pieces(kernel, name, places, pieces, vectors=(), dtype=bf16, size=None):
    local, d = pieces[0].shape
    size = local if size is None else size
    last = local // size - 1
    fixed = lambda i, places: (0, 0)
    return pl.pallas_call(
        kernel,
        grid_spec=pltpu.PrefetchScalarGridSpec(
            num_scalar_prefetch=1,
            grid=(len(pieces),),
            in_specs=[pl.BlockSpec((1, d), fixed)] * len(vectors)
            + [pl.BlockSpec((size, d), lambda i, places: (last, 0))] * len(pieces),
            out_specs=pl.BlockSpec((size, d), lambda i, places: (places[i], 0)),
        ),
        out_shape=jax.ShapeDtypeStruct((len(pieces) * size, d), dtype),
        compiler_params=pltpu.CompilerParams(vmem_limit_bytes=48 * 1024 * 1024),
        name=name,
    )(places, *[v[None] for v in vectors], *pieces)


def row_blocks(rows):
    return min(64, rows)


def unit_kernel(nz, ns, w, place_ref, in_ref, out_ref):
    for c in range(CORES):
        for q in range(nz):
            at = pl.multiple_of(((q * CORES + c) * ns + place_ref[0]) * w, w)
            to = (c * nz + q) * w
            out_ref[:, to : to + w] = in_ref[:, pl.ds(at, w)]


def unit_columns(weight, place, nz, ns, w):
    rows, ff = weight.shape
    block = row_blocks(rows)
    wide = CORES * nz * w
    return pl.pallas_call(
        functools.partial(unit_kernel, nz, ns, w),
        grid_spec=pltpu.PrefetchScalarGridSpec(
            num_scalar_prefetch=1,
            grid=(rows // block,),
            in_specs=[pl.BlockSpec((block, ff), lambda i, place: (i, 0))],
            out_specs=pl.BlockSpec((block, wide), lambda i, place: (i, 0)),
        ),
        out_shape=jax.ShapeDtypeStruct((rows, wide), weight.dtype),
        name="unit_columns",
    )(place, weight)


def place_units_kernel(nz, w, places_ref, *refs):
    *pieces, out_ref = refs
    ns = len(pieces)
    for i, piece in enumerate(pieces):
        for c in range(CORES):
            for q in range(nz):
                core = c ^ places_ref[ns]
                to = pl.multiple_of(((q * CORES + core) * ns + places_ref[i]) * w, w)
                at = (c * nz + q) * w
                out_ref[:, pl.ds(to, w)] = piece[:, at : at + w].astype(f32)


def place_units(places, pieces, rows, nz, w):
    width = pieces[0].shape[1]
    block = row_blocks(rows)
    ff = width * len(pieces)
    return pl.pallas_call(
        functools.partial(place_units_kernel, nz, w),
        grid_spec=pltpu.PrefetchScalarGridSpec(
            num_scalar_prefetch=1,
            grid=(rows // block,),
            in_specs=[pl.BlockSpec((block, width), lambda i, places: (i, 0)) for _ in pieces],
            out_specs=pl.BlockSpec((block, ff), lambda i, places: (i, 0)),
        ),
        out_shape=jax.ShapeDtypeStruct((rows, ff), f32),
        name="place_units",
    )(places, *pieces)


def low_half():
    return lax.broadcasted_iota(jnp.int32, (1, PAIR), 1) < HD


def lows(first, second):
    return jnp.where(low_half(), first, pltpu.roll(second, HD, 1))


def highs(first, second):
    return jnp.where(low_half(), pltpu.roll(first, HD, 1), second)


def head_kernel(nz, ns, place_ref, in_ref, out_ref):
    tiles = ns // 2
    part = nz * CORES * tiles
    even = lax.rem(place_ref[0], 2) == 0

    def tile(j, q, c):
        at = (j * part + (q * CORES + c) * tiles + lax.div(place_ref[0], 2)) * PAIR
        return in_ref[:, pl.ds(pl.multiple_of(at, PAIR), PAIR)].astype(f32)

    for c in range(CORES):
        for p in range(nz // 2):
            for j in range(3):
                first, second = tile(j, 2 * p, c), tile(j, 2 * p + 1, c)
                to = ((c * (nz // 2) + p) * 3 + j) * PAIR
                out_ref[:, to : to + PAIR] = jnp.where(
                    even, lows(first, second), highs(first, second)
                ).astype(out_ref.dtype)


def head_columns(weight, place, nz, ns):
    rows, width = weight.shape
    block = row_blocks(rows)
    wide = CORES * nz * 3 * HD
    return pl.pallas_call(
        functools.partial(head_kernel, nz, ns),
        grid_spec=pltpu.PrefetchScalarGridSpec(
            num_scalar_prefetch=1,
            grid=(rows // block,),
            in_specs=[pl.BlockSpec((block, width), lambda i, place: (i, 0))],
            out_specs=pl.BlockSpec((block, wide), lambda i, place: (i, 0)),
        ),
        out_shape=jax.ShapeDtypeStruct((rows, wide), weight.dtype),
        name="head_columns",
    )(place, weight)


def place_heads_kernel(nz, places_ref, *refs):
    *pieces, out_ref = refs
    ns = len(pieces)
    tiles = ns // 2
    even = lax.rem(places_ref[0], 2) == 0
    straight = (places_ref[0] ^ places_ref[1]) == 1
    for a in range(0, ns, 2):
        mates = [(a, a + 1)] if ns != 4 else [((0, 1), (0, 2)), ((2, 3), (1, 3))][a // 2]
        tile = lax.div(places_ref[mates[0][0]] if ns == 4 else places_ref[a], 2)
        if ns == 4:
            tile = jnp.where(straight, tile, lax.div(places_ref[mates[1][0]], 2))
        for j in range(3):
            for p in range(nz // 2):
                at = (p * 3 + j) * PAIR
                for c in range(CORES):
                    own = slice(c * nz * 3 * HD + at, c * nz * 3 * HD + at + PAIR)
                    loaded = [[pieces[i][:, own].astype(f32) for i in pair] for pair in mates]
                    core = c ^ places_ref[ns]
                    one, two = loaded[0]
                    if ns == 4:
                        one = jnp.where(straight, one, loaded[1][0])
                        two = jnp.where(straight, two, loaded[1][1])
                    first, second = jnp.where(even, one, two), jnp.where(even, two, one)
                    for q, value in ((2 * p, lows(first, second)), (2 * p + 1, highs(first, second))):
                        to = (((j * nz + q) * CORES + core) * tiles + tile) * PAIR
                        out_ref[:, pl.ds(pl.multiple_of(to, PAIR), PAIR)] = value


def place_heads(places, pieces, nz):
    rows = pieces[0].shape[0]
    width = CORES * nz * 3 * HD
    block = row_blocks(rows)
    whole = width * len(pieces)
    return pl.pallas_call(
        functools.partial(place_heads_kernel, nz),
        grid_spec=pltpu.PrefetchScalarGridSpec(
            num_scalar_prefetch=1,
            grid=(rows // block,),
            in_specs=[pl.BlockSpec((block, width), lambda i, places: (i, 0)) for _ in pieces],
            out_specs=pl.BlockSpec((block, whole), lambda i, places: (i, 0)),
        ),
        out_shape=jax.ShapeDtypeStruct((rows, whole), f32),
        name="place_heads",
    )(places, *pieces)


def place_out_kernel(places_ref, *refs):
    *pieces, out_ref = refs
    rows = out_ref.shape[0]
    for i, piece in enumerate(pieces):

        @pl.when(pl.program_id(0) == i)
        def _(piece=piece):
            wide = piece.shape[1]
            for r in range(piece.shape[0] // rows):
                out_ref[:, r * wide : (r + 1) * wide] = piece[r * rows : (r + 1) * rows, :].astype(f32)


def place_out(places, pieces, wide, hw, d):
    rows, width = pieces[0].shape
    return pl.pallas_call(
        place_out_kernel,
        grid_spec=pltpu.PrefetchScalarGridSpec(
            num_scalar_prefetch=1,
            grid=(len(pieces),),
            in_specs=[pl.BlockSpec((rows, wide), lambda i, places: (0, width // wide - 1)) for _ in pieces],
            out_specs=pl.BlockSpec((hw, d), lambda i, places: (places[i], 0)),
        ),
        out_shape=jax.ShapeDtypeStruct((len(pieces) * hw, d), f32),
        name="place_out",
    )(places, *pieces)


def pack_kernel(near_ref, got_ref, out_ref, packed_ref):
    width = near_ref.shape[1]
    hw = out_ref.shape[0]
    wide = packed_ref.shape[1] - 2 * width
    packed_ref[:, :width] = near_ref[...]
    packed_ref[:, width : 2 * width] = got_ref[...]
    for i in range(out_ref.shape[1] // wide):
        packed_ref[i * hw : (i + 1) * hw, 2 * width :] = out_ref[:, i * wide : (i + 1) * wide]


def pack(near, got, out_local, rows, hw):
    count, width = near.shape
    d = out_local.shape[1]
    whole = 2 * width + d * hw // rows
    half = pl.BlockSpec((rows, width), lambda i: (i, 0))
    return pl.pallas_call(
        pack_kernel,
        grid=(count // rows,),
        in_specs=[half, half, pl.BlockSpec((hw, d), lambda i: (i, 0))],
        out_specs=pl.BlockSpec((rows, whole), lambda i: (i, 0)),
        out_shape=jax.ShapeDtypeStruct((count, whole), bf16),
        name="pack",
    )(near, got, out_local)


def two_products_kernel(first_ref, first_right_ref, second_ref, second_right_ref, far_ref, near_ref):
    def products(out_ref):
        width = out_ref.shape[1]
        step = min(512, width)
        for at in range(0, width, step):
            columns = slice(at, at + step)
            out_ref[:, columns] = (
                last_last(first_ref[...], first_right_ref[columns, :])
                + last_last(second_ref[...], second_right_ref[columns, :])
            ).astype(bf16)

    half = pl.num_programs(0) // 2
    pl.when(pl.program_id(0) < half)(lambda: products(far_ref))
    pl.when(pl.program_id(0) >= half)(lambda: products(near_ref))


def two_products(first, first_right, second, second_right):
    rows = first.shape[0] // 2
    block = min(512, rows)
    half = rows // block
    width = first_right.shape[0]

    def left(x):
        return pl.BlockSpec((block, x.shape[1]), lambda i: (lax.rem(i + half, 2 * half), 0))

    def right(x):
        return pl.BlockSpec(x.shape, lambda i: (0, 0))

    depth = first.shape[1] + second.shape[1]
    out = jax.ShapeDtypeStruct((rows, width), bf16)
    return pl.pallas_call(
        two_products_kernel,
        grid=(2 * half,),
        in_specs=[left(first), right(first_right), left(second), right(second_right)],
        out_specs=[
            pl.BlockSpec((block, width), lambda i: (jnp.minimum(i, half - 1), 0)),
            pl.BlockSpec((block, width), lambda i: (jnp.maximum(i - half, 0), 0)),
        ],
        out_shape=[out, out],
        compiler_params=pltpu.CompilerParams(vmem_limit_bytes=48 * 1024 * 1024),
        cost_estimate=pl.CostEstimate(
            flops=4 * rows * width * depth,
            bytes_accessed=2 * (2 * rows + width) * depth + 4 * rows * width,
            transcendentals=0,
        ),
        name="two_products",
    )(first, first_right, second, second_right)


def gelu_and_slope(u):
    cubic = 0.044715
    root = 0.7978845608
    square = u * u
    t = jnp.tanh(root * u * (1.0 + cubic * square))
    value = 0.5 * u * (1.0 + t)
    slope = 0.5 * (1.0 + t) + 0.5 * u * (1.0 - t * t) * root * (1.0 + 3.0 * cubic * square)
    return value, slope


def on_device(
    ns,
    nf,
    tokens,
    qkv_weight,
    out_weight,
    up_weight,
    down_weight,
    norm_gain,
    norm_bias,
    qkv_bias,
    out_bias,
    up_bias,
    down_bias,
    cotangent,
):
    nz = nf // CORES
    ranks = CORES * ns
    s = lax.axis_index("seq")
    f = lax.axis_index("fsdp")
    k = f % CORES
    z = f // CORES
    local, d = tokens.shape[1:]
    length = ns * local
    rows = qkv_weight.shape[0]
    ff = up_weight.shape[1]
    w = ff // (nf * ns)
    shard_heads = rows // HD
    spread = shard_heads % ns == 0 and (shard_heads // ns * nz) % 2 == 0
    hw = shard_heads // ns * HD
    one_each = spread and hw == HD and ns % 2 == 0 and nz % 2 == 0
    tiled = w % PAIR == 0
    place = s[None].astype(jnp.int32)
    rank_cols = d // ranks
    pairs = rank_cols // PAIR
    lines = [[CORES * z + c for z in range(nz)] for c in range(CORES)]
    swap = [(i, i ^ 1) for i in range(nf)]
    everyone = ("seq", "fsdp")

    def after(x, *others):
        return lax.optimization_barrier((x,) + others)[0]

    def other_core(x):
        return lax.ppermute(x, "fsdp", swap)

    two_steps = ns == 4

    def plane_send(x, d):
        return lax.ppermute(x, "seq", [(i, i ^ d) for i in range(ns)])

    def plane_hop(x, second):
        hops = []
        for i in range(ns):
            for g in range(nf):
                hops.append((i * nf + g, (i ^ (1 + (g % CORES ^ second))) * nf + g))
        return lax.ppermute(x, everyone, hops)

    first_hop, second_hop = 1 + k, 2 - k
    steps = [0, first_hop, second_hop, 3] if two_steps else list(range(ns))
    other_steps = [0, second_hop, first_hop, 3] if two_steps else steps
    places = jnp.stack([s ^ step for step in steps]).astype(jnp.int32)
    other_places = jnp.stack([s ^ step for step in other_steps]).astype(jnp.int32)
    both_places = jnp.concatenate([places, ns + other_places])
    places = jnp.concatenate([places, k[None].astype(jnp.int32)])

    class Pieces:
        def __init__(self, x):
            self.pieces = [x]
            if two_steps:
                self.pieces += [plane_hop(x, 0), plane_hop(x, 1)]
            else:
                self.pieces += [plane_send(x, d) for d in range(1, ns)]

        def middle(self, *passed):
            if two_steps:
                near = after(self.pieces[1], self.pieces[2], *passed)
                self.pieces.append(plane_hop(near, 1))
                return [near]
            return self.pieces[1:]

        def all(self, *passed):
            return self.pieces[:1] + [after(piece, *passed) for piece in self.pieces[1:]]

    def plane_pieces(x):
        pieces = Pieces(x)
        pieces.middle()
        return pieces.pieces

    def arrange(pieces, dtype):
        size = pieces[0].shape[0]
        whole = jnp.zeros((ns * size,) + pieces[0].shape[1:], dtype)
        for at, piece in zip(steps, pieces):
            whole = lax.dynamic_update_slice_in_dim(whole, piece.astype(dtype), (s ^ at) * size, 0)
        return whole

    def pick(x, index, axis):
        return lax.dynamic_index_in_dim(x, index, axis, keepdims=False)

    vectors = (norm_gain, norm_bias, qkv_bias, out_bias, up_bias, down_bias)
    sizes = [v.shape[0] for v in vectors]
    small = jnp.concatenate(vectors)
    small = jnp.broadcast_to(small[None], (nf,) + small.shape)
    small = lax.all_to_all(small, "fsdp", split_axis=0, concat_axis=0, tiled=True)
    cuts, at = [], 0
    for size in sizes:
        cuts.append(small[:, at : at + size].reshape(-1).astype(f32))
        at += size
    gain, nbias, qkvb, outb, upb, downb = cuts

    def heads_of(weight):
        lead = weight.shape[0]
        if spread:
            part = pick(weight.reshape(lead, 3, nz, CORES, ns, hw), s, 4)
            part = part.transpose(0, 3, 1, 2, 4).reshape(lead, CORES, 3, pairs, PAIR)
        else:
            part = pick(weight.reshape(lead, 3, ns, CORES, pairs, PAIR), s, 2)
            part = part.transpose(0, 2, 1, 3, 4)
        return part.transpose(0, 1, 3, 2, 4).reshape(lead, CORES, 3 * rank_cols)

    def units_of(weight):
        lead = weight.shape[0]
        part = pick(weight.reshape(lead, nz, CORES, ns, w), s, 3)
        return part.transpose(0, 2, 1, 3).reshape(lead, CORES, nz * w)

    def core_half(x):
        return lax.dynamic_slice_in_dim(x, k * (x.shape[1] // CORES), x.shape[1] // CORES, 1)

    qkvb_mine = pick(heads_of(qkvb[None])[0], k, 0)
    upb_mine = pick(units_of(upb[None])[0], k, 0)
    tables = rotary_lanes(length)

    up_part = units_of(up_weight) if not tiled else unit_columns(up_weight, place, nz, ns, w)
    up_part = up_part.reshape(rows, -1)
    down_part = lax.dynamic_slice_in_dim(down_weight, s * w, w, 0)
    merged = up_part.shape[1] == d
    if merged:
        ff_both = lax.all_gather(jnp.concatenate([up_part, down_part]), "fsdp", axis=0, tiled=True)
    else:
        up_both = lax.all_gather(up_part, "fsdp", axis=0, tiled=True)
        down_mine = lax.all_gather(down_part, "fsdp", axis=0, tiled=True, axis_index_groups=lines)

    qkv_part = heads_of(qkv_weight) if not one_each else head_columns(qkv_weight, place, nz, ns)
    qkv_part = qkv_part.reshape(rows, CORES, -1)
    out_part = lax.dynamic_slice_in_dim(out_weight, s * hw, hw, 0)

    x_pieces = plane_pieces(tokens[0])
    ready = (gain, nbias, qkvb_mine, upb_mine, qkv_part, out_part) + tuple(tables)
    x_pieces = x_pieces[:1] + [after(piece, *ready) for piece in x_pieces[1:]]
    c_pieces = plane_pieces(after(cotangent[0], *x_pieces[1:]))
    x_pieces = x_pieces + [other_core(piece) for piece in x_pieces]

    norm_places = jnp.concatenate([both_places, k[None].astype(jnp.int32)])
    normed, normed_near, normed_far = norm_pieces(norm_places, x_pieces, gain, nbias, rows)

    if one_each:
        out_wide = d * hw // rows
        beside = out_part.reshape(hw, -1, out_wide).transpose(1, 0, 2).reshape(rows, out_wide)
        both = jnp.concatenate([qkv_part.reshape(rows, -1), beside], axis=1)
        both = lax.all_gather(after(both, normed), "fsdp", axis=0, tiled=True)
    else:
        qkv_both = lax.all_gather(qkv_part.reshape(rows, -1), "fsdp", axis=0, tiled=True)
        qkv_mine = core_half(qkv_both)
        if spread:
            out_mine = lax.all_gather(out_part, "fsdp", axis=0, tiled=True, axis_index_groups=lines)
        else:
            out_full = lax.all_gather(out_weight, "fsdp", axis=0, tiled=True)
            out_mine = lax.dynamic_slice_in_dim(out_full, (CORES * s + k) * rank_cols, rank_cols, 0)

    def first_first(left, right):
        return lax.dot_general(left, right, (((0,), (0,)), ((), ())), preferred_element_type=f32)

    def pair_cores(x):
        by_core = x.reshape(nz, CORES, rows, -1)
        keep, got = pick(by_core, k, 1), other_core(pick(by_core, 1 - k, 1))
        return jnp.concatenate([keep, got], axis=2).reshape(nz * rows, -1)

    def both_in_order(pieces):
        every = arrange([piece[None] for piece in pieces], bf16).reshape(ns, rows, CORES, -1)
        return jnp.where(k == 0, every, every[:, :, ::-1])

    def halves(left, right, dot, more=None):
        far = dot(left[length:], right)
        near = dot(left[:length], right)
        if more is not None:
            far, near = far + more[0].astype(f32), near + more[1].astype(f32)
        return far.astype(bf16), near.astype(bf16)

    def rank_parts(near, got):
        parts = []
        for step in steps:
            at = (s ^ step) * local
            part = lax.dynamic_slice_in_dim(near, at, local, 0).astype(f32)
            parts.append(part + lax.dynamic_slice_in_dim(got, at, local, 0).astype(f32))
        return parts[:1] + [part.astype(bf16) for part in parts[1:]]

    class RankSum:
        def __init__(self, parts):
            self.parts = parts
            if two_steps:
                self.across, self.beside = plane_hop(parts[3], 0), plane_hop(parts[1], 0)
            else:
                self.others = [plane_send(parts[d], d) for d in range(1, ns)]

        def first(self):
            return [self.across, self.beside] if two_steps else self.others

        def middle(self, *passed):
            if not two_steps:
                return list(passed)
            across = after(self.across, self.beside, *passed)
            self.rest = (self.parts[2].astype(f32) + across.astype(f32)).astype(bf16)
            return [self.rest]

        def total(self, *passed):
            others = [self.beside, plane_hop(self.rest, 1)] if two_steps else self.others
            total = self.parts[0]
            for other in others:
                total = total + after(other, *passed).astype(f32)
            return total

    def line_sum(x):
        return lax.psum_scatter(
            x, "fsdp", scatter_dimension=0, tiled=True, axis_index_groups=lines
        )

    c_pieces = c_pieces[:1] + [after(piece, normed) for piece in c_pieces[1:]]
    c2 = order_pieces(order_kernel, "order_both", both_places, c_pieces + [other_core(piece) for piece in c_pieces])
    if merged:
        ff_both = after(ff_both, c2).reshape(nz, CORES, rows + w, d)
        up_mine = core_half(ff_both[:, :, :rows].reshape(d, d))
        down_mine = pick(ff_both[:, :, rows:], k, 1).reshape(nz * w, d)
    else:
        up_mine = core_half(up_both)
    hidden = plain_dot(normed, up_mine) + upb_mine
    activated, slope = gelu_and_slope(hidden)
    activated = activated.astype(bf16)
    down_local = first_first(activated, c2).astype(bf16)
    c2 = after(c2, down_local)
    hidden_grad = (last_last(c2, down_mine) * slope).astype(bf16)
    up_local = pair_cores(first_first(normed, hidden_grad).astype(bf16))
    if merged:
        ff_local = [x.reshape(nz, -1, d) for x in (up_local, down_local)]
        ff_local = [jnp.concatenate(ff_local, axis=1).reshape(-1, d)]
    else:
        ff_local = [up_local, down_local]
    ff_own = [line_sum(x) for x in ff_local]

    if one_each:
        both = after(both, *ff_local)
        qkv_mine = lax.dynamic_slice_in_dim(both, k * 3 * rank_cols, 3 * rank_cols, 1)
        out_mine = pick(both.reshape(nz, CORES, rows, -1), k, 1)[:, :, CORES * 3 * rank_cols :]
        out_mine = out_mine.reshape(nz, -1, hw, out_wide).transpose(0, 2, 1, 3).reshape(rank_cols, d)
    normed = after(normed, *ff_local)
    mixed = plain_dot(normed, qkv_mine) + qkvb_mine
    heads, attended, logsums = attend(mixed, tables, length)
    c2 = after(c2, attended)
    attended_grad = last_last(c2, out_mine).astype(bf16)
    attended = after(attended, attended_grad)
    out_local = first_first(attended, c2).astype(bf16)
    activated, attended = after(activated, out_local), after(attended, out_local)
    branch_far, branch_near = halves(activated, down_mine, plain_dot, halves(attended, out_mine, plain_dot))
    branch_got = after(other_core(branch_far), branch_near)
    branch_parts = rank_parts(branch_near, branch_got)
    branch_sum = RankSum(branch_parts)
    attended_grad = after(attended_grad, *branch_parts)
    mixed_grad = attend_back(heads, attended_grad, logsums, tables, length)
    normed_far = after(normed_far, mixed_grad)
    qkv_far = first_first(normed_far, mixed_grad).astype(bf16)
    qkv_got = other_core(qkv_far)
    normed_near = after(normed_near, qkv_far)
    qkv_near = first_first(normed_near, mixed_grad).astype(bf16)
    passed = branch_sum.middle(qkv_near)
    hidden_grad, mixed_grad = after(hidden_grad, *passed), after(mixed_grad, qkv_got)
    far, near = two_products(hidden_grad, up_mine, mixed_grad, qkv_mine)
    got = other_core(far)
    if one_each:
        attn_local = pack(qkv_near, after(qkv_got, near), out_local, rows, hw)
    else:
        attn_local = jnp.concatenate([qkv_near, qkv_got], axis=1)
    grad_parts = rank_parts(near, after(got, attn_local))
    grad_sum = RankSum(grad_parts)
    branches = branch_sum.total(*grad_parts)
    mixed_grad, hidden_grad = after(mixed_grad, branches), after(hidden_grad, branches)
    mixed_sum = jnp.sum(mixed_grad.astype(f32), axis=0).reshape(pairs, 3, PAIR).transpose(1, 0, 2)
    if spread:
        mixed_sum = mixed_sum.reshape(3, nz, 1, 1, hw)
        mixed_full = jnp.zeros((3, nz, CORES, ns, hw), f32)
        mixed_full = lax.dynamic_update_slice(mixed_full, mixed_sum, (0, 0, k, s, 0))
    else:
        mixed_full = jnp.zeros((3, ns, CORES, rank_cols), f32)
        mixed_full = lax.dynamic_update_slice(
            mixed_full, mixed_sum.reshape(3, 1, 1, rank_cols), (0, s, k, 0)
        )
    hidden_sum = jnp.sum(hidden_grad.astype(f32), axis=0).reshape(nz, 1, 1, w)
    hidden_full = lax.dynamic_update_slice(
        jnp.zeros((nz, CORES, ns, w), f32), hidden_sum, (0, k, s, 0)
    )
    c_local = jnp.sum(after(cotangent[0], branches).astype(f32), axis=0)
    passed = (branches, mixed_full, hidden_full, c_local)
    ff_own = [after(x, *passed, *grad_sum.first()) for x in ff_own]
    attn_own = line_sum(after(attn_local, *ff_own))
    out_own = line_sum(out_local) if spread and not one_each else None
    ff_pieces = [Pieces(x) for x in ff_own]
    passed = grad_sum.middle(*ff_own)
    normed_grad = grad_sum.total(*passed)

    token_rows = tokens[0].astype(f32)
    block_out = (token_rows + branches + outb + downb).astype(bf16)[None]

    centred_own = token_rows - jnp.mean(token_rows, axis=-1, keepdims=True)
    variance_own = jnp.mean(centred_own * centred_own, axis=-1, keepdims=True)
    inverse = lax.rsqrt(variance_own + epsilon)
    xhat = centred_own * inverse
    g = normed_grad * gain
    rows_grad = inverse * (
        g - jnp.mean(g, axis=-1, keepdims=True) - xhat * jnp.mean(g * xhat, axis=-1, keepdims=True)
    )
    upstream = cotangent[0].astype(f32)
    tokens_grad = (upstream + rows_grad).astype(bf16)[None]

    passed = [x for pieces in ff_pieces for x in pieces.middle(tokens_grad)]
    attn_pieces = Pieces(after(attn_own, *passed))
    ff_pieces = [pieces.all(attn_pieces.pieces[0]) for pieces in ff_pieces]
    up_pieces, down_pieces = ff_pieces[0], ff_pieces[-1]
    if tiled:
        up_wgrad = place_units(places, up_pieces, rows, nz, w)
    else:
        up_all = both_in_order(up_pieces).reshape(ns, rows, CORES, nz, w)
        up_wgrad = up_all.transpose(1, 3, 2, 0, 4).reshape(rows, ff).astype(f32)
    passed = attn_pieces.middle(up_wgrad)
    down_pieces = down_pieces[:1] + [after(piece, *passed) for piece in down_pieces[1:]]
    down_wgrad = order_pieces(order_kernel, "place_down", places, down_pieces, dtype=f32, size=w)

    def everyone_sum(sums):
        flat = jnp.concatenate([v.reshape(nf, -1) for v in sums], axis=1)
        flat = after(flat, attn_pieces.pieces[0])
        flat = lax.all_to_all(flat, "fsdp", split_axis=0, concat_axis=0, tiled=True)
        part = after(jnp.sum(flat, axis=0), *passed)
        flat = part
        for step in range(1, ns):
            flat = flat + plane_send(part, step)
        shards, at = [], 0
        for v in sums:
            size = v.shape[0] // nf
            shards.append(flat[at : at + size])
            at += size
        return shards

    sums = (
        mixed_full.reshape(-1)[: 2 * d],
        mixed_full.reshape(-1)[2 * d :],
        hidden_full.reshape(-1),
        c_local,
        jnp.sum(xhat * normed_grad, axis=0),
        jnp.sum(normed_grad, axis=0),
    )
    bias_grads = everyone_sum(sums)
    qkv_bgrad, value_bgrad, up_bgrad, out_bgrad, gain_grad, norm_bgrad = bias_grads

    attn_pieces = attn_pieces.all()
    out_pieces = plane_pieces(out_own) if spread and not one_each else None
    if one_each:
        qkv_wgrad = place_heads(places, attn_pieces, nz)
        out_wgrad = place_out(places, attn_pieces, out_wide, hw, d)
    elif spread:
        qkv_all = both_in_order(attn_pieces).reshape(ns, rows, CORES, pairs, 3, PAIR)
        qkv_all = qkv_all.transpose(0, 2, 1, 4, 3, 5).reshape(ns, CORES, rows, 3, nz, hw)
        qkv_wgrad = qkv_all.transpose(2, 3, 4, 1, 0, 5).reshape(rows, 3 * d).astype(f32)
        out_wgrad = order_pieces(order_kernel, "place_out", places, out_pieces, dtype=f32)
    else:
        qkv_all = both_in_order(attn_pieces).reshape(ns, rows, CORES, pairs, 3, PAIR)
        qkv_wgrad = qkv_all.transpose(1, 4, 0, 2, 3, 5).reshape(rows, 3 * d).astype(f32)
        rank = CORES * s + k
        out_padded = lax.dynamic_update_slice_in_dim(
            jnp.zeros((d, d), bf16), out_local, rank * rank_cols, 0
        )
        out_shard = lax.psum_scatter(out_padded, "fsdp", scatter_dimension=0, tiled=True)
        out_wgrad = lax.psum(out_shard.astype(f32), "seq")
    return (
        block_out,
        tokens_grad,
        qkv_wgrad,
        out_wgrad,
        up_wgrad,
        down_wgrad,
        gain_grad,
        norm_bgrad,
        qkv_bgrad,
        value_bgrad,
        out_bgrad,
        up_bgrad,
        out_bgrad,
    )


def solution(mesh):
    sharded = P("fsdp", "seq", None)
    matrix = P("fsdp", None)
    vector = P("fsdp")
    return jax.shard_map(
        functools.partial(on_device, mesh.shape["seq"], mesh.shape["fsdp"]),
        mesh=mesh,
        in_specs=(sharded,) + (matrix,) * 4 + (vector,) * 6 + (sharded,),
        out_specs=(sharded,) * 2 + (matrix,) * 4 + (vector,) * 7,
        check_vma=False,
    )
```
